512 devices in a mesh: band: 8 (over x, core), tile: 64 (over z, y).
Axes of the slice: x: 4, y: 8, z: 8, core: 2. Of those that a mesh axis runs over, the one named last changes fastest.
Arguments:
- coarse_blocks: bfloat16 [512, 4480], P('band'), may hold values from -6 to 6
- block_anchor: int32 [8, 64], replicated, may hold values from 0 to 511
- nest_width: int32 [8], P('band'), may hold values from 128 to 256, as said below
- sigmas: float32 [3], replicated, as said below
- noise: float32 [8, 4, 256, 256], P('band', None, 'tile'), may hold values from -6 to 6
- w_context: bfloat16 [256, 70], replicated, may hold values from -0.75 to 0.75
- w_in: bfloat16 [9, 128, 4], replicated, may hold values from -1 to 1
- w_sigma: float32 [128], replicated, may hold values from -4 to 4
- w_enc: bfloat16 [9, 128, 128], replicated, may hold values from -0.1875 to 0.1875
- w_down: bfloat16 [9, 256, 128], replicated, may hold values from -0.1875 to 0.1875
- w_mid: bfloat16 [9, 256, 256], replicated, may hold values from -0.125 to 0.125
- w_dec: bfloat16 [9, 128, 384], replicated, may hold values from -0.109375 to 0.109375
- w_out: bfloat16 [9, 4, 128], replicated, may hold values from -0.75 to 0.75
Outputs:
- downscaled: float32 [8, 4, 256, 256], P('band', None, 'tile')
The draws below stay inside these ranges and needn't reach their ends.
Inputs may be any that keep to these rules, and one draw needn't show every extreme that they name: `nest_width`: one nest uses all 256 columns. `sigmas`: the levels fall strictly from each entry to the next.
All inputs are finite; a program needn't handle non-finite values.
Results may differ from the reference program's by a relative error of at most 0.014.
Values may be sent and summed in bfloat16 or wider, within the bound.
No kernel may reach another device: no remote copies, remote signals or barrier semaphores. Data moves between devices by JAX's collectives and lax.ppermute only.
A program may use at most 64 MiB of HBM per device.

```python
import math
import jax
import jax.numpy as jnp
from jax import lax

FV = 4
CC = 70
CH1 = 128
CH2 = 256
BLK = 64
K = 96
NB_DEV = 64
TR = 4
TC = 256
STEPS = 2
NESTS = 8
ROWS = 256
COARSE_BLOCKS = 512
N_BAND = 8
N_TILE = 64


def draw_nest_width(key, part):
    key = jax.random.fold_in(key, 11)
    first_key, second_key = jax.random.split(key)
    widths = jax.random.randint(first_key, (NESTS,), TC // 2, TC + 1)
    full_nest = jax.random.randint(second_key, (), 0, NESTS)
    return jnp.where(jnp.arange(NESTS) == full_nest, TC, widths).astype(jnp.int32)


def draw_sigmas(key, part):
    key = jax.random.fold_in(key, 5)
    levels = 3.0 * 0.35 ** jnp.arange(STEPS + 1, dtype=jnp.float32)
    return levels * jax.random.uniform(key, (STEPS + 1,), jnp.float32, 0.8, 1.2)


def touch_ends(result, stream_key, low, largest):
    index_at = [jax.random.randint(jax.random.fold_in(stream_key, axis), (), 0, length) for axis, length in enumerate(result.shape)]
    widest = result.shape.index(max(result.shape))
    next_to = index_at[:widest] + [(index_at[widest] + 1) % result.shape[widest]] + index_at[widest + 1:]
    return result.at[tuple(index_at)].set(low).at[tuple(next_to)].set(largest)


def block_scale(stream_key, dims, cuts, smallest, high):
    level = 1.0
    for dim, blocks in cuts:
        draws = jax.random.uniform(jax.random.fold_in(jax.random.fold_in(stream_key, 6), dim), (blocks,), jnp.float32, smallest / len(cuts), high / len(cuts))
        level = level * jnp.repeat(jnp.exp(draws), dims[dim] // blocks).reshape((-1,) + (1,) * (len(dims) - 1 - dim))
    return level


def gaussian(rng, shape, spread, reach, shards=(), held_as=jnp.bfloat16):
    drawn = spread * jax.random.normal(rng, shape, jnp.float32)
    if shards:
        drawn = drawn * block_scale(rng, shape, shards, -0.22, 0.18)
    return jnp.clip(drawn, -reach, reach).astype(held_as)


def setup_inputs(seed: int = 0) -> dict:
    key_list = jax.random.split(jax.random.key(seed), 14)
    return {
        "coarse_blocks": gaussian(key_list[0], (COARSE_BLOCKS, CC * BLK), 1.0, 6.0, ((0, 8),)),
        "block_anchor": touch_ends(jax.random.randint(key_list[1], (NESTS, N_TILE), 0, COARSE_BLOCKS), jax.random.fold_in(key_list[1], 1), 0, COARSE_BLOCKS - 1).astype(jnp.int32),
        "nest_width": draw_nest_width(jax.random.fold_in(key_list[13], 71), 0),
        "sigmas": draw_sigmas(jax.random.fold_in(key_list[13], 71), 0),
        "noise": gaussian(key_list[4], (NESTS, FV, ROWS, TC), 1.0, 6.0, ((0, 8), (2, 64)), jnp.float32),
        "w_context": gaussian(key_list[5], (CH2, CC), CC ** -0.5, 0.75),
        "w_in": gaussian(key_list[6], (9, CH1, FV), (9 * FV) ** -0.5, 1.0),
        "w_sigma": gaussian(key_list[7], (CH1,), 1.0, 4.0, (), jnp.float32),
        "w_enc": gaussian(key_list[8], (9, CH1, CH1), (9 * CH1) ** -0.5, 0.1875),
        "w_down": gaussian(key_list[9], (9, CH2, CH1), (9 * CH1) ** -0.5, 0.1875),
        "w_mid": gaussian(key_list[10], (9, CH2, CH2), (9 * CH2) ** -0.5, 0.125),
        "w_dec": gaussian(key_list[11], (9, CH1, CH1 + CH2), (9 * (CH1 + CH2)) ** -0.5, 0.109375),
        "w_out": gaussian(key_list[12], (9, FV, CH1), (9 * CH1 // 16) ** -0.5, 0.75),
    }


SIGMA_DATA = 0.5

def conv_taps(padded, weight, out_rows, out_cols, stride):
    channels = padded.shape[0]
    summed = jnp.zeros((weight.shape[1], out_rows, out_cols), jnp.float32)
    for tap_index in range(9):
        row_off = tap_index // 3
        col_off = tap_index % 3
        window = lax.slice(padded, (0, row_off, col_off), (channels, row_off + stride * (out_rows - 1) + 1, col_off + stride * (out_cols - 1) + 1), (1, stride, stride))
        summed = summed + jnp.einsum('oi,irc->orc', weight[tap_index].astype(jnp.float32), window.astype(jnp.float32))
    return summed

def pad_all(field_in):
    return jnp.pad(field_in, ((0, 0), (1, 1), (1, 1)))

def nest_context(coarse_blocks, nest_anchors, w_context):
    offsets = jnp.arange(K, dtype=jnp.int32)
    block_ids = (nest_anchors[:, None] + offsets[None, :]) % (NB_DEV * N_BAND)
    row_ids = block_ids % N_BAND * NB_DEV + block_ids // N_BAND
    blocks = coarse_blocks[row_ids].reshape(N_TILE, K, CC, BLK)
    encoded = jax.nn.silu(jnp.einsum('hc,tkcb->tkhb', w_context.astype(jnp.float32), blocks.astype(jnp.float32))).astype(jnp.bfloat16)
    group_size = K // (TR // 2)
    pooled = lax.optimization_barrier(jnp.sum(encoded.astype(jnp.float32).reshape(N_TILE, TR // 2, group_size, CH2, BLK), axis=2)) * (1.0 / math.sqrt(group_size))
    context_map = jnp.transpose(pooled, (2, 0, 1, 3)).reshape(CH2, ROWS // 2, BLK)
    return jnp.repeat(context_map, TC // 2 // BLK, axis=2)

def denoise(field_now, sigma_now, context_map, colmask, halfmask, weights):
    w_in, w_sigma, w_enc, w_down, w_mid, w_dec, w_out = weights
    scale_in = 1.0 / jnp.sqrt(sigma_now * sigma_now + SIGMA_DATA * SIGMA_DATA)
    scaled = (field_now * scale_in).astype(jnp.bfloat16)
    embedded = w_sigma[:, None, None] * jnp.log(sigma_now)
    first_act = (jax.nn.silu(conv_taps(pad_all(scaled), w_in, ROWS, TC, 1) + embedded) * colmask).astype(jnp.bfloat16)
    second = (jax.nn.silu(conv_taps(pad_all(first_act), w_enc, ROWS, TC, 1)) * colmask).astype(jnp.bfloat16)
    third_act = (jax.nn.silu(conv_taps(pad_all(second), w_down, ROWS // 2, TC // 2, 2) + context_map) * halfmask).astype(jnp.bfloat16)
    fourth = (jax.nn.silu(conv_taps(pad_all(third_act), w_mid, ROWS // 2, TC // 2, 1)) * halfmask).astype(jnp.bfloat16)
    upward = jnp.repeat(jnp.repeat(fourth, 2, axis=1), 2, axis=2)
    joined = jnp.concatenate([second, upward], axis=0)
    fifth_act = (jax.nn.silu(conv_taps(pad_all(joined), w_dec, ROWS, TC, 1)) * colmask).astype(jnp.bfloat16)
    return conv_taps(pad_all(fifth_act), w_out, ROWS, TC, 1)

def reference(coarse_blocks, block_anchor, nest_width, sigmas, noise, w_context, w_in, w_sigma, w_enc, w_down, w_mid, w_dec, w_out):
    weights = (w_in, w_sigma, w_enc, w_down, w_mid, w_dec, w_out)

    def one_nest(nest_item):
        nest_noise, nest_anchors, width_now = nest_item
        context_map = nest_context(coarse_blocks, nest_anchors, w_context)
        colmask = (jnp.arange(TC, dtype=jnp.int32) < width_now).astype(jnp.float32)[None, None, :]
        halfmask = (jnp.arange(TC // 2, dtype=jnp.int32) * 2 < width_now).astype(jnp.float32)[None, None, :]
        field_now = sigmas[0] * nest_noise * colmask
        for step_index in range(STEPS):
            sigma_now = sigmas[step_index]
            sigma_next = sigmas[step_index + 1]
            output_net = denoise(field_now, sigma_now, context_map, colmask, halfmask, weights)
            total_var = sigma_now * sigma_now + SIGMA_DATA * SIGMA_DATA
            denoised = SIGMA_DATA * SIGMA_DATA / total_var * field_now + sigma_now * SIGMA_DATA / jnp.sqrt(total_var) * output_net
            field_now = (field_now + (sigma_next - sigma_now) / sigma_now * (field_now - denoised)) * colmask
        return field_now
    return lax.map(one_nest, (noise, block_anchor, nest_width))
```

```python
import functools
import math

import jax
import jax.numpy as jnp
from jax import lax
from jax.experimental import pallas as pl
from jax.experimental.pallas import tpu as pltpu
from jax.sharding import PartitionSpec as P

K = 96
SIGMA_DATA = 0.5
BF = jnp.bfloat16
F32 = jnp.float32
HALF = 128
ROWS = 256
NT = (((1,), (1,)), ((), ()))
TN = (((0,), (1,)), ((), ()))

STEP_ROWS = (
    dict(scaled=(-15, 31), first=(-14, 29), second=(-13, 27), third=(-6, 13), fourth=(-5, 11), fifth=(-8, 19), out=(-7, 17)),
    dict(scaled=(-7, 17), first=(-6, 15), second=(-5, 13), third=(-2, 6), fourth=(-1, 4), fifth=(-1, 6), out=(0, 4)),
)


def silu(v):
    h = 0.5 * v
    return h + h * jnp.tanh(h)


def dot_nt(a, b):
    return lax.dot_general(a, b, NT, preferred_element_type=F32)


def encode_kernel(anchor_ref, blocks_ref, w_ref, out_ref, enc_ref):
    band = lax.axis_index("band")
    tile = lax.axis_index("tile")
    count = enc_ref.shape[0]
    cells = enc_ref.shape[1]

    def encode(i, carry):
        part = blocks_ref[pl.ds(pl.multiple_of(i * 512, 512), 512), :]
        v = silu(dot_nt(part, w_ref[...])).astype(BF).astype(F32)
        enc_ref[pl.ds(i * 8, 8)] = v.reshape(8, cells, 256)
        return carry

    lax.fori_loop(0, count // 8, encode, 0)

    def window(k, carry):
        nest = k // 2
        part = k % 2
        anchor = anchor_ref[nest, tile]
        begin = anchor + (band - anchor + 512) % 8 + part * 48
        row = (begin % 512) // 8
        total = enc_ref[row]
        for m in range(1, 6):
            total = total + enc_ref[(row + m) % count]
        out_ref[nest, pl.ds(pl.multiple_of(part * cells, cells), cells), :] = total.astype(BF)
        return carry

    lax.fori_loop(0, 16, window, 0)


def pair_weight(w, a):
    zero = jnp.zeros_like(w(a, 0))
    own = jnp.concatenate(
        [jnp.concatenate([w(a, 1), w(a, 2)], 1), jnp.concatenate([w(a, 0), w(a, 1)], 1)], 0
    )
    rim = jnp.concatenate(
        [jnp.concatenate([w(a, 0), zero], 1), jnp.concatenate([zero, w(a, 2)], 1)], 0
    )
    return own, rim


def prep_kernel(w_enc, w_down, w_mid, w_dec, enc_o, down_o, mid_o, dec2_o, even_o, odd_o):
    for a in range(3):
        own, rim = pair_weight(lambda i, b: w_enc[3 * i + b], a)
        enc_o[:, 512 * a : 512 * a + 256] = own
        enc_o[:, 512 * a + 256 : 512 * a + 512] = rim
        own, rim = pair_weight(lambda i, b: w_dec[3 * i + b, :, 0:128], a)
        dec2_o[:, 512 * a : 512 * a + 256] = own
        dec2_o[:, 512 * a + 256 : 512 * a + 512] = rim
        down_o[:, 256 * a : 256 * a + 128] = w_down[3 * a + 1]
        down_o[:, 256 * a + 128 : 256 * a + 256] = w_down[3 * a + 2]
        down_o[:, 768 + 128 * a : 896 + 128 * a] = w_down[3 * a]
        for b in range(3):
            mid_o[:, 768 * a + 256 * b : 768 * a + 256 * b + 256] = w_mid[3 * a + b]

    def up(a, b):
        return w_dec[3 * a + b, :, 128:384].astype(F32)

    for o_ref, sets in ((even_o, ((0,), (1, 2))), (odd_o, ((0, 1), (2,)))):
        for k, taps in enumerate(sets):
            col = [sum(up(a, b) for a in taps) for b in range(3)]
            zero = jnp.zeros_like(col[0])
            o_ref[:, 768 * k : 768 * k + 256] = jnp.concatenate([col[0], zero], 0).astype(BF)
            o_ref[:, 768 * k + 256 : 768 * k + 512] = jnp.concatenate(
                [col[1] + col[2], col[0] + col[1]], 0
            ).astype(BF)
            o_ref[:, 768 * k + 512 : 768 * k + 768] = jnp.concatenate([zero, col[2]], 0).astype(BF)


def main_kernel(
    width_ref, coef_ref,
    far_up, near_up, own, near_down, far_down,
    cond_far_up, cond_up, cond_own, cond_down, cond_far_down,
    bias_ref, w_in, w_enc, w_down, w_mid, w_dec2, w_even, w_odd, w_out,
    out_ref,
    state, spread, firstc, firste, secondc, seconde, third, thirdl, thirdr, fourth, fourthl, fourthr,
    fifthc, fifthe, prod, picked,
):
    tile = lax.axis_index("tile")
    base = tile * 4
    width = width_ref[0]
    lane = lax.broadcasted_iota(jnp.int32, (HALF, 256), 1)
    pair = lax.broadcasted_iota(jnp.int32, (HALF, 256), 0)
    colmask = (2 * pair + lane // 128 < width).astype(F32)
    halfmask = (2 * pair < width).astype(F32)
    natural = (lax.broadcasted_iota(jnp.int32, (8, 256), 1) < width).astype(F32)

    def fine_ok(rho):
        row = base + rho
        return jnp.logical_and(row >= 0, row < ROWS).astype(F32)

    def half_ok(h):
        row = tile * 2 + h
        return jnp.logical_and(row >= 0, row < ROWS // 2).astype(F32)

    def slide(x, by):
        rows = x.shape[0]
        edge = 0 if by == 1 else HALF - 1
        where = lax.broadcasted_iota(jnp.int32, x.shape, 0) % HALF
        return jnp.where(where == edge, 0.0, pltpu.roll(x, by % rows, 0))

    def keep_pairs(y, center, rim, at, n, mask, lo):
        y = jnp.concatenate(
            [y[k * HALF : (k + 1) * HALF] * (mask * fine_ok(lo + at + k)) for k in range(n)], 0
        )
        side = jnp.concatenate([slide(y[:, 128:], 1), slide(y[:, :128], -1)], 1).astype(BF)
        y = y.astype(BF)
        for k in range(n):
            center[at + k] = y[k * HALF : (k + 1) * HALF]
            rim[at + k] = side[k * HALF : (k + 1) * HALF]

    def keep_half(y, center, left, right, at, n, lo):
        y = jnp.concatenate(
            [y[k * HALF : (k + 1) * HALF] * (halfmask * half_ok(lo + at + k)) for k in range(n)], 0
        )
        sides = (slide(y, 1).astype(BF), slide(y, -1).astype(BF))
        y = y.astype(BF)
        for k in range(n):
            cut = slice(k * HALF, (k + 1) * HALF)
            center[at + k] = y[cut]
            left[at + k] = sides[0][cut]
            right[at + k] = sides[1][cut]

    def stacked(ref, at, n, step=1):
        return jnp.concatenate([ref[at + step * k] for k in range(n)], 0)

    def chunks(total, size, body):
        full = total // size
        if full == 1:
            body(0, size)
        elif full:
            lax.fori_loop(0, full, lambda i, c: (body(i * size, size), c)[1], 0)
        if total % size:
            body(full * size, total % size)

    pieces = ((far_up, -16, 12), (near_up, -4, 4), (own, 0, 4), (near_down, 4, 4), (far_down, 8, 12))
    start = coef_ref[0, 0]
    empty = jnp.zeros((4, 256), F32)
    for ref, lo, n in pieces:
        for k in range(n):
            rho = lo + k
            if -15 <= rho <= 15:
                value = jnp.concatenate([ref[4 * k : 4 * k + 4, :], empty], 0)
                state[8 * (rho + 15) : 8 * (rho + 16), :] = start * value * (natural * fine_ok(rho))

    col = lax.broadcasted_iota(jnp.int32, (256, 512), 0)
    place = lax.broadcasted_iota(jnp.int32, (256, 512), 1)
    pick = (col == 2 * (place % 128) + place // 128 - 1).astype(F32).astype(BF)
    weave_j = lax.broadcasted_iota(jnp.int32, (HALF, 256), 0)
    weave_c = lax.broadcasted_iota(jnp.int32, (HALF, 256), 1)
    weave = [(weave_c == 2 * weave_j + p).astype(F32) for p in range(2)]
    repeat = (
        lax.broadcasted_iota(jnp.int32, (HALF, 64), 0) // 2 == lax.broadcasted_iota(jnp.int32, (HALF, 64), 1)
    ).astype(F32).astype(BF)

    conds = (
        (cond_far_up, 0), (cond_far_up, 1), (cond_far_up, 2), (cond_far_up, 3),
        (cond_up, 0), (cond_up, 1), (cond_own, 0), (cond_own, 1), (cond_down, 0), (cond_down, 1),
        (cond_far_down, 0), (cond_far_down, 1), (cond_far_down, 2), (cond_far_down, 3),
    )

    for step in range(2):
        rows = STEP_ROWS[step]
        state_lo = rows["scaled"][0]
        scale, keep, mix, move = (coef_ref[step, 1 + i] for i in range(4))
        bias = bias_ref[step : step + 1, :]

        n_scaled = rows["scaled"][1]
        scaled = (state[0 : 8 * n_scaled, :] * scale).astype(BF)
        spread[0 : 8 * n_scaled, :] = jnp.dot(scaled, pick, preferred_element_type=F32)
        lo, total = rows["first"]

        def first_rows(at, n):
            cols = []
            for k in range(n):
                cols.append(
                    jnp.concatenate(
                        [
                            spread[pl.ds(pl.multiple_of((at + k + a) * 8, 8), 8), 128 * q : 128 * q + 128]
                            for a in range(3)
                            for q in range(4)
                        ],
                        0,
                    )
                )
            x = jnp.concatenate(cols, 1).astype(BF)
            y = lax.dot_general(x, w_in[...], TN, preferred_element_type=F32)
            keep_pairs(silu(y + bias), firstc, firste, at, n, colmask, lo)

        chunks(total, 5, first_rows)

        lo, total = rows["second"]

        def second_rows(at, n):
            x = jnp.concatenate(
                [stacked(ref, at + a, n) for a in range(3) for ref in (firstc, firste)], 1
            )
            keep_pairs(silu(dot_nt(x, w_enc[...])), secondc, seconde, at, n, colmask, rows["second"][0])

        chunks(total, 9 if step == 0 else 13, second_rows)

        second_lo = rows["second"][0]
        third_lo, total = rows["third"]

        def third_rows(at, n):
            begin = 2 * third_lo - 1 - second_lo + 2 * at
            x = jnp.concatenate(
                [stacked(secondc, begin + a, n, 2) for a in range(3)]
                + [
                    jnp.concatenate([seconde[begin + a + 2 * k][:, :128] for k in range(n)], 0)
                    for a in range(3)
                ],
                1,
            )
            y = dot_nt(x, w_down[...])
            add = []
            for k in range(n):
                ref, r = conds[third_lo + at + k + 6]
                add.append(jnp.dot(repeat, ref[64 * r : 64 * r + 64, :], preferred_element_type=F32))
            y = y + jnp.concatenate(add, 0)
            keep_half(silu(y), third, thirdl, thirdr, at, n, third_lo)

        for at in range(0, total, 7):
            third_rows(at, min(7, total - at))

        fourth_lo, total = rows["fourth"]

        def fourth_rows(at, n):
            begin = fourth_lo - 1 - third_lo + at
            x = jnp.concatenate(
                [stacked(ref, begin + a, n) for a in range(3) for ref in (thirdl, third, thirdr)], 1
            )
            keep_half(silu(dot_nt(x, w_mid[...])), fourth, fourthl, fourthr, at, n, fourth_lo)

        for at in range(0, total, 6):
            fourth_rows(at, min(6, total - at))

        fifth_lo, total = rows["fifth"]

        def fifth_rows(at, n):
            rho = fifth_lo + at
            odd = rho % 2
            begin = rho - 1 - second_lo
            h = (rho - odd) // 2 - fourth_lo - (0 if odd else 1)
            x = jnp.concatenate(
                [stacked(ref, begin + a, n, 2) for a in range(3) for ref in (secondc, seconde)], 1
            )
            z = jnp.concatenate(
                [stacked(ref, h + a, n) for a in range(2) for ref in (fourthl, fourth, fourthr)], 1
            )
            y = dot_nt(x, w_dec2[...]) + dot_nt(z, (w_odd if odd else w_even)[...])
            y = silu(y)
            for k in range(n):
                part = y[k * HALF : (k + 1) * HALF]
                keep_pairs(part, fifthc, fifthe, at + 2 * k, 1, colmask, fifth_lo)

        for parity in range(2):
            n_rows = (total - parity + 1) // 2
            for at in range(0, n_rows, 5):
                fifth_rows(parity + 2 * at, min(5, n_rows - at))

        def out_rows(at, n):
            x = jnp.concatenate([stacked(fifthc, at, n), stacked(fifthe, at, n)], 1)
            prod[:, at * HALF : (at + n) * HALF] = dot_nt(w_out[...], x)

        for at in range(0, total, 10):
            out_rows(at, min(10, total - at))
        out_lo, total = rows["out"]
        for k in range(total):
            for p in range(2):
                picked[p, 8 * k : 8 * k + 8, :] = sum(
                    prod[16 * a + 8 * p : 16 * a + 8 * p + 8, (k + a) * HALF : (k + a + 1) * HALF]
                    for a in range(3)
                )
        net = sum(
            jnp.dot(
                picked[p, 0 : 8 * total, :], weave[p], preferred_element_type=F32, precision=lax.Precision.HIGHEST
            )
            for p in range(2)
        )
        skip = 8 * (out_lo - state_lo)
        now = state[skip : skip + 8 * total, :]
        denoised = keep * now + mix * net
        now = now + move * (now - denoised)
        for k in range(total):
            value = now[8 * k : 8 * k + 8] * (natural * fine_ok(out_lo + k))
            if step == 0:
                state[8 * k : 8 * k + 8, :] = value
            else:
                out_ref[:, k, :] = value[0:4]


def shift(x, by):
    n = lax.axis_size("tile")
    return lax.ppermute(x, "tile", [(i, i + by) for i in range(n) if 0 <= i + by < n])


def turn(x, by):
    n = lax.axis_size("tile")
    return lax.ppermute(x, "tile", [(i, (i + by) % n) for i in range(n)])


VMEM = pl.BlockSpec(memory_space=pltpu.VMEM)
SMEM = pl.BlockSpec(memory_space=pltpu.SMEM)
PARAMS = pltpu.CompilerParams(vmem_limit_bytes=56 << 20)


def pair_map(count):
    return [[q - p if 0 <= q - p <= 2 else None for q in range(count)] for p in range(2)]


def small_weights(w_in, w_out):
    pad_in = jnp.pad(w_in.reshape(3, 3, 128, 4), ((0, 0), (0, 0), (0, 0), (0, 4)))
    zero = jnp.zeros((128, 8), BF)
    rows = []
    for p in range(2):
        cols = [
            pad_in[a, q - p] if 0 <= q - p <= 2 else zero for a in range(3) for q in range(4)
        ]
        rows.append(jnp.concatenate(cols, 1))
    packed_in = jnp.concatenate(rows, 0)
    pad_out = jnp.pad(w_out.reshape(3, 3, 4, 128), ((0, 0), (0, 0), (0, 4), (0, 0)))
    zero = jnp.zeros((8, 128), BF)
    rows = []
    for a in range(3):
        for p in range(2):
            cols = [q - p for q in (1, 2, 0, 3)]
            rows.append(jnp.concatenate([pad_out[a, b] if 0 <= b <= 2 else zero for b in cols], 1))
    return packed_in, jnp.concatenate(rows, 0)


def prep_call(w_enc, w_down, w_mid, w_dec):
    shapes = ((256, 1536), (256, 1152), (256, 2304), (256, 1536), (256, 1536), (256, 1536))
    return pl.pallas_call(
        prep_kernel,
        out_shape=[jax.ShapeDtypeStruct(s, BF) for s in shapes],
        in_specs=[VMEM] * 4,
        out_specs=[VMEM] * 6,
        compiler_params=PARAMS,
        name="prep",
    )(w_enc, w_down, w_mid, w_dec)


def main_call(width, coef, noise_parts, cond_parts, bias, weights):
    def rowbuf(n):
        return pltpu.VMEM((n, HALF, 256), BF)

    return pl.pallas_call(
        main_kernel,
        out_shape=jax.ShapeDtypeStruct((4, 4, 256), F32),
        in_specs=[SMEM, SMEM] + [VMEM] * 19,
        out_specs=VMEM,
        scratch_shapes=[
            pltpu.VMEM((31 * 8, 256), F32),
            pltpu.VMEM((31 * 8, 512), F32),
            rowbuf(29), rowbuf(29), rowbuf(27), rowbuf(27),
            rowbuf(13), rowbuf(13), rowbuf(13), rowbuf(11), rowbuf(11), rowbuf(11),
            rowbuf(19), rowbuf(19),
            pltpu.VMEM((48, 19 * HALF), F32),
            pltpu.VMEM((2, 17 * 8, HALF), F32),
        ],
        compiler_params=PARAMS,
        name="steps",
    )(width, coef, *noise_parts, *cond_parts, bias, *weights)


def coefficients(sigmas, w_sigma):
    now = sigmas[:2]
    var = now * now + SIGMA_DATA * SIGMA_DATA
    coef = jnp.stack(
        [
            jnp.broadcast_to(sigmas[0], (2,)),
            1.0 / jnp.sqrt(var),
            SIGMA_DATA * SIGMA_DATA / var,
            now * SIGMA_DATA / jnp.sqrt(var),
            (sigmas[1:] - now) / now,
        ],
        1,
    )
    bias = jnp.log(now)[:, None] * jnp.concatenate([w_sigma, w_sigma])[None, :]
    return coef, bias


def per_device(
    coarse_blocks, block_anchor, nest_width, sigmas, noise,
    w_context, w_in, w_sigma, w_enc, w_down, w_mid, w_dec, w_out,
):
    coef, bias = coefficients(sigmas, w_sigma)
    packed_in, packed_out = small_weights(w_in, w_out)

    chans = w_context.shape[1]
    cells = coarse_blocks.shape[1] // chans
    count = coarse_blocks.shape[0]
    blocks = coarse_blocks.reshape(count, chans, cells).transpose(0, 2, 1).reshape(count * cells, chans)
    partial = pl.pallas_call(
        encode_kernel,
        out_shape=jax.ShapeDtypeStruct((8, 2 * cells, 256), BF),
        in_specs=[SMEM, VMEM, VMEM],
        out_specs=VMEM,
        scratch_shapes=[pltpu.VMEM((count, cells, 256), F32)],
        compiler_params=PARAMS,
        name="encode",
    )(block_anchor, blocks, w_context)
    arrived = lax.all_to_all(partial, "band", 0, 0, tiled=True)

    own = noise[0].transpose(1, 0, 2).reshape(16, 256)
    near_up = turn(own, 1)
    near_down = turn(own, -1)
    three = jnp.concatenate([near_up, own, near_down], 0)
    far_up = turn(three, 3)
    far_down = turn(three, -3)

    enc, down, mid, dec2, even, odd = prep_call(w_enc, w_down, w_mid, w_dec)

    cond = (jnp.sum(arrived.astype(F32), axis=0) * (1.0 / math.sqrt(K // 2))).astype(BF)
    cond_up = shift(cond, 1)
    cond_down = shift(cond, -1)
    cond_far_up = shift(jnp.concatenate([cond_up, cond], 0), 2)
    cond_far_down = shift(jnp.concatenate([cond, cond_down], 0), -2)

    out = main_call(
        nest_width, coef,
        (far_up, near_up, own, near_down, far_down),
        (cond_far_up, cond_up, cond, cond_down, cond_far_down),
        bias,
        (packed_in, enc, down, mid, dec2, even, odd, packed_out),
    )
    return out[None]


def solution(mesh):
    return jax.shard_map(
        per_device,
        mesh=mesh,
        in_specs=(
            P("band", None), P(), P("band"), P(), P("band", None, "tile", None),
            P(), P(), P(), P(), P(), P(), P(), P(),
        ),
        out_specs=P("band", None, "tile", None),
        check_vma=False,
    )
```

```python
import functools
import math

import jax
import jax.numpy as jnp
from jax import lax
from jax.experimental import pallas as pl
from jax.experimental.pallas import tpu as pltpu
from jax.sharding import PartitionSpec as P

K = 96
SIGMA_DATA = 0.5
BF = jnp.bfloat16
F32 = jnp.float32
HALF = 128
ROWS = 256
NT = (((1,), (1,)), ((), ()))
TN = (((0,), (1,)), ((), ()))

STEP_ROWS = (
    dict(scaled=(-15, 31), first=(-14, 29), second=(-13, 27), third=(-6, 13), fourth=(-5, 11), fifth=(-8, 19), out=(-7, 17)),
    dict(scaled=(-7, 17), first=(-6, 15), second=(-5, 13), third=(-2, 6), fourth=(-1, 4), fifth=(-1, 6), out=(0, 4)),
)


def silu(v):
    h = 0.5 * v
    return h + h * jnp.tanh(h)


def dot_nt(a, b):
    return lax.dot_general(a, b, NT, preferred_element_type=F32)


def encode_kernel(anchor_ref, blocks_ref, w_ref, out_ref, enc_ref, flat, wide):
    band = lax.axis_index("band")
    tile = lax.axis_index("tile")
    count, cells = enc_ref.shape[:2]
    chans = w_ref.shape[0]
    tiles = blocks_ref.shape[1] // 128
    group = 8 * tiles

    flat[count * tiles :, :] = jnp.zeros((flat.shape[0] - count * tiles, 128), F32)
    for g in range(count // 16):
        for t in range(tiles):
            v = blocks_ref[16 * g : 16 * g + 16, 128 * t : 128 * t + 128].astype(F32)
            flat[2 * g * group + 8 * t : 2 * g * group + 8 * t + 8, :] = v[:8]
            flat[(2 * g + 1) * group + 8 * t : (2 * g + 1) * group + 8 * t + 8, :] = v[8:]

    w = w_ref[...].astype(F32)
    for half in range(2):
        wide[half, 0:chans, :] = w[:, 128 * half : 128 * half + 128]
        wide[half, chans:80, :] = jnp.zeros((80 - chans, 128), F32)
    weight = jnp.concatenate(
        [
            jnp.concatenate([wide[half, pl.ds(odd, 40, stride=2), :] for half in range(2)], 1)
            for odd in range(2)
        ],
        0,
    ).astype(BF)
    first = lax.broadcasted_iota(jnp.int32, (40, 128), 1) < 64

    def encode(g, carry):
        begin = pl.multiple_of(g * group, 8)
        cols = []
        for k in range(4):
            one = flat[pl.ds(begin + 2 * k, 40, stride=8), :]
            two = flat[pl.ds(begin + 2 * k + 1, 40, stride=8), :]
            even = jnp.where(first, one, pltpu.roll(two, 64, 1))
            odd = jnp.where(first, pltpu.roll(one, 64, 1), two)
            cols.append(jnp.concatenate([even, odd], 0))
        x = jnp.concatenate(cols, 1).astype(BF)
        v = lax.dot_general(x, weight, (((0,), (0,)), ((), ())), preferred_element_type=F32)
        v = silu(v).astype(BF).astype(F32)
        enc_ref[pl.ds(g * 8, 8)] = v.reshape(8, cells, 256)
        return carry

    lax.fori_loop(0, count // 8, encode, 0)

    def window(k, carry):
        nest = k // 2
        part = k % 2
        anchor = anchor_ref[nest, tile]
        begin = anchor + (band - anchor + 512) % 8 + part * 48
        row = (begin % 512) // 8
        total = enc_ref[row]
        for m in range(1, 6):
            total = total + enc_ref[(row + m) % count]
        out_ref[nest, pl.ds(pl.multiple_of(part * cells, cells), cells), :] = total.astype(BF)
        return carry

    lax.fori_loop(0, 16, window, 0)


def pair_weight(w, a):
    zero = jnp.zeros_like(w(a, 0))
    own = jnp.concatenate(
        [jnp.concatenate([w(a, 1), w(a, 2)], 1), jnp.concatenate([w(a, 0), w(a, 1)], 1)], 0
    )
    rim = jnp.concatenate(
        [jnp.concatenate([w(a, 0), zero], 1), jnp.concatenate([zero, w(a, 2)], 1)], 0
    )
    return own, rim


def prep_kernel(w_enc, w_down, w_mid, w_dec, enc_o, down_o, mid_o, dec2_o, even_o, odd_o):
    for a in range(3):
        own, rim = pair_weight(lambda i, b: w_enc[3 * i + b], a)
        enc_o[:, 512 * a : 512 * a + 256] = own
        enc_o[:, 512 * a + 256 : 512 * a + 512] = rim
        own, rim = pair_weight(lambda i, b: w_dec[3 * i + b, :, 0:128], a)
        dec2_o[:, 512 * a : 512 * a + 256] = own
        dec2_o[:, 512 * a + 256 : 512 * a + 512] = rim
        down_o[:, 256 * a : 256 * a + 128] = w_down[3 * a + 1]
        down_o[:, 256 * a + 128 : 256 * a + 256] = w_down[3 * a + 2]
        down_o[:, 768 + 128 * a : 896 + 128 * a] = w_down[3 * a]
        for b in range(3):
            mid_o[:, 768 * a + 256 * b : 768 * a + 256 * b + 256] = w_mid[3 * a + b]

    def up(a, b):
        return w_dec[3 * a + b, :, 128:384].astype(F32)

    for o_ref, sets in ((even_o, ((0,), (1, 2))), (odd_o, ((0, 1), (2,)))):
        for k, taps in enumerate(sets):
            col = [sum(up(a, b) for a in taps) for b in range(3)]
            zero = jnp.zeros_like(col[0])
            o_ref[:, 768 * k : 768 * k + 256] = jnp.concatenate([col[0], zero], 0).astype(BF)
            o_ref[:, 768 * k + 256 : 768 * k + 512] = jnp.concatenate(
                [col[1] + col[2], col[0] + col[1]], 0
            ).astype(BF)
            o_ref[:, 768 * k + 512 : 768 * k + 768] = jnp.concatenate([zero, col[2]], 0).astype(BF)


class Field:
    def __init__(self, width):
        self.tile = lax.axis_index("tile")
        lane = lax.broadcasted_iota(jnp.int32, (HALF, 256), 1)
        pair = lax.broadcasted_iota(jnp.int32, (HALF, 256), 0)
        self.colmask = (2 * pair + lane // 128 < width).astype(F32)
        self.halfmask = (2 * pair < width).astype(F32)
        self.natural = (lax.broadcasted_iota(jnp.int32, (8, 256), 1) < width).astype(F32)

    def fine_ok(self, rho):
        row = self.tile * 4 + rho
        return jnp.logical_and(row >= 0, row < ROWS).astype(F32)

    def half_ok(self, h):
        row = self.tile * 2 + h
        return jnp.logical_and(row >= 0, row < ROWS // 2).astype(F32)

    def keep_pairs(self, y, center, rim, at, n, lo):
        y = jnp.concatenate(
            [y[k * HALF : (k + 1) * HALF] * (self.colmask * self.fine_ok(lo + at + k)) for k in range(n)], 0
        )
        side = jnp.concatenate([slide(y[:, 128:], 1), slide(y[:, :128], -1)], 1).astype(BF)
        y = y.astype(BF)
        for k in range(n):
            center[at + k] = y[k * HALF : (k + 1) * HALF]
            rim[at + k] = side[k * HALF : (k + 1) * HALF]

    def keep_half(self, y, center, left, right, at, n, lo):
        y = jnp.concatenate(
            [y[k * HALF : (k + 1) * HALF] * (self.halfmask * self.half_ok(lo + at + k)) for k in range(n)], 0
        )
        sides = (slide(y, 1).astype(BF), slide(y, -1).astype(BF))
        y = y.astype(BF)
        for k in range(n):
            cut = slice(k * HALF, (k + 1) * HALF)
            center[at + k] = y[cut]
            left[at + k] = sides[0][cut]
            right[at + k] = sides[1][cut]


def slide(x, by):
    rows = x.shape[0]
    edge = 0 if by == 1 else HALF - 1
    where = lax.broadcasted_iota(jnp.int32, x.shape, 0) % HALF
    return jnp.where(where == edge, 0.0, pltpu.roll(x, by % rows, 0))


def stacked(ref, at, n, step=1):
    return jnp.concatenate([ref[at + step * k] for k in range(n)], 0)


def chunks(total, size, body):
    full = total // size
    if full == 1:
        body(0, size)
    elif full:
        lax.fori_loop(0, full, lambda i, c: (body(i * size, size), c)[1], 0)
    if total % size:
        body(full * size, total % size)


def encoder(field, rows, state, scale, bias, w_in, w_enc, spread, firstc, firste, secondc, seconde, size):
    col = lax.broadcasted_iota(jnp.int32, (256, 512), 0)
    place = lax.broadcasted_iota(jnp.int32, (256, 512), 1)
    pick = (col == 2 * (place % 128) + place // 128 - 1).astype(F32).astype(BF)
    n_scaled = rows["scaled"][1]
    scaled = (state[0 : 8 * n_scaled, :] * scale).astype(BF)
    spread[0 : 8 * n_scaled, :] = jnp.dot(scaled, pick, preferred_element_type=F32)
    first_lo, total = rows["first"]

    def first_rows(at, n):
        cols = []
        for k in range(n):
            cols.append(
                jnp.concatenate(
                    [
                        spread[pl.ds(pl.multiple_of((at + k + a) * 8, 8), 8), 128 * q : 128 * q + 128]
                        for a in range(3)
                        for q in range(4)
                    ],
                    0,
                )
            )
        x = jnp.concatenate(cols, 1).astype(BF)
        y = lax.dot_general(x, w_in[...], TN, preferred_element_type=F32)
        field.keep_pairs(silu(y + bias), firstc, firste, at, n, first_lo)

    chunks(total, 5, first_rows)
    second_lo, total = rows["second"]

    def second_rows(at, n):
        x = jnp.concatenate([stacked(ref, at + a, n) for a in range(3) for ref in (firstc, firste)], 1)
        field.keep_pairs(silu(dot_nt(x, w_enc[...])), secondc, seconde, at, n, second_lo)

    chunks(total, size, second_rows)


def first_kernel(
    width_ref, coef_ref, own, up3, down3, near_up, near_down, bias_ref, w_in, w_enc,
    state_ref, secondc, seconde,
    state, spread, firstc, firste,
):
    field = Field(width_ref[0])
    rows = STEP_ROWS[0]
    start = coef_ref[0, 0]
    empty = jnp.zeros((4, 256), F32)
    pieces = {-3: up3, 0: own, 3: down3}
    for tile_off in range(-4, 4):
        if tile_off in pieces:
            value = pieces[tile_off][...]
        else:
            ref = near_up if (tile_off + 1) % 3 == 0 else near_down
            slot = (tile_off + (1 if ref is near_up else -1)) // 3 + 1
            begin = 128 + 16 * slot
            value = ref[begin : begin + 16, :].astype(F32) + ref[begin + 48 : begin + 64, :].astype(F32)
        for r in range(4):
            rho = 4 * tile_off + r
            if rho >= -15:
                row = jnp.concatenate([value[4 * r : 4 * r + 4], empty], 0)
                state[8 * (rho + 15) : 8 * (rho + 16), :] = start * row * (field.natural * field.fine_ok(rho))
    out_lo, n_out = rows["out"]
    state_ref[...] = state[8 * (out_lo + 15) : 8 * (out_lo + 15 + n_out), :]
    encoder(
        field, rows, state, coef_ref[0, 1], bias_ref[0:1, :], w_in, w_enc,
        spread, firstc, firste, secondc, seconde, 9,
    )


def second_kernel(
    width_ref, coef_ref, state_in, secondc0, seconde0,
    far_up, near_up, near_down, far_down, own_cond,
    bias_ref, w_in, w_enc, w_down, w_mid, w_dec2, w_even, w_odd, w_out,
    out_ref,
    state, spread, firstc, firste, secondc1, seconde1, third, thirdl, thirdr, fourth, fourthl, fourthr,
    fifthc, fifthe, prod, picked,
):
    field = Field(width_ref[0])
    weave_j = lax.broadcasted_iota(jnp.int32, (HALF, 256), 0)
    weave_c = lax.broadcasted_iota(jnp.int32, (HALF, 256), 1)
    weave = [(weave_c == 2 * weave_j + p).astype(F32) for p in range(2)]
    repeat = (
        lax.broadcasted_iota(jnp.int32, (HALF, 64), 0) // 2 == lax.broadcasted_iota(jnp.int32, (HALF, 64), 1)
    ).astype(F32).astype(BF)
    conds = (
        (far_up, 0), (far_up, 1), (far_up, 2), (far_up, 3),
        (near_up, 0), (near_up, 1), (own_cond, 0), (own_cond, 1), (near_down, 0), (near_down, 1),
        (far_down, 0), (far_down, 1), (far_down, 2), (far_down, 3),
    )

    for step in range(2):
        rows = STEP_ROWS[step]
        scale, keep, mix, move = (coef_ref[step, 1 + i] for i in range(4))
        if step == 0:
            secondc, seconde = secondc0, seconde0
        else:
            secondc, seconde = secondc1, seconde1
            encoder(
                field, rows, state, scale, bias_ref[1:2, :], w_in, w_enc,
                spread, firstc, firste, secondc, seconde, 13,
            )

        second_lo = rows["second"][0]
        third_lo, total = rows["third"]

        def third_rows(at, n):
            begin = 2 * third_lo - 1 - second_lo + 2 * at
            x = jnp.concatenate(
                [stacked(secondc, begin + a, n, 2) for a in range(3)]
                + [
                    jnp.concatenate([seconde[begin + a + 2 * k][:, :128] for k in range(n)], 0)
                    for a in range(3)
                ],
                1,
            )
            y = dot_nt(x, w_down[...])
            add = []
            for k in range(n):
                ref, r = conds[third_lo + at + k + 6]
                add.append(jnp.dot(repeat, ref[64 * r : 64 * r + 64, :], preferred_element_type=F32))
            y = y + jnp.concatenate(add, 0)
            field.keep_half(silu(y), third, thirdl, thirdr, at, n, third_lo)

        for at in range(0, total, 7):
            third_rows(at, min(7, total - at))

        fourth_lo, total = rows["fourth"]

        def fourth_rows(at, n):
            begin = fourth_lo - 1 - third_lo + at
            x = jnp.concatenate(
                [stacked(ref, begin + a, n) for a in range(3) for ref in (thirdl, third, thirdr)], 1
            )
            field.keep_half(silu(dot_nt(x, w_mid[...])), fourth, fourthl, fourthr, at, n, fourth_lo)

        for at in range(0, total, 6):
            fourth_rows(at, min(6, total - at))

        fifth_lo, total = rows["fifth"]

        def fifth_rows(at, n):
            rho = fifth_lo + at
            odd = rho % 2
            begin = rho - 1 - second_lo
            h = (rho - odd) // 2 - fourth_lo - (0 if odd else 1)
            x = jnp.concatenate(
                [stacked(ref, begin + a, n, 2) for a in range(3) for ref in (secondc, seconde)], 1
            )
            z = jnp.concatenate(
                [stacked(ref, h + a, n) for a in range(2) for ref in (fourthl, fourth, fourthr)], 1
            )
            y = silu(dot_nt(x, w_dec2[...]) + dot_nt(z, (w_odd if odd else w_even)[...]))
            for k in range(n):
                field.keep_pairs(y[k * HALF : (k + 1) * HALF], fifthc, fifthe, at + 2 * k, 1, fifth_lo)

        for parity in range(2):
            n_rows = (total - parity + 1) // 2
            for at in range(0, n_rows, 5):
                fifth_rows(parity + 2 * at, min(5, n_rows - at))

        def out_rows(at, n):
            x = jnp.concatenate([stacked(fifthc, at, n), stacked(fifthe, at, n)], 1)
            prod[:, at * HALF : (at + n) * HALF] = dot_nt(w_out[...], x)

        for at in range(0, total, 10):
            out_rows(at, min(10, total - at))
        out_lo, total = rows["out"]
        for k in range(total):
            for p in range(2):
                picked[p, 8 * k : 8 * k + 8, :] = sum(
                    prod[16 * a + 8 * p : 16 * a + 8 * p + 8, (k + a) * HALF : (k + a + 1) * HALF]
                    for a in range(3)
                )
        net = sum(
            jnp.dot(
                picked[p, 0 : 8 * total, :], weave[p], preferred_element_type=F32, precision=lax.Precision.HIGHEST
            )
            for p in range(2)
        )
        if step == 0:
            now = state_in[...]
        else:
            skip = 8 * (out_lo - rows["scaled"][0])
            now = state[skip : skip + 8 * total, :]
        denoised = keep * now + mix * net
        now = now + move * (now - denoised)
        for k in range(total):
            value = now[8 * k : 8 * k + 8] * (field.natural * field.fine_ok(out_lo + k))
            if step == 0:
                state[8 * k : 8 * k + 8, :] = value
            else:
                out_ref[:, k, :] = value[0:4]


def turn(x, by):
    n = lax.axis_size("tile")
    return lax.ppermute(x, "tile", [(i, (i + by) % n) for i in range(n)])


VMEM = pl.BlockSpec(memory_space=pltpu.VMEM)
SMEM = pl.BlockSpec(memory_space=pltpu.SMEM)
PARAMS = pltpu.CompilerParams(vmem_limit_bytes=56 << 20)


def pair_map(count):
    return [[q - p if 0 <= q - p <= 2 else None for q in range(count)] for p in range(2)]


def small_weights(w_in, w_out):
    pad_in = jnp.pad(w_in.reshape(3, 3, 128, 4), ((0, 0), (0, 0), (0, 0), (0, 4)))
    zero = jnp.zeros((128, 8), BF)
    rows = []
    for p in range(2):
        cols = [
            pad_in[a, q - p] if 0 <= q - p <= 2 else zero for a in range(3) for q in range(4)
        ]
        rows.append(jnp.concatenate(cols, 1))
    packed_in = jnp.concatenate(rows, 0)
    pad_out = jnp.pad(w_out.reshape(3, 3, 4, 128), ((0, 0), (0, 0), (0, 4), (0, 0)))
    zero = jnp.zeros((8, 128), BF)
    rows = []
    for a in range(3):
        for p in range(2):
            cols = [q - p for q in (1, 2, 0, 3)]
            rows.append(jnp.concatenate([pad_out[a, b] if 0 <= b <= 2 else zero for b in cols], 1))
    return packed_in, jnp.concatenate(rows, 0)


def prep_call(w_enc, w_down, w_mid, w_dec):
    shapes = ((256, 1536), (256, 1152), (256, 2304), (256, 1536), (256, 1536), (256, 1536))
    return pl.pallas_call(
        prep_kernel,
        out_shape=[jax.ShapeDtypeStruct(s, BF) for s in shapes],
        in_specs=[VMEM] * 4,
        out_specs=[VMEM] * 6,
        compiler_params=PARAMS,
        name="prep",
    )(w_enc, w_down, w_mid, w_dec)


def rowbuf(n):
    return pltpu.VMEM((n, HALF, 256), BF)


def cost(passes):
    return pl.CostEstimate(flops=passes * 128 * 65536 * 2, bytes_accessed=1 << 20, transcendentals=0)


def first_call(width, coef, noise_parts, bias, w_in, w_enc):
    return pl.pallas_call(
        first_kernel,
        out_shape=[
            jax.ShapeDtypeStruct((17 * 8, 256), F32),
            jax.ShapeDtypeStruct((27, HALF, 256), BF),
            jax.ShapeDtypeStruct((27, HALF, 256), BF),
        ],
        in_specs=[SMEM, SMEM] + [VMEM] * 8,
        out_specs=[VMEM] * 3,
        scratch_shapes=[
            pltpu.VMEM((31 * 8, 256), F32), pltpu.VMEM((31 * 8, 512), F32), rowbuf(29), rowbuf(29),
        ],
        compiler_params=PARAMS,
        cost_estimate=cost(200),
        name="first",
    )(width, coef, *noise_parts, bias, w_in, w_enc)


def second_call(width, coef, fields, cond_parts, bias, weights):
    return pl.pallas_call(
        second_kernel,
        out_shape=jax.ShapeDtypeStruct((4, 4, 256), F32),
        in_specs=[SMEM, SMEM] + [VMEM] * 17,
        out_specs=VMEM,
        scratch_shapes=[
            pltpu.VMEM((17 * 8, 256), F32),
            pltpu.VMEM((17 * 8, 512), F32),
            rowbuf(15), rowbuf(15), rowbuf(13), rowbuf(13),
            rowbuf(13), rowbuf(13), rowbuf(13), rowbuf(11), rowbuf(11), rowbuf(11),
            rowbuf(19), rowbuf(19),
            pltpu.VMEM((48, 19 * HALF), F32),
            pltpu.VMEM((2, 17 * 8, HALF), F32),
        ],
        compiler_params=PARAMS,
        cost_estimate=cost(600),
        name="second",
    )(width, coef, *fields, *cond_parts, bias, *weights)


def encode_call(block_anchor, coarse_blocks, w_context):
    chans = w_context.shape[1]
    cells = coarse_blocks.shape[1] // chans
    count = coarse_blocks.shape[0]
    tiles = coarse_blocks.shape[1] // 128
    return pl.pallas_call(
        encode_kernel,
        out_shape=jax.ShapeDtypeStruct((8, 2 * cells, 256), BF),
        in_specs=[SMEM, VMEM, VMEM],
        out_specs=VMEM,
        scratch_shapes=[
            pltpu.VMEM((count, cells, 256), F32),
            pltpu.VMEM((count * tiles + 64, 128), F32),
            pltpu.VMEM((2, 80, 128), F32),
        ],
        compiler_params=PARAMS,
        cost_estimate=cost(100),
        name="encode",
    )(block_anchor, coarse_blocks, w_context.T)


def coefficients(sigmas, w_sigma):
    now = sigmas[:2]
    var = now * now + SIGMA_DATA * SIGMA_DATA
    coef = jnp.stack(
        [
            jnp.broadcast_to(sigmas[0], (2,)),
            1.0 / jnp.sqrt(var),
            SIGMA_DATA * SIGMA_DATA / var,
            now * SIGMA_DATA / jnp.sqrt(var),
            (sigmas[1:] - now) / now,
        ],
        1,
    )
    bias = jnp.log(now)[:, None] * jnp.concatenate([w_sigma, w_sigma])[None, :]
    return coef, bias


def per_device(
    coarse_blocks, block_anchor, nest_width, sigmas, noise,
    w_context, w_in, w_sigma, w_enc, w_down, w_mid, w_dec, w_out,
):
    partial = encode_call(block_anchor, coarse_blocks, w_context)
    arrived = lax.all_to_all(partial, "band", 0, 0, tiled=True)

    held = lax.optimization_barrier((partial, noise, sigmas, w_sigma, w_in, w_out, w_enc, w_down, w_mid, w_dec))
    noise, sigmas, w_sigma, w_in, w_out, w_enc, w_down, w_mid, w_dec = held[1:]
    own = noise[0].transpose(1, 0, 2).reshape(16, 256)
    up3 = turn(own, 3)
    down3 = turn(own, -3)
    coef, bias = coefficients(sigmas, w_sigma)
    packed_in, packed_out = small_weights(w_in, w_out)
    enc, down, mid, dec2, even, odd = prep_call(w_enc, w_down, w_mid, w_dec)
    arrived, own, up3, down3, coef, bias, packed_in, packed_out, enc, down, mid, dec2, even, odd = (
        lax.optimization_barrier(
            (arrived, own, up3, down3, coef, bias, packed_in, packed_out, enc, down, mid, dec2, even, odd)
        )
    )

    cond = (jnp.sum(arrived.astype(F32), axis=0) * (1.0 / math.sqrt(K // 2))).astype(BF)
    noises = jnp.concatenate([up3, own, down3], 0)
    high = lax.reduce_precision(noises, 8, 7)
    parcel = jnp.concatenate([cond, high.astype(BF), (noises - high).astype(BF)], 0)
    near_up = turn(parcel, 1)
    near_down = turn(parcel, -1)
    far_up = turn(jnp.concatenate([near_up[:128], cond], 0), 2)
    far_down = turn(jnp.concatenate([cond, near_down[:128]], 0), -2)

    fields = first_call(nest_width, coef, (own, up3, down3, near_up, near_down), bias, packed_in, enc)
    out = second_call(
        nest_width, coef, fields, (far_up, near_up, near_down, far_down, cond), bias,
        (packed_in, enc, down, mid, dec2, even, odd, packed_out),
    )
    return out[None]


def solution(mesh):
    return jax.shard_map(
        per_device,
        mesh=mesh,
        in_specs=(
            P("band", None), P(), P("band"), P(), P("band", None, "tile", None),
            P(), P(), P(), P(), P(), P(), P(), P(),
        ),
        out_specs=P("band", None, "tile", None),
        check_vma=False,
    )
```

```python
import functools
import math

import jax
import jax.numpy as jnp
from jax import lax
from jax.experimental import pallas as pl
from jax.experimental.pallas import tpu as pltpu
from jax.sharding import PartitionSpec as P

K = 96
SIGMA_DATA = 0.5
BF = jnp.bfloat16
F32 = jnp.float32
HALF = 128
ROWS = 256
NT = (((1,), (1,)), ((), ()))
TN = (((0,), (0,)), ((), ()))

STEP_ROWS = (
    dict(scaled=(-15, 31), first=(-14, 29), second=(-13, 27), third=(-6, 13), fourth=(-5, 11), fifth=(-8, 19), out=(-7, 17)),
    dict(scaled=(-7, 17), first=(-6, 15), second=(-5, 13), third=(-2, 6), fourth=(-1, 4), fifth=(-1, 6), out=(0, 4)),
)


def silu(v):
    h = 0.5 * v
    return h + h * jnp.tanh(h)


def dot_nt(a, b):
    return lax.dot_general(a, b, NT, preferred_element_type=F32)


def encode_kernel(anchor_ref, blocks_ref, w_ref, out_ref, enc_ref, flat, wide):
    band = lax.axis_index("band")
    tile = lax.axis_index("tile")
    count = blocks_ref.shape[0]
    cells = enc_ref.shape[1]
    chans = w_ref.shape[0]
    tiles = blocks_ref.shape[1] // 128
    group = 8 * tiles

    flat[count * tiles :, :] = jnp.zeros((flat.shape[0] - count * tiles, 128), F32)
    for g in range(count // 16):
        for t in range(tiles):
            v = blocks_ref[16 * g : 16 * g + 16, 128 * t : 128 * t + 128].astype(F32)
            flat[2 * g * group + 8 * t : 2 * g * group + 8 * t + 8, :] = v[:8]
            flat[(2 * g + 1) * group + 8 * t : (2 * g + 1) * group + 8 * t + 8, :] = v[8:]

    w = w_ref[...].astype(F32)
    for half in range(2):
        wide[half, 0:chans, :] = w[:, 128 * half : 128 * half + 128]
        wide[half, chans:80, :] = jnp.zeros((80 - chans, 128), F32)
    weight = jnp.concatenate(
        [
            jnp.concatenate([wide[half, pl.ds(odd, 40, stride=2), :] for half in range(2)], 1)
            for odd in range(2)
        ],
        0,
    ).astype(BF)
    first = lax.broadcasted_iota(jnp.int32, (40, 128), 1) < 64

    def encode(g, carry):
        begin = pl.multiple_of(g * group, 8)
        cols = []
        for k in range(4):
            one = flat[pl.ds(begin + 2 * k, 40, stride=8), :]
            two = flat[pl.ds(begin + 2 * k + 1, 40, stride=8), :]
            even = jnp.where(first, one, pltpu.roll(two, 64, 1))
            odd = jnp.where(first, pltpu.roll(one, 64, 1), two)
            cols.append(jnp.concatenate([even, odd], 0))
        x = jnp.concatenate(cols, 1).astype(BF)
        v = lax.dot_general(x, weight, TN, preferred_element_type=F32)
        v = silu(v).astype(BF).astype(F32)
        enc_ref[pl.ds(g * 8, 8)] = v.reshape(8, cells, 256)
        return carry

    lax.fori_loop(0, count // 8, encode, 0)

    enc_ref[pl.ds(count, 8)] = enc_ref[pl.ds(0, 8)]

    def window(k, carry):
        nest = k // 6
        part = k % 6
        at = jnp.clip(tile + part // 2 - 1, 0, anchor_ref.shape[1] - 1)
        anchor = anchor_ref[nest, at]
        begin = anchor + (band - anchor + 512) % 8 + (part % 2) * 48
        row = (begin % 512) // 8
        total = enc_ref[row]
        for m in range(1, 6):
            total = total + enc_ref[row + m]
        out_ref[nest, pl.ds(pl.multiple_of(part * cells, cells), cells), :] = total.astype(BF)
        return carry

    lax.fori_loop(0, 48, window, 0, unroll=4)


def pair_weight(w, a):
    zero = jnp.zeros_like(w(a, 0))
    own = jnp.concatenate(
        [jnp.concatenate([w(a, 1), w(a, 2)], 1), jnp.concatenate([w(a, 0), w(a, 1)], 1)], 0
    )
    rim = jnp.concatenate(
        [jnp.concatenate([w(a, 0), zero], 1), jnp.concatenate([zero, w(a, 2)], 1)], 0
    )
    return own, rim


def prep_kernel(
    w_in, w_enc, w_down, w_mid, w_dec, w_out, in_o, enc_o, down_o, mid_o, dec2_o, even_o, odd_o, out_o
):
    def tall(ref, a, b):
        if not 0 <= b <= 2:
            return jnp.zeros((8, 128), F32)
        return jnp.concatenate([ref[3 * a + b].astype(F32), jnp.zeros((4, 128), F32)], 0)

    in_o[...] = jnp.concatenate(
        [
            jnp.concatenate([tall(w_in, a, q - p) for p in range(2)], 1)
            for a in range(3)
            for q in range(4)
        ],
        0,
    ).astype(BF)
    out_o[...] = jnp.concatenate(
        [
            jnp.concatenate([tall(w_out, a, q - p) for q in (1, 2, 0, 3)], 1)
            for a in range(3)
            for p in range(2)
        ],
        0,
    ).astype(BF)
    for a in range(3):
        own, rim = pair_weight(lambda i, b: w_enc[3 * i + b], a)
        enc_o[:, 512 * a : 512 * a + 256] = own
        enc_o[:, 512 * a + 256 : 512 * a + 512] = rim
        own, rim = pair_weight(lambda i, b: w_dec[3 * i + b, :, 0:128], a)
        dec2_o[:, 512 * a : 512 * a + 256] = own
        dec2_o[:, 512 * a + 256 : 512 * a + 512] = rim
        down_o[:, 256 * a : 256 * a + 128] = w_down[3 * a + 1]
        down_o[:, 256 * a + 128 : 256 * a + 256] = w_down[3 * a + 2]
        down_o[:, 768 + 128 * a : 896 + 128 * a] = w_down[3 * a]
        for b in range(3):
            mid_o[:, 768 * a + 256 * b : 768 * a + 256 * b + 256] = w_mid[3 * a + b]

    def up(a, b):
        return w_dec[3 * a + b, :, 128:384].astype(F32)

    for o_ref, sets in ((even_o, ((0,), (1, 2))), (odd_o, ((0, 1), (2,)))):
        for k, taps in enumerate(sets):
            col = [sum(up(a, b) for a in taps) for b in range(3)]
            zero = jnp.zeros_like(col[0])
            o_ref[:, 768 * k : 768 * k + 256] = jnp.concatenate([col[0], zero], 0).astype(BF)
            o_ref[:, 768 * k + 256 : 768 * k + 512] = jnp.concatenate(
                [col[1] + col[2], col[0] + col[1]], 0
            ).astype(BF)
            o_ref[:, 768 * k + 512 : 768 * k + 768] = jnp.concatenate([zero, col[2]], 0).astype(BF)


class Field:
    def __init__(self, width):
        self.tile = lax.axis_index("tile")
        lane = lax.broadcasted_iota(jnp.int32, (HALF, 256), 1)
        pair = lax.broadcasted_iota(jnp.int32, (HALF, 256), 0)
        self.colmask = (2 * pair + lane // 128 < width).astype(F32)
        self.halfmask = (2 * pair < width).astype(F32)
        self.natural = (lax.broadcasted_iota(jnp.int32, (8, 256), 1) < width).astype(F32)

    def fine_ok(self, rho):
        row = self.tile * 4 + rho
        return jnp.logical_and(row >= 0, row < ROWS).astype(F32)

    def half_ok(self, h):
        row = self.tile * 2 + h
        return jnp.logical_and(row >= 0, row < ROWS // 2).astype(F32)

    def keep_pairs(self, y, center, rim, at, n, lo):
        y = jnp.concatenate(
            [y[k * HALF : (k + 1) * HALF] * (self.colmask * self.fine_ok(lo + at + k)) for k in range(n)], 0
        )
        side = jnp.concatenate([slide(y[:, 128:], 1), slide(y[:, :128], -1)], 1).astype(BF)
        y = y.astype(BF)
        for k in range(n):
            center[at + k] = y[k * HALF : (k + 1) * HALF]
            rim[at + k] = side[k * HALF : (k + 1) * HALF]

    def keep_half(self, y, center, left, right, at, n, lo):
        y = jnp.concatenate(
            [y[k * HALF : (k + 1) * HALF] * (self.halfmask * self.half_ok(lo + at + k)) for k in range(n)], 0
        )
        sides = (slide(y, 1).astype(BF), slide(y, -1).astype(BF))
        y = y.astype(BF)
        for k in range(n):
            cut = slice(k * HALF, (k + 1) * HALF)
            center[at + k] = y[cut]
            left[at + k] = sides[0][cut]
            right[at + k] = sides[1][cut]


def levels(sigma_ref, step):
    now = jnp.full((1, 256), sigma_ref[step], F32)
    after = jnp.full((1, 256), sigma_ref[step + 1], F32)
    var = now * now + SIGMA_DATA * SIGMA_DATA
    root = jnp.sqrt(var)
    return now, 1.0 / root, SIGMA_DATA * SIGMA_DATA / var, now * SIGMA_DATA / root, (after - now) / now


def embedding(w_sigma, now):
    return jnp.concatenate([w_sigma[...], w_sigma[...]], 1) * jnp.log(now)


def slide(x, by):
    rows = x.shape[0]
    edge = 0 if by == 1 else HALF - 1
    where = lax.broadcasted_iota(jnp.int32, x.shape, 0) % HALF
    return jnp.where(where == edge, 0.0, pltpu.roll(x, by % rows, 0))


def stacked(ref, at, n, step=1):
    return jnp.concatenate([ref[at + step * k] for k in range(n)], 0)


def chunks(total, size, body):
    full = total // size
    if full == 1:
        body(0, size)
    elif full:
        lax.fori_loop(0, full, lambda i, c: (body(i * size, size), c)[1], 0)
    if total % size:
        body(full * size, total % size)


def encoder(field, rows, state, scale, bias, w_in, w_enc, spread, firstc, firste, secondc, seconde, size):
    col = lax.broadcasted_iota(jnp.int32, (256, 512), 0)
    place = lax.broadcasted_iota(jnp.int32, (256, 512), 1)
    pick = (col == 2 * (place % 128) + place // 128 - 1).astype(F32).astype(BF)
    n_scaled = rows["scaled"][1]
    scaled = (state[0 : 8 * n_scaled, :] * scale).astype(BF)
    spread[0 : 8 * n_scaled, :] = jnp.dot(scaled, pick, preferred_element_type=F32)
    first_lo, total = rows["first"]

    def first_rows(at, n):
        cols = []
        for k in range(n):
            cols.append(
                jnp.concatenate(
                    [
                        spread[pl.ds(pl.multiple_of((at + k + a) * 8, 8), 8), 128 * q : 128 * q + 128]
                        for a in range(3)
                        for q in range(4)
                    ],
                    0,
                )
            )
        x = jnp.concatenate(cols, 1).astype(BF)
        y = lax.dot_general(x, w_in[...], TN, preferred_element_type=F32)
        field.keep_pairs(silu(y + bias), firstc, firste, at, n, first_lo)

    chunks(total, 5, first_rows)
    second_lo, total = rows["second"]

    def second_rows(at, n):
        x = jnp.concatenate([stacked(ref, at + a, n) for a in range(3) for ref in (firstc, firste)], 1)
        field.keep_pairs(silu(dot_nt(x, w_enc[...])), secondc, seconde, at, n, second_lo)

    chunks(total, size, second_rows)


def first_kernel(
    width_ref, sigma_ref, own, up3, down3, near_up, near_down, w_sigma, w_in, w_enc,
    state_ref, secondc, seconde,
    state, spread, firstc, firste,
):
    field = Field(width_ref[0])
    rows = STEP_ROWS[0]
    now, scale = levels(sigma_ref, 0)[:2]
    empty = jnp.zeros((4, 256), F32)
    pieces = {-3: (up3, 0), 0: (own, 0), 3: (down3, 0)}
    for slot in range(3):
        pieces[3 * slot - 4] = (near_up, 16 * slot)
        pieces[3 * slot - 2] = (near_down, 16 * slot)
    for tile_off in range(-4, 4):
        ref, begin = pieces[tile_off]
        for r in range(4):
            rho = 4 * tile_off + r
            if rho >= -15:
                row = jnp.concatenate([ref[begin + 4 * r : begin + 4 * r + 4, :], empty], 0)
                state[8 * (rho + 15) : 8 * (rho + 16), :] = now * row * (field.natural * field.fine_ok(rho))
    out_lo, n_out = rows["out"]
    state_ref[...] = state[8 * (out_lo + 15) : 8 * (out_lo + 15 + n_out), :]
    encoder(
        field, rows, state, scale, embedding(w_sigma, now), w_in, w_enc,
        spread, firstc, firste, secondc, seconde, 9,
    )


def second_kernel(
    width_ref, sigma_ref, state_in, secondc0, seconde0, far_up, near, far_down, w_sigma, w_in, w_enc, w_down, w_mid, w_dec2, w_even, w_odd, w_out,
    out_ref,
    state, spread, firstc, firste, secondc1, seconde1, third, thirdl, thirdr, fourth, fourthl, fourthr,
    fifthc, fifthe, prod, picked,
):
    field = Field(width_ref[0])
    weave_j = lax.broadcasted_iota(jnp.int32, (HALF, 256), 0)
    weave_c = lax.broadcasted_iota(jnp.int32, (HALF, 256), 1)
    weave = [(weave_c == 2 * weave_j + p).astype(F32) for p in range(2)]
    repeat = (
        lax.broadcasted_iota(jnp.int32, (HALF, 64), 0) // 2 == lax.broadcasted_iota(jnp.int32, (HALF, 64), 1)
    ).astype(F32).astype(BF)
    conds = [(ref, r) for ref, n in ((far_up, 4), (near, 6), (far_down, 4)) for r in range(n)]

    for step in range(2):
        rows = STEP_ROWS[step]
        sigma, scale, keep, mix, move = levels(sigma_ref, step)
        if step == 0:
            secondc, seconde = secondc0, seconde0
        else:
            secondc, seconde = secondc1, seconde1
            encoder(
                field, rows, state, scale, embedding(w_sigma, sigma), w_in, w_enc,
                spread, firstc, firste, secondc, seconde, 13,
            )

        second_lo = rows["second"][0]
        third_lo, total = rows["third"]

        def third_rows(at, n):
            begin = 2 * third_lo - 1 - second_lo + 2 * at
            x = jnp.concatenate(
                [stacked(secondc, begin + a, n, 2) for a in range(3)]
                + [
                    jnp.concatenate([seconde[begin + a + 2 * k][:, :128] for k in range(n)], 0)
                    for a in range(3)
                ],
                1,
            )
            y = dot_nt(x, w_down[...])
            add = []
            for k in range(n):
                ref, r = conds[third_lo + at + k + 6]
                add.append(jnp.dot(repeat, ref[64 * r : 64 * r + 64, :], preferred_element_type=F32))
            y = y + jnp.concatenate(add, 0)
            field.keep_half(silu(y), third, thirdl, thirdr, at, n, third_lo)

        for at in range(0, total, 7):
            third_rows(at, min(7, total - at))

        fourth_lo, total = rows["fourth"]

        def fourth_rows(at, n):
            begin = fourth_lo - 1 - third_lo + at
            x = jnp.concatenate(
                [stacked(ref, begin + a, n) for a in range(3) for ref in (thirdl, third, thirdr)], 1
            )
            field.keep_half(silu(dot_nt(x, w_mid[...])), fourth, fourthl, fourthr, at, n, fourth_lo)

        for at in range(0, total, 6):
            fourth_rows(at, min(6, total - at))

        fifth_lo, total = rows["fifth"]

        def fifth_rows(at, n):
            rho = fifth_lo + at
            odd = rho % 2
            begin = rho - 1 - second_lo
            h = (rho - odd) // 2 - fourth_lo - (0 if odd else 1)
            x = jnp.concatenate(
                [stacked(ref, begin + a, n, 2) for a in range(3) for ref in (secondc, seconde)], 1
            )
            z = jnp.concatenate(
                [stacked(ref, h + a, n) for a in range(2) for ref in (fourthl, fourth, fourthr)], 1
            )
            y = silu(dot_nt(x, w_dec2[...]) + dot_nt(z, (w_odd if odd else w_even)[...]))
            for k in range(n):
                field.keep_pairs(y[k * HALF : (k + 1) * HALF], fifthc, fifthe, at + 2 * k, 1, fifth_lo)

        for parity in range(2):
            n_rows = (total - parity + 1) // 2
            for at in range(0, n_rows, 5):
                fifth_rows(parity + 2 * at, min(5, n_rows - at))

        def out_rows(at, n):
            x = jnp.concatenate([stacked(fifthc, at, n), stacked(fifthe, at, n)], 1)
            prod[:, at * HALF : (at + n) * HALF] = dot_nt(w_out[...], x)

        for at in range(0, total, 10):
            out_rows(at, min(10, total - at))
        out_lo, total = rows["out"]
        for k in range(total):
            for p in range(2):
                picked[p, 8 * k : 8 * k + 8, :] = sum(
                    prod[16 * a + 8 * p : 16 * a + 8 * p + 8, (k + a) * HALF : (k + a + 1) * HALF]
                    for a in range(3)
                )
        net = sum(
            jnp.dot(
                picked[p, 0 : 8 * total, :], weave[p], preferred_element_type=F32, precision=lax.Precision.HIGHEST
            )
            for p in range(2)
        )
        if step == 0:
            now = state_in[...]
        else:
            skip = 8 * (out_lo - rows["scaled"][0])
            now = state[skip : skip + 8 * total, :]
        denoised = keep * now + mix * net
        now = now + move * (now - denoised)
        for k in range(total):
            value = now[8 * k : 8 * k + 8] * (field.natural * field.fine_ok(out_lo + k))
            if step == 0:
                state[8 * k : 8 * k + 8, :] = value
            else:
                out_ref[:, k, :] = value[0:4]


def turn(x, by):
    n = lax.axis_size("tile")
    return lax.ppermute(x, "tile", [(i, (i + by) % n) for i in range(n)])


VMEM = pl.BlockSpec(memory_space=pltpu.VMEM)
SMEM = pl.BlockSpec(memory_space=pltpu.SMEM)


def limit(mib):
    return pltpu.CompilerParams(vmem_limit_bytes=mib << 20)


def prep_call(w_in, w_enc, w_down, w_mid, w_dec, w_out):
    shapes = ((96, 256), (256, 1536), (256, 1152), (256, 2304), (256, 1536), (256, 1536), (256, 1536), (48, 512))
    return pl.pallas_call(
        prep_kernel,
        out_shape=[jax.ShapeDtypeStruct(s, BF) for s in shapes],
        in_specs=[VMEM] * 6,
        out_specs=[VMEM] * 8,
        compiler_params=limit(12),
        cost_estimate=cost(20),
        name="prep",
    )(w_in.transpose(0, 2, 1), w_enc, w_down, w_mid, w_dec, w_out)


def rowbuf(n):
    return pltpu.VMEM((n, HALF, 256), BF)


def cost(passes):
    return pl.CostEstimate(flops=passes * 128 * 65536 * 2, bytes_accessed=1 << 20, transcendentals=0)


def first_call(width, sigmas, noise_parts, w_sigma, w_in, w_enc):
    return pl.pallas_call(
        first_kernel,
        out_shape=[
            jax.ShapeDtypeStruct((17 * 8, 256), F32),
            jax.ShapeDtypeStruct((27, HALF, 256), BF),
            jax.ShapeDtypeStruct((27, HALF, 256), BF),
        ],
        in_specs=[SMEM, SMEM] + [VMEM] * 8,
        out_specs=[VMEM] * 3,
        scratch_shapes=[
            pltpu.VMEM((31 * 8, 256), F32), pltpu.VMEM((31 * 8, 512), F32), rowbuf(29), rowbuf(29),
        ],
        compiler_params=limit(16),
        cost_estimate=cost(200),
        name="first",
    )(width, sigmas, *noise_parts, w_sigma, w_in, w_enc)


def second_call(width, sigmas, fields, conds, w_sigma, weights):
    return pl.pallas_call(
        second_kernel,
        out_shape=jax.ShapeDtypeStruct((4, 4, 256), F32),
        in_specs=[SMEM, SMEM] + [VMEM] * 15,
        out_specs=VMEM,
        scratch_shapes=[
            pltpu.VMEM((17 * 8, 256), F32),
            pltpu.VMEM((17 * 8, 512), F32),
            rowbuf(15), rowbuf(15), rowbuf(13), rowbuf(13),
            rowbuf(13), rowbuf(13), rowbuf(13), rowbuf(11), rowbuf(11), rowbuf(11),
            rowbuf(19), rowbuf(19),
            pltpu.VMEM((48, 19 * HALF), F32),
            pltpu.VMEM((2, 17 * 8, HALF), F32),
        ],
        compiler_params=limit(28),
        cost_estimate=cost(600),
        name="second",
    )(width, sigmas, *fields, *conds, w_sigma, *weights)


def encode_call(block_anchor, coarse_blocks, w_context):
    chans = w_context.shape[1]
    cells = coarse_blocks.shape[1] // chans
    count = coarse_blocks.shape[0]
    tiles = coarse_blocks.shape[1] // 128
    return pl.pallas_call(
        encode_kernel,
        out_shape=jax.ShapeDtypeStruct((8, 6 * cells, 256), BF),
        in_specs=[SMEM, VMEM, VMEM],
        out_specs=VMEM,
        scratch_shapes=[
            pltpu.VMEM((count + 8, cells, 256), F32),
            pltpu.VMEM((count * tiles + 64, 128), F32),
            pltpu.VMEM((2, 80, 128), F32),
        ],
        compiler_params=limit(16),
        cost_estimate=cost(100),
        name="encode",
    )(block_anchor, coarse_blocks, w_context.T)


def per_device(
    coarse_blocks, block_anchor, nest_width, sigmas, noise,
    w_context, w_in, w_sigma, w_enc, w_down, w_mid, w_dec, w_out,
):
    partial = encode_call(block_anchor, coarse_blocks, w_context)
    arrived = lax.all_to_all(partial, "band", 0, 0, tiled=True)

    held = lax.optimization_barrier((partial, noise, w_in, w_enc, w_down, w_mid, w_dec, w_out))
    noise = held[1]
    own = noise[0].transpose(1, 0, 2).reshape(16, 256)
    up3 = turn(own, 3)
    down3 = turn(own, -3)
    three = jnp.concatenate([up3, own, down3], 0)
    near_up = turn(three, 1)
    near_down = turn(three, -1)
    packed_in, enc, *rest = prep_call(*held[2:])
    w_sigma = w_sigma.reshape(1, -1)
    fields = first_call(nest_width, sigmas, (own, up3, down3, near_up, near_down), w_sigma, packed_in, enc)
    arrived, fields, rest = lax.optimization_barrier((arrived, fields, rest))

    near = (jnp.sum(arrived.astype(F32), axis=0) * (1.0 / math.sqrt(K // 2))).astype(BF)
    far_up = turn(near[:256], 2)
    far_down = turn(near[128:], -2)
    out = second_call(
        nest_width, sigmas, fields, (far_up, near, far_down), w_sigma, (packed_in, enc, *rest)
    )
    return out[None]


def solution(mesh):
    return jax.shard_map(
        per_device,
        mesh=mesh,
        in_specs=(
            P("band", None), P(), P("band"), P(), P("band", None, "tile", None),
            P(), P(), P(), P(), P(), P(), P(), P(),
        ),
        out_specs=P("band", None, "tile", None),
        check_vma=False,
    )
```

```python
import functools
import math

import jax
import jax.numpy as jnp
from jax import lax
from jax.experimental import pallas as pl
from jax.experimental.pallas import tpu as pltpu
from jax.sharding import PartitionSpec as P

K = 96
SIGMA_DATA = 0.5
BF = jnp.bfloat16
F32 = jnp.float32
HALF = 128
ROWS = 256
NT = (((1,), (1,)), ((), ()))
TN = (((0,), (0,)), ((), ()))

SCALED = (-7, 17)
FIRST = (-6, 15)
SECOND = (-5, 13)
THIRD = (-2, 6)
FOURTH = (-1, 4)
FIFTH = (-1, 6)


def silu(v):
    h = 0.5 * v
    return h + h * jnp.tanh(h)


def dot_nt(a, b):
    return lax.dot_general(a, b, NT, preferred_element_type=F32)


def encode_kernel(anchor_ref, blocks_ref, w_ref, out_ref, enc_ref, flat, wide):
    band = lax.axis_index("band")
    tile = lax.axis_index("tile")
    count = blocks_ref.shape[0]
    cells = enc_ref.shape[1]
    chans = w_ref.shape[0]
    tiles = blocks_ref.shape[1] // 128
    group = 8 * tiles

    flat[count * tiles :, :] = jnp.zeros((flat.shape[0] - count * tiles, 128), F32)
    for g in range(count // 16):
        for t in range(tiles):
            v = blocks_ref[16 * g : 16 * g + 16, 128 * t : 128 * t + 128].astype(F32)
            flat[2 * g * group + 8 * t : 2 * g * group + 8 * t + 8, :] = v[:8]
            flat[(2 * g + 1) * group + 8 * t : (2 * g + 1) * group + 8 * t + 8, :] = v[8:]

    w = w_ref[...].astype(F32)
    for half in range(2):
        wide[half, 0:chans, :] = w[:, 128 * half : 128 * half + 128]
        wide[half, chans:80, :] = jnp.zeros((80 - chans, 128), F32)
    weight = jnp.concatenate(
        [
            jnp.concatenate([wide[half, pl.ds(odd, 40, stride=2), :] for half in range(2)], 1)
            for odd in range(2)
        ],
        0,
    ).astype(BF)
    first = lax.broadcasted_iota(jnp.int32, (40, 128), 1) < 64

    def encode(g, carry):
        begin = pl.multiple_of(g * group, 8)
        cols = []
        for k in range(4):
            one = flat[pl.ds(begin + 2 * k, 40, stride=8), :]
            two = flat[pl.ds(begin + 2 * k + 1, 40, stride=8), :]
            even = jnp.where(first, one, pltpu.roll(two, 64, 1))
            odd = jnp.where(first, pltpu.roll(one, 64, 1), two)
            cols.append(jnp.concatenate([even, odd], 0))
        x = jnp.concatenate(cols, 1).astype(BF)
        v = lax.dot_general(x, weight, TN, preferred_element_type=F32)
        v = silu(v).astype(BF).astype(F32)
        enc_ref[pl.ds(g * 8, 8)] = v.reshape(8, cells, 256)
        return carry

    lax.fori_loop(0, count // 8, encode, 0)

    enc_ref[pl.ds(count, 8)] = enc_ref[pl.ds(0, 8)]

    def window(k, carry):
        nest = k // 2
        part = k % 2
        anchor = anchor_ref[nest, tile]
        begin = anchor + (band - anchor + 512) % 8 + part * 48
        row = (begin % 512) // 8
        total = enc_ref[row]
        for m in range(1, 6):
            total = total + enc_ref[row + m]
        out_ref[nest, pl.ds(pl.multiple_of(part * cells, cells), cells), :] = total.astype(BF)
        return carry

    lax.fori_loop(0, 16, window, 0, unroll=4)


def pair_weight(w, a):
    zero = jnp.zeros_like(w(a, 0))
    own = jnp.concatenate(
        [jnp.concatenate([w(a, 1), w(a, 2)], 1), jnp.concatenate([w(a, 0), w(a, 1)], 1)], 0
    )
    rim = jnp.concatenate(
        [jnp.concatenate([w(a, 0), zero], 1), jnp.concatenate([zero, w(a, 2)], 1)], 0
    )
    return own, rim


def form_small(w_in, w_out, in_o, out_o):
    def tall(ref, a, b):
        if not 0 <= b <= 2:
            return jnp.zeros((8, 128), F32)
        return jnp.concatenate([ref[3 * a + b].astype(F32), jnp.zeros((4, 128), F32)], 0)

    in_o[...] = jnp.concatenate(
        [
            jnp.concatenate([tall(w_in, a, q - p) for p in range(2)], 1)
            for a in range(3)
            for q in range(4)
        ],
        0,
    ).astype(BF)
    out_o[...] = jnp.concatenate(
        [
            jnp.concatenate([tall(w_out, a, q - p) for q in (1, 2, 0, 3)], 1)
            for a in range(3)
            for p in range(2)
        ],
        0,
    ).astype(BF)


def form_pairs(w, chans, out):
    for a in range(3):
        own, rim = pair_weight(lambda i, b: w[3 * i + b][:, 0:chans], a)
        out[:, 512 * a : 512 * a + 256] = own
        out[:, 512 * a + 256 : 512 * a + 512] = rim


def form_down(w, out):
    for a in range(3):
        out[:, 256 * a : 256 * a + 128] = w[3 * a + 1]
        out[:, 256 * a + 128 : 256 * a + 256] = w[3 * a + 2]
        out[:, 768 + 128 * a : 896 + 128 * a] = w[3 * a]


def form_mid(w, out):
    for a in range(3):
        for b in range(3):
            out[:, 768 * a + 256 * b : 768 * a + 256 * b + 256] = w[3 * a + b]


def form_up(w, even, odd):
    def up(a, b):
        return w[3 * a + b][:, 128:384].astype(F32)

    for out, sets in ((even, ((0,), (1, 2))), (odd, ((0, 1), (2,)))):
        for k, taps in enumerate(sets):
            col = [sum(up(a, b) for a in taps) for b in range(3)]
            zero = jnp.zeros_like(col[0])
            out[:, 768 * k : 768 * k + 256] = jnp.concatenate([col[0], zero], 0).astype(BF)
            out[:, 768 * k + 256 : 768 * k + 512] = jnp.concatenate(
                [col[1] + col[2], col[0] + col[1]], 0
            ).astype(BF)
            out[:, 768 * k + 512 : 768 * k + 768] = jnp.concatenate([zero, col[2]], 0).astype(BF)


class Field:
    def __init__(self, width):
        self.tile = lax.axis_index("tile")
        lane = lax.broadcasted_iota(jnp.int32, (HALF, 256), 1)
        pair = lax.broadcasted_iota(jnp.int32, (HALF, 256), 0)
        self.colmask = (2 * pair + lane // 128 < width).astype(F32)
        self.halfmask = (2 * pair < width).astype(F32)
        self.natural = (lax.broadcasted_iota(jnp.int32, (8, 256), 1) < width).astype(F32)

    def fine_ok(self, rho):
        row = self.tile * 4 + rho
        return jnp.logical_and(row >= 0, row < ROWS).astype(F32)

    def half_ok(self, h):
        row = self.tile * 2 + h
        return jnp.logical_and(row >= 0, row < ROWS // 2).astype(F32)

    def keep_pairs(self, y, center, rim, at, n, lo):
        y = jnp.concatenate(
            [y[k * HALF : (k + 1) * HALF] * (self.colmask * self.fine_ok(lo + at + k)) for k in range(n)], 0
        )
        side = jnp.concatenate([slide(y[:, 128:], 1), slide(y[:, :128], -1)], 1).astype(BF)
        y = y.astype(BF)
        for k in range(n):
            center[at + k] = y[k * HALF : (k + 1) * HALF]
            rim[at + k] = side[k * HALF : (k + 1) * HALF]

    def keep_half(self, y, center, left, right, at, n, lo):
        y = jnp.concatenate(
            [y[k * HALF : (k + 1) * HALF] * (self.halfmask * self.half_ok(lo + at + k)) for k in range(n)], 0
        )
        sides = (slide(y, 1).astype(BF), slide(y, -1).astype(BF))
        y = y.astype(BF)
        for k in range(n):
            cut = slice(k * HALF, (k + 1) * HALF)
            center[at + k] = y[cut]
            left[at + k] = sides[0][cut]
            right[at + k] = sides[1][cut]


def levels(sigma_ref, step):
    now = jnp.full((1, 256), sigma_ref[step], F32)
    after = jnp.full((1, 256), sigma_ref[step + 1], F32)
    var = now * now + SIGMA_DATA * SIGMA_DATA
    root = jnp.sqrt(var)
    return now, 1.0 / root, SIGMA_DATA * SIGMA_DATA / var, now * SIGMA_DATA / root, (after - now) / now


def embedding(w_sigma, now):
    return jnp.concatenate([w_sigma[...], w_sigma[...]], 1) * jnp.log(now)


def slide(x, by):
    rows = x.shape[0]
    edge = 0 if by == 1 else HALF - 1
    where = lax.broadcasted_iota(jnp.int32, x.shape, 0) % HALF
    return jnp.where(where == edge, 0.0, pltpu.roll(x, by % rows, 0))


def stacked(ref, at, n, step=1):
    return jnp.concatenate([ref[at + step * k] for k in range(n)], 0)


def chunks(total, size, body):
    full = total // size
    if full == 1:
        body(0, size)
    elif full:
        lax.fori_loop(0, full, lambda i, c: (body(i * size, size), c)[1], 0)
    if total % size:
        body(full * size, total % size)


def step_kernel(
    step, offsets,
    width_ref, sigma_ref, own, up2, up1, down1, down2, cond_up, cond_own, cond_down,
    w_sigma, w_in, w_out, w_enc_h, w_down_h, w_mid_h, w_dec_h,
    state_ref, scaled_ref,
    scaled, spread, firstc, firste, secondc, seconde, third, thirdl, thirdr, fourth, fourthl, fourthr,
    fifthc, fifthe, prod, picked,
    raw_enc, raw_down, raw_mid, raw_dec, f_in, f_out, f_enc, f_down, f_mid, f_dec, f_even, f_odd, sems,
):
    loads = [
        pltpu.make_async_copy(src, dst, sems.at[i])
        for i, (src, dst) in enumerate(
            ((w_enc_h, raw_enc), (w_down_h, raw_down), (w_mid_h, raw_mid), (w_dec_h, raw_dec))
        )
    ]
    for load in loads:
        load.start()
    field = Field(width_ref[0])
    sigma, scale, keep, mix, move = levels(sigma_ref, step)

    empty = jnp.zeros((4, 256), F32)
    scaled_lo = SCALED[0]
    for tile_off, ref, begin in ((-2, up2, offsets[0]), (-1, up1, offsets[1]), (1, down1, offsets[2]), (2, down2, offsets[3])):
        value = ref[begin : begin + 16, :].astype(F32)
        for r in range(4):
            rho = 4 * tile_off + r
            if scaled_lo <= rho < scaled_lo + SCALED[1]:
                row = jnp.concatenate([value[4 * r : 4 * r + 4], empty], 0)
                scaled[8 * (rho - scaled_lo) : 8 * (rho - scaled_lo) + 8, :] = row * field.fine_ok(rho)
    if step == 0:
        states = [sigma * own[4 * r : 4 * r + 4, :] * field.natural[0:4] for r in range(4)]
    else:
        states = [own[4 * r : 4 * r + 4, :] for r in range(4)]
    for r in range(4):
        row = jnp.concatenate([(states[r] * scale).astype(BF).astype(F32), empty], 0)
        scaled[8 * (r - scaled_lo) : 8 * (r - scaled_lo) + 8, :] = row

    form_small(w_in, w_out, f_in, f_out)

    col = lax.broadcasted_iota(jnp.int32, (256, 512), 0)
    place = lax.broadcasted_iota(jnp.int32, (256, 512), 1)
    pick = (col == 2 * (place % 128) + place // 128 - 1).astype(F32).astype(BF)
    spread[...] = jnp.dot(scaled[...].astype(BF), pick, preferred_element_type=F32)
    bias = embedding(w_sigma, sigma)

    def first_rows(at, n):
        cols = [
            jnp.concatenate(
                [
                    spread[pl.ds(pl.multiple_of((at + k + a) * 8, 8), 8), 128 * q : 128 * q + 128]
                    for a in range(3)
                    for q in range(4)
                ],
                0,
            )
            for k in range(n)
        ]
        x = jnp.concatenate(cols, 1).astype(BF)
        y = lax.dot_general(x, f_in[...], TN, preferred_element_type=F32)
        field.keep_pairs(silu(y + bias), firstc, firste, at, n, FIRST[0])

    chunks(FIRST[1], 5, first_rows)

    loads[0].wait()
    form_pairs(raw_enc, 128, f_enc)
    x = jnp.concatenate([stacked(ref, a, SECOND[1]) for a in range(3) for ref in (firstc, firste)], 1)
    field.keep_pairs(silu(dot_nt(x, f_enc[...])), secondc, seconde, 0, SECOND[1], SECOND[0])

    loads[1].wait()
    form_down(raw_down, f_down)
    repeat = (
        lax.broadcasted_iota(jnp.int32, (HALF, 64), 0) // 2 == lax.broadcasted_iota(jnp.int32, (HALF, 64), 1)
    ).astype(F32).astype(BF)
    n = THIRD[1]
    begin = 2 * THIRD[0] - 1 - SECOND[0]
    x = jnp.concatenate(
        [stacked(secondc, begin + a, n, 2) for a in range(3)]
        + [jnp.concatenate([seconde[begin + a + 2 * k][:, :128] for k in range(n)], 0) for a in range(3)],
        1,
    )
    add = [
        jnp.dot(repeat, ref[64 * r : 64 * r + 64, :], preferred_element_type=F32)
        for ref in (cond_up, cond_own, cond_down)
        for r in range(2)
    ]
    y = dot_nt(x, f_down[...]) + jnp.concatenate(add, 0)
    field.keep_half(silu(y), third, thirdl, thirdr, 0, n, THIRD[0])

    loads[2].wait()
    form_mid(raw_mid, f_mid)
    n = FOURTH[1]
    x = jnp.concatenate([stacked(ref, a, n) for a in range(3) for ref in (thirdl, third, thirdr)], 1)
    field.keep_half(silu(dot_nt(x, f_mid[...])), fourth, fourthl, fourthr, 0, n, FOURTH[0])

    loads[3].wait()
    form_pairs(raw_dec, 128, f_dec)
    form_up(raw_dec, f_even, f_odd)
    for at in range(2):
        rho = FIFTH[0] + at
        odd = rho % 2
        n = FIFTH[1] // 2
        begin = rho - 1 - SECOND[0]
        h = (rho - odd) // 2 - FOURTH[0] - (0 if odd else 1)
        x = jnp.concatenate(
            [stacked(ref, begin + a, n, 2) for a in range(3) for ref in (secondc, seconde)], 1
        )
        z = jnp.concatenate(
            [stacked(ref, h + a, n) for a in range(2) for ref in (fourthl, fourth, fourthr)], 1
        )
        y = silu(dot_nt(x, f_dec[...]) + dot_nt(z, (f_odd if odd else f_even)[...]))
        for k in range(n):
            field.keep_pairs(y[k * HALF : (k + 1) * HALF], fifthc, fifthe, at + 2 * k, 1, FIFTH[0])

    n = FIFTH[1]
    x = jnp.concatenate([stacked(fifthc, 0, n), stacked(fifthe, 0, n)], 1)
    prod[...] = dot_nt(f_out[...], x)
    for k in range(4):
        for p in range(2):
            picked[p, 8 * k : 8 * k + 8, :] = sum(
                prod[16 * a + 8 * p : 16 * a + 8 * p + 8, (k + a) * HALF : (k + a + 1) * HALF]
                for a in range(3)
            )
    weave_j = lax.broadcasted_iota(jnp.int32, (HALF, 256), 0)
    weave_c = lax.broadcasted_iota(jnp.int32, (HALF, 256), 1)
    net = sum(
        jnp.dot(
            picked[p],
            (weave_c == 2 * weave_j + p).astype(F32),
            preferred_element_type=F32,
            precision=lax.Precision.HIGHEST,
        )
        for p in range(2)
    )
    for r in range(4):
        denoised = keep * states[r] + mix * net[8 * r : 8 * r + 4]
        now = (states[r] + move * (states[r] - denoised)) * field.natural[0:4]
        if step == 0:
            state_ref[4 * r : 4 * r + 4, :] = now
            scaled_ref[4 * r : 4 * r + 4, :] = (now * levels(sigma_ref, 1)[1]).astype(BF)
        else:
            state_ref[:, r, :] = now


def turn(x, by):
    n = lax.axis_size("tile")
    return lax.ppermute(x, "tile", [(i, (i + by) % n) for i in range(n)])


VMEM = pl.BlockSpec(memory_space=pltpu.VMEM)
SMEM = pl.BlockSpec(memory_space=pltpu.SMEM)


def limit(mib):
    return pltpu.CompilerParams(vmem_limit_bytes=mib << 20)


def rowbuf(n):
    return pltpu.VMEM((n, HALF, 256), BF)


def cost(passes):
    return pl.CostEstimate(flops=passes * 128 * 65536 * 2, bytes_accessed=1 << 20, transcendentals=0)


def step_call(step, offsets, width, sigmas, own, pieces, conds, w_sigma, weights):
    raw = [pltpu.VMEM(w.shape, BF) for w in weights[2:]]
    if step == 0:
        outs = [jax.ShapeDtypeStruct((16, 256), F32), jax.ShapeDtypeStruct((16, 256), BF)]
        kernel = functools.partial(step_kernel, step, offsets)
    else:
        outs = [jax.ShapeDtypeStruct((4, 4, 256), F32)]

        def kernel(*refs):
            step_kernel(step, offsets, *refs[:18], None, *refs[18:])

    return pl.pallas_call(
        kernel,
        out_shape=outs,
        in_specs=[SMEM, SMEM] + [VMEM] * 11 + [pl.BlockSpec(memory_space=pl.ANY)] * 4,
        out_specs=[VMEM] * len(outs),
        scratch_shapes=[
            pltpu.VMEM((SCALED[1] * 8, 256), F32), pltpu.VMEM((SCALED[1] * 8, 512), F32),
            rowbuf(FIRST[1]), rowbuf(FIRST[1]), rowbuf(SECOND[1]), rowbuf(SECOND[1]),
            *[rowbuf(THIRD[1])] * 3, *[rowbuf(FOURTH[1])] * 3, *[rowbuf(FIFTH[1])] * 2,
            pltpu.VMEM((48, FIFTH[1] * HALF), F32), pltpu.VMEM((2, 32, HALF), F32),
            *raw,
            *[
                pltpu.VMEM(shape, BF)
                for shape in (
                    (96, 256), (48, 512), (256, 1536), (256, 1152), (256, 2304),
                    (256, 1536), (256, 1536), (256, 1536),
                )
            ],
            pltpu.SemaphoreType.DMA((4,)),
        ],
        compiler_params=limit(56),
        cost_estimate=cost(240),
        name="step" + str(step),
    )(width, sigmas, own, *pieces, *conds, w_sigma, *weights)


def encode_call(block_anchor, coarse_blocks, w_context):
    chans = w_context.shape[1]
    cells = coarse_blocks.shape[1] // chans
    count = coarse_blocks.shape[0]
    tiles = coarse_blocks.shape[1] // 128
    return pl.pallas_call(
        encode_kernel,
        out_shape=jax.ShapeDtypeStruct((8, 2 * cells, 256), BF),
        in_specs=[SMEM, VMEM, VMEM],
        out_specs=VMEM,
        scratch_shapes=[
            pltpu.VMEM((count + 8, cells, 256), F32),
            pltpu.VMEM((count * tiles + 64, 128), F32),
            pltpu.VMEM((2, 80, 128), F32),
        ],
        compiler_params=limit(56),
        cost_estimate=cost(100),
        name="encode",
    )(block_anchor, coarse_blocks, w_context.T)


def per_device(
    coarse_blocks, block_anchor, nest_width, sigmas, noise,
    w_context, w_in, w_sigma, w_enc, w_down, w_mid, w_dec, w_out,
):
    partial = encode_call(block_anchor, coarse_blocks, w_context)
    arrived = lax.all_to_all(partial, "band", 0, 0, tiled=True)

    held = lax.optimization_barrier((partial, noise))
    own = held[1][0].transpose(1, 0, 2).reshape(16, 256)
    mask = (jnp.arange(256, dtype=jnp.int32) < nest_width[0]).astype(F32)
    scale = 1.0 / jnp.sqrt(sigmas[0] * sigmas[0] + SIGMA_DATA * SIGMA_DATA)
    scaled = (sigmas[0] * own * mask[None, :] * scale).astype(BF)
    up = turn(scaled, 1)
    down = turn(scaled, -1)
    arrived, own, scaled, up, down = lax.optimization_barrier((arrived, own, scaled, up, down))

    cond = (jnp.sum(arrived.astype(F32), axis=0) * (1.0 / math.sqrt(K // 2))).astype(BF)
    near_up = turn(jnp.concatenate([cond, up, scaled], 0), 1)
    near_down = turn(jnp.concatenate([cond, scaled, down], 0), -1)
    conds = (near_up, cond, near_down)
    w_sigma = w_sigma.reshape(1, -1)
    weights = (w_in.transpose(0, 2, 1), w_out, w_enc, w_down, w_mid, w_dec)
    state, scaled = step_call(
        0, (128, 144, 128, 144), nest_width, sigmas, own, (near_up, near_up, near_down, near_down),
        conds, w_sigma, weights,
    )
    pieces = tuple(turn(scaled, by) for by in (2, 1, -1, -2))
    (out,) = step_call(1, (0, 0, 0, 0), nest_width, sigmas, state, pieces, conds, w_sigma, weights)
    return out[None]


def solution(mesh):
    return jax.shard_map(
        per_device,
        mesh=mesh,
        in_specs=(
            P("band", None), P(), P("band"), P(), P("band", None, "tile", None),
            P(), P(), P(), P(), P(), P(), P(), P(),
        ),
        out_specs=P("band", None, "tile", None),
        check_vma=False,
    )
```

```python
import functools
import math

import jax
import jax.numpy as jnp
from jax import lax
from jax.experimental import pallas as pl
from jax.experimental.pallas import tpu as pltpu
from jax.sharding import PartitionSpec as P

K = 96
SIGMA_DATA = 0.5
BF = jnp.bfloat16
F32 = jnp.float32
HALF = 128
ROWS = 256
NT = (((1,), (1,)), ((), ()))
TN = (((0,), (0,)), ((), ()))

BLOCKS = (5, 5, 3, 2)
SCALED = (-7, 17)
FIRST = (-6, 15)
SECOND = (-5, 13)
THIRD = (-2, 6)
FOURTH = (-1, 4)
FIFTH = (-1, 6)


def silu_twice(h):
    return h + h * jnp.tanh(h)


def dot_nt(a, b):
    return lax.dot_general(a, b, NT, preferred_element_type=F32)


def levels(sigma_ref, step):
    now = jnp.full((1, 256), sigma_ref[step], F32)
    after = jnp.full((1, 256), sigma_ref[step + 1], F32)
    var = now * now + SIGMA_DATA * SIGMA_DATA
    root = jnp.sqrt(var)
    return now, 1.0 / root, SIGMA_DATA * SIGMA_DATA / var, now * SIGMA_DATA / root, (after - now) / now


def encode_kernel(
    anchor_ref, width_ref, sigma_ref, blocks_ref, w_ref, noise_ref, out_ref, state_ref, scaled_ref, enc_ref, flat, wide
):
    band = lax.axis_index("band")
    tile = lax.axis_index("tile")
    count = blocks_ref.shape[0]
    cells = enc_ref.shape[1]
    chans = w_ref.shape[0]
    tiles = blocks_ref.shape[1] // 128
    group = 8 * tiles

    flat[count * tiles :, :] = jnp.zeros((flat.shape[0] - count * tiles, 128), F32)
    for g in range(count // 16):
        for t in range(tiles):
            v = blocks_ref[16 * g : 16 * g + 16, 128 * t : 128 * t + 128].astype(F32)
            flat[2 * g * group + 8 * t : 2 * g * group + 8 * t + 8, :] = v[:8]
            flat[(2 * g + 1) * group + 8 * t : (2 * g + 1) * group + 8 * t + 8, :] = v[8:]

    sigma, scale = levels(sigma_ref, 0)[:2]
    natural = (lax.broadcasted_iota(jnp.int32, (4, 256), 1) < width_ref[0]).astype(F32)
    for r in range(4):
        row = sigma * noise_ref[:, r, :] * natural
        state_ref[4 * r : 4 * r + 4, :] = row
        scaled_ref[4 * r : 4 * r + 4, :] = (row * scale).astype(BF)

    w = 0.5 * w_ref[...].astype(F32)
    for half in range(2):
        wide[half, 0:chans, :] = w[:, 128 * half : 128 * half + 128]
        wide[half, chans:80, :] = jnp.zeros((80 - chans, 128), F32)
    weight = jnp.concatenate(
        [
            jnp.concatenate([wide[half, pl.ds(odd, 40, stride=2), :] for half in range(2)], 1)
            for odd in range(2)
        ],
        0,
    ).astype(BF)
    first = lax.broadcasted_iota(jnp.int32, (40, 128), 1) < 64

    def encode(g, carry):
        begin = pl.multiple_of(g * group, 8)
        cols = []
        for k in range(4):
            one = flat[pl.ds(begin + 2 * k, 40, stride=8), :]
            two = flat[pl.ds(begin + 2 * k + 1, 40, stride=8), :]
            even = jnp.where(first, one, pltpu.roll(two, 64, 1))
            odd = jnp.where(first, pltpu.roll(one, 64, 1), two)
            cols.append(jnp.concatenate([even, odd], 0))
        x = jnp.concatenate(cols, 1).astype(BF)
        v = lax.dot_general(x, weight, TN, preferred_element_type=F32)
        v = silu_twice(v).astype(BF).astype(F32)
        enc_ref[pl.ds(g * 8, 8)] = v.reshape(8, cells, 256)
        return carry

    lax.fori_loop(0, count // 8, encode, 0, unroll=True)

    enc_ref[pl.ds(count, 8)] = enc_ref[pl.ds(0, 8)]

    def window(k, carry):
        nest = k // 2
        part = k % 2
        anchor = anchor_ref[nest, tile]
        begin = anchor + (band - anchor + 512) % 8 + part * 48
        row = (begin % 512) // 8
        total = enc_ref[row]
        for m in range(1, 6):
            total = total + enc_ref[row + m]
        out_ref[nest, pl.ds(pl.multiple_of(part * cells, cells), cells), :] = total.astype(BF)
        return carry

    lax.fori_loop(0, 16, window, 0, unroll=4)


def pair_weight(w, a):
    zero = jnp.zeros_like(w(a, 0))
    own = jnp.concatenate(
        [jnp.concatenate([w(a, 1), w(a, 2)], 1), jnp.concatenate([w(a, 0), w(a, 1)], 1)], 0
    )
    rim = jnp.concatenate(
        [jnp.concatenate([w(a, 0), zero], 1), jnp.concatenate([zero, w(a, 2)], 1)], 0
    )
    return own, rim


def form_small(w_in, w_out, in_o, out_o):
    half = jnp.asarray(0.5, BF)

    def tall(ref, a, b):
        if not 0 <= b <= 2:
            return jnp.zeros((8, 128), F32)
        return jnp.concatenate([ref[3 * a + b].astype(F32), jnp.zeros((4, 128), F32)], 0)

    in_o[...] = jnp.concatenate(
        [
            jnp.concatenate([tall(w_in, a, q - p) for p in range(2)], 1)
            for a in range(3)
            for q in range(4)
        ],
        0,
    ).astype(BF)
    in_o[...] = in_o[...] * half
    out_o[...] = jnp.concatenate(
        [
            jnp.concatenate([tall(w_out, a, q - p) for q in (1, 2, 0, 3)], 1)
            for a in range(3)
            for p in range(2)
        ],
        0,
    ).astype(BF)


def form_pairs(w, chans, out):
    half = jnp.asarray(0.5, BF)
    for a in range(3):
        own, rim = pair_weight(lambda i, b: w[3 * i + b][:, 0:chans] * half, a)
        out[:, 512 * a : 512 * a + 256] = own
        out[:, 512 * a + 256 : 512 * a + 512] = rim


def form_down(w, out):
    half = jnp.asarray(0.5, BF)
    for a in range(3):
        out[:, 256 * a : 256 * a + 128] = w[3 * a + 1] * half
        out[:, 256 * a + 128 : 256 * a + 256] = w[3 * a + 2] * half
        out[:, 768 + 128 * a : 896 + 128 * a] = w[3 * a] * half


def form_mid(w, out):
    half = jnp.asarray(0.5, BF)
    for a in range(3):
        for b in range(3):
            out[:, 768 * a + 256 * b : 768 * a + 256 * b + 256] = w[3 * a + b] * half


def form_up(w, even, odd):
    def up(a, b):
        return 0.5 * w[3 * a + b][:, 128:384].astype(F32)

    for out, sets in ((even, ((0,), (1, 2))), (odd, ((0, 1), (2,)))):
        for k, taps in enumerate(sets):
            col = [sum(up(a, b) for a in taps) for b in range(3)]
            zero = jnp.zeros_like(col[0])
            out[:, 768 * k : 768 * k + 256] = jnp.concatenate([col[0], zero], 0).astype(BF)
            out[:, 768 * k + 256 : 768 * k + 512] = jnp.concatenate(
                [col[1] + col[2], col[0] + col[1]], 0
            ).astype(BF)
            out[:, 768 * k + 512 : 768 * k + 768] = jnp.concatenate([zero, col[2]], 0).astype(BF)


def parts(total, most):
    count = -(-total // most)
    cuts = [total * i // count for i in range(count + 1)]
    return [(a, b - a) for a, b in zip(cuts, cuts[1:])]


class Field:
    def __init__(self, width, masks):
        self.tile = lax.axis_index("tile")
        self.masks = masks
        lane = lax.broadcasted_iota(jnp.int32, (HALF, 256), 1)
        pair = lax.broadcasted_iota(jnp.int32, (HALF, 256), 0)
        masks[0] = jnp.zeros((HALF, 256), F32)
        masks[1] = (2 * pair + lane // 128 < width).astype(F32)
        masks[2] = (2 * pair < width).astype(F32)
        self.natural = (lax.broadcasted_iota(jnp.int32, (4, 256), 1) < width).astype(F32)

    def fine_ok(self, rho):
        row = self.tile * 4 + rho
        return jnp.logical_and(row >= 0, row < ROWS).astype(jnp.int32)

    def half_ok(self, h):
        row = self.tile * 2 + h
        return jnp.logical_and(row >= 0, row < ROWS // 2).astype(jnp.int32)

    def keep_pairs(self, y, center, rim, at, rho):
        y = y * self.masks[self.fine_ok(rho)]
        center[at] = y.astype(BF)
        rim[at] = jnp.concatenate([slide(y[:, 128:], 1), slide(y[:, :128], -1)], 1).astype(BF)

    def keep_half(self, y, center, left, right, at, h):
        y = y * self.masks[2 * self.half_ok(h)]
        center[at] = y.astype(BF)
        left[at] = slide(y, 1).astype(BF)
        right[at] = slide(y, -1).astype(BF)


def embedding(w_sigma, now):
    return jnp.concatenate([w_sigma[...], w_sigma[...]], 1) * jnp.log(now)


def slide(x, by):
    x = pltpu.roll(x, by % HALF, 0)
    where = lax.broadcasted_iota(jnp.int32, (8, x.shape[1]), 0)
    if by == 1:
        return jnp.concatenate([jnp.where(where == 0, 0.0, x[:8]), x[8:]], 0)
    return jnp.concatenate([x[: HALF - 8], jnp.where(where == 7, 0.0, x[HALF - 8 :])], 0)


def stacked(ref, at, n, step=1):
    return jnp.concatenate([ref[at + step * k] for k in range(n)], 0)


def step_kernel(
    step, width_ref, sigma_ref, own, halo, cond_up, cond_own, cond_down, weights, state_ref, scaled_ref,
    scaled, spread, firstc, firste, secondc, seconde, third, thirdl, thirdr, fourth, fourthl, fourthr,
    fifthc, fifthe, prod, picked, masks,
    f_in, f_out, f_enc, f_down, f_mid, f_dec, f_even, f_odd,
):
    w_sigma, w_in, w_out, w_enc, w_down, w_mid, w_dec = weights
    field = Field(width_ref[0], masks)
    sigma, scale, keep, mix, move = levels(sigma_ref, step)

    empty = jnp.zeros((4, 256), F32)
    scaled_lo = SCALED[0]
    for tile_off, ref, begin in halo:
        value = ref[begin : begin + 16, :].astype(F32)
        for r in range(4):
            rho = 4 * tile_off + r
            if scaled_lo <= rho < scaled_lo + SCALED[1]:
                row = jnp.concatenate([value[4 * r : 4 * r + 4], empty], 0)
                scaled[8 * (rho - scaled_lo) : 8 * (rho - scaled_lo) + 8, :] = row * field.fine_ok(rho).astype(F32)
    states = [own[4 * r : 4 * r + 4, :] for r in range(4)]
    for r in range(4):
        row = jnp.concatenate([(states[r] * scale).astype(BF).astype(F32), empty], 0)
        scaled[8 * (r - scaled_lo) : 8 * (r - scaled_lo) + 8, :] = row

    form_small(w_in, w_out, f_in, f_out)

    col = lax.broadcasted_iota(jnp.int32, (256, 512), 0)
    place = lax.broadcasted_iota(jnp.int32, (256, 512), 1)
    pick = (col == 2 * (place % 128) + place // 128 - 1).astype(F32).astype(BF)
    spread[...] = jnp.dot(scaled[...].astype(BF), pick, preferred_element_type=F32)
    bias = 0.5 * embedding(w_sigma, sigma)
    for at, n in parts(FIRST[1], BLOCKS[0]):
        cols = [
            jnp.concatenate(
                [spread[8 * (k + a) : 8 * (k + a) + 8, 128 * q : 128 * q + 128] for a in range(3) for q in range(4)],
                0,
            )
            for k in range(at, at + n)
        ]
        x = jnp.concatenate(cols, 1).astype(BF)
        y = lax.dot_general(x, f_in[...], TN, preferred_element_type=F32)
        for k in range(n):
            part = silu_twice(y[k * HALF : (k + 1) * HALF] + bias)
            field.keep_pairs(part, firstc, firste, at + k, FIRST[0] + at + k)

    form_pairs(w_enc, 128, f_enc)
    for at, n in parts(SECOND[1], BLOCKS[1]):
        x = jnp.concatenate([stacked(ref, at + a, n) for a in range(3) for ref in (firstc, firste)], 1)
        y = dot_nt(x, f_enc[...])
        for k in range(n):
            part = silu_twice(y[k * HALF : (k + 1) * HALF])
            field.keep_pairs(part, secondc, seconde, at + k, SECOND[0] + at + k)

    form_down(w_down, f_down)
    repeat = (
        lax.broadcasted_iota(jnp.int32, (HALF, 64), 0) // 2 == lax.broadcasted_iota(jnp.int32, (HALF, 64), 1)
    ).astype(F32)
    repeat = (0.5 * repeat).astype(BF)
    add = [
        jnp.dot(repeat, ref[64 * r : 64 * r + 64, :], preferred_element_type=F32)
        for ref in (cond_up, cond_own, cond_down)
        for r in range(2)
    ]
    for at, n in parts(THIRD[1], BLOCKS[2]):
        begin = 2 * (THIRD[0] + at) - 1 - SECOND[0]
        x = jnp.concatenate(
            [stacked(secondc, begin + a, n, 2) for a in range(3)]
            + [jnp.concatenate([seconde[begin + a + 2 * k][:, :128] for k in range(n)], 0) for a in range(3)],
            1,
        )
        y = dot_nt(x, f_down[...])
        for k in range(n):
            part = silu_twice(y[k * HALF : (k + 1) * HALF] + add[at + k])
            field.keep_half(part, third, thirdl, thirdr, at + k, THIRD[0] + at + k)

    form_mid(w_mid, f_mid)
    for at, n in parts(FOURTH[1], BLOCKS[3]):
        x = jnp.concatenate(
            [stacked(ref, at + a, n) for a in range(3) for ref in (thirdl, third, thirdr)], 1
        )
        y = dot_nt(x, f_mid[...])
        for k in range(n):
            part = silu_twice(y[k * HALF : (k + 1) * HALF])
            field.keep_half(part, fourth, fourthl, fourthr, at + k, FOURTH[0] + at + k)

    form_pairs(w_dec, 128, f_dec)
    form_up(w_dec, f_even, f_odd)
    for at in range(2):
        rho = FIFTH[0] + at
        odd = rho % 2
        n = FIFTH[1] // 2
        begin = rho - 1 - SECOND[0]
        h = (rho - odd) // 2 - FOURTH[0] - (0 if odd else 1)
        x = jnp.concatenate(
            [stacked(ref, begin + a, n, 2) for a in range(3) for ref in (secondc, seconde)], 1
        )
        z = jnp.concatenate(
            [stacked(ref, h + a, n) for a in range(2) for ref in (fourthl, fourth, fourthr)], 1
        )
        y = dot_nt(x, f_dec[...]) + dot_nt(z, (f_odd if odd else f_even)[...])
        for k in range(n):
            part = silu_twice(y[k * HALF : (k + 1) * HALF])
            field.keep_pairs(part, fifthc, fifthe, at + 2 * k, FIFTH[0] + at + 2 * k)

    n = FIFTH[1]
    x = jnp.concatenate([stacked(fifthc, 0, n), stacked(fifthe, 0, n)], 1)
    prod[...] = dot_nt(f_out[...], x)
    for k in range(4):
        for p in range(2):
            picked[8 * k : 8 * k + 8, HALF * p : HALF * p + HALF] = sum(
                prod[16 * a + 8 * p : 16 * a + 8 * p + 8, (k + a) * HALF : (k + a + 1) * HALF]
                for a in range(3)
            )
    high = picked[...].astype(BF)
    low = (picked[...] - high.astype(F32)).astype(BF)
    weave_j = lax.broadcasted_iota(jnp.int32, (256, 256), 0)
    weave_c = lax.broadcasted_iota(jnp.int32, (256, 256), 1)
    weave = (weave_c == 2 * (weave_j % HALF) + weave_j // HALF).astype(F32).astype(BF)
    net = jnp.dot(high, weave, preferred_element_type=F32) + jnp.dot(low, weave, preferred_element_type=F32)
    for r in range(4):
        denoised = keep * states[r] + mix * net[8 * r : 8 * r + 4]
        now = (states[r] + move * (states[r] - denoised)) * field.natural
        if step == 0:
            state_ref[4 * r : 4 * r + 4, :] = now
            scaled_ref[4 * r : 4 * r + 4, :] = (now * levels(sigma_ref, 1)[1]).astype(BF)
        else:
            state_ref[:, r, :] = now


def turn(x, by):
    n = lax.axis_size("tile")
    return lax.ppermute(x, "tile", [(i, (i + by) % n) for i in range(n)])


VMEM = pl.BlockSpec(memory_space=pltpu.VMEM)
SMEM = pl.BlockSpec(memory_space=pltpu.SMEM)


LIMIT = 20


def limit(mib):
    return pltpu.CompilerParams(vmem_limit_bytes=mib << 20)


def rowbuf(n):
    return pltpu.VMEM((n, HALF, 256), BF)


def cost(passes):
    return pl.CostEstimate(flops=passes * 128 * 65536 * 2, bytes_accessed=1 << 20, transcendentals=0)


def step_call(step, width, sigmas, own, pieces, conds, weights):
    distinct = list(conds)
    for array, _ in pieces:
        if not any(array is d for d in distinct):
            distinct.append(array)
    place = [next(i for i, d in enumerate(distinct) if d is array) for array, _ in pieces]
    outs = [jax.ShapeDtypeStruct((16, 256), F32), jax.ShapeDtypeStruct((16, 256), BF)]
    if step == 1:
        outs = [jax.ShapeDtypeStruct((4, 4, 256), F32)]
    n_arrays, n_weights = len(distinct), len(weights)

    def kernel(width_ref, sigma_ref, own_ref, *refs):
        arrays, refs = refs[:n_arrays], refs[n_arrays:]
        weight_refs, refs = refs[:n_weights], refs[n_weights:]
        out_refs, refs = list(refs[: len(outs)]), refs[len(outs) :]
        halo = [(off, arrays[place[i]], pieces[i][1]) for i, off in enumerate((-2, -1, 1, 2))]
        step_kernel(
            step, width_ref, sigma_ref, own_ref, halo, *arrays[:3], weight_refs,
            *(out_refs + [None])[:2], *refs,
        )

    return pl.pallas_call(
        kernel,
        out_shape=outs,
        in_specs=[SMEM, SMEM] + [VMEM] * (1 + n_arrays + n_weights),
        out_specs=[VMEM] * len(outs),
        scratch_shapes=[
            pltpu.VMEM((SCALED[1] * 8, 256), F32), pltpu.VMEM((SCALED[1] * 8, 512), F32),
            rowbuf(FIRST[1]), rowbuf(FIRST[1]), rowbuf(SECOND[1]), rowbuf(SECOND[1]),
            *[rowbuf(THIRD[1])] * 3, *[rowbuf(FOURTH[1])] * 3, *[rowbuf(FIFTH[1])] * 2,
            pltpu.VMEM((48, FIFTH[1] * HALF), F32), pltpu.VMEM((32, 256), F32), pltpu.VMEM((3, HALF, 256), F32),
            *[
                pltpu.VMEM(shape, BF)
                for shape in (
                    (96, 256), (48, 512), (256, 1536), (256, 1152), (256, 2304),
                    (256, 1536), (256, 1536), (256, 1536),
                )
            ],
        ],
        compiler_params=limit(LIMIT),
        cost_estimate=cost(240),
        name="step" + str(step),
    )(width, sigmas, own, *distinct, *weights)


def encode_call(block_anchor, nest_width, sigmas, coarse_blocks, w_context, noise):
    chans = w_context.shape[1]
    cells = coarse_blocks.shape[1] // chans
    count = coarse_blocks.shape[0]
    tiles = coarse_blocks.shape[1] // 128
    return pl.pallas_call(
        encode_kernel,
        out_shape=[
            jax.ShapeDtypeStruct((8, 2 * cells, 256), BF),
            jax.ShapeDtypeStruct((16, 256), F32),
            jax.ShapeDtypeStruct((16, 256), BF),
        ],
        in_specs=[SMEM, SMEM, SMEM, VMEM, VMEM, VMEM],
        out_specs=[VMEM] * 3,
        scratch_shapes=[
            pltpu.VMEM((count + 8, cells, 256), F32),
            pltpu.VMEM((count * tiles + 64, 128), F32),
            pltpu.VMEM((2, 80, 128), F32),
        ],
        compiler_params=limit(56),
        cost_estimate=cost(100),
        name="encode",
    )(block_anchor, nest_width, sigmas, coarse_blocks, w_context.T, noise)


def per_device(
    coarse_blocks, block_anchor, nest_width, sigmas, noise,
    w_context, w_in, w_sigma, w_enc, w_down, w_mid, w_dec, w_out,
):
    partial, state, scaled = encode_call(block_anchor, nest_width, sigmas, coarse_blocks, w_context, noise[0])
    arrived = lax.all_to_all(partial, "band", 0, 0, tiled=True)

    up = turn(scaled, 1)
    down = turn(scaled, -1)
    arrived, up, down = lax.optimization_barrier((arrived, up, down))

    cond = (jnp.sum(arrived.astype(F32), axis=0) * (1.0 / math.sqrt(K // 2))).astype(BF)
    near_up = turn(jnp.concatenate([cond, up, scaled], 0), 1)
    near_down = turn(jnp.concatenate([cond, scaled, down], 0), -1)
    conds = (near_up, cond, near_down)
    weights = (w_sigma.reshape(1, -1), w_in.transpose(0, 2, 1), w_out, w_enc, w_down, w_mid, w_dec)
    pieces = ((near_up, 128), (near_up, 144), (near_down, 128), (near_down, 144))
    state, scaled = step_call(0, nest_width, sigmas, state, pieces, conds, weights)
    pieces = tuple((turn(scaled, by), 0) for by in (2, 1, -1, -2))
    (out,) = step_call(1, nest_width, sigmas, state, pieces, conds, weights)
    return out[None]


def solution(mesh):
    return jax.shard_map(
        per_device,
        mesh=mesh,
        in_specs=(
            P("band", None), P(), P("band"), P(), P("band", None, "tile", None),
            P(), P(), P(), P(), P(), P(), P(), P(),
        ),
        out_specs=P("band", None, "tile", None),
        check_vma=False,
    )
```

```python
import functools
import math

import jax
import jax.numpy as jnp
from jax import lax
from jax.experimental import pallas as pl
from jax.experimental.pallas import tpu as pltpu
from jax.sharding import PartitionSpec as P

K = 96
SIGMA_DATA = 0.5
BF = jnp.bfloat16
F32 = jnp.float32
HALF = 128
ROWS = 256
NT = (((1,), (1,)), ((), ()))
TN = (((0,), (0,)), ((), ()))

BLOCKS = (4, 4, 4, 3, 3, 4)
FIELDS = ("scaled", "first", "second", "third", "fourth", "fifth", "out")
STEP_ROWS = (
    dict(zip(FIELDS, ((-15, 31), (-14, 29), (-13, 27), (-6, 13), (-5, 11), (-8, 19), (-7, 17)))),
    dict(zip(FIELDS, ((-7, 17), (-6, 15), (-5, 13), (-2, 6), (-1, 4), (-1, 6), (0, 4)))),
)


def silu_twice(h):
    return h + h * jnp.tanh(h)


def dot_nt(a, b):
    return lax.dot_general(a, b, NT, preferred_element_type=F32)


def levels(sigma_ref, step):
    now = jnp.full((1, 256), sigma_ref[step], F32)
    after = jnp.full((1, 256), sigma_ref[step + 1], F32)
    var = now * now + SIGMA_DATA * SIGMA_DATA
    root = jnp.sqrt(var)
    return now, 1.0 / root, SIGMA_DATA * SIGMA_DATA / var, now * SIGMA_DATA / root, (after - now) / now


def encode_kernel(
    anchor_ref, width_ref, sigma_ref, blocks_ref, w_ref, noise_ref, out_ref, state_ref, parts_ref, enc_ref, flat, wide
):
    band = lax.axis_index("band")
    tile = lax.axis_index("tile")
    count = blocks_ref.shape[0]
    cells = enc_ref.shape[1]
    chans = w_ref.shape[0]
    tiles = blocks_ref.shape[1] // 128
    group = 8 * tiles

    flat[count * tiles :, :] = jnp.zeros((flat.shape[0] - count * tiles, 128), F32)
    for g in range(count // 16):
        for t in range(tiles):
            v = blocks_ref[16 * g : 16 * g + 16, 128 * t : 128 * t + 128].astype(F32)
            flat[2 * g * group + 8 * t : 2 * g * group + 8 * t + 8, :] = v[:8]
            flat[(2 * g + 1) * group + 8 * t : (2 * g + 1) * group + 8 * t + 8, :] = v[8:]

    sigma = levels(sigma_ref, 0)[0]
    natural = (lax.broadcasted_iota(jnp.int32, (4, 256), 1) < width_ref[0]).astype(F32)
    for r in range(4):
        row = sigma * noise_ref[:, r, :] * natural
        state_ref[4 * r : 4 * r + 4, :] = row
    state = state_ref[...]
    high = state.astype(BF)
    parts_ref[0:16, :] = high
    parts_ref[16:32, :] = (state - high.astype(F32)).astype(BF)

    w = 0.5 * w_ref[...].astype(F32)
    for half in range(2):
        wide[half, 0:chans, :] = w[:, 128 * half : 128 * half + 128]
        wide[half, chans:80, :] = jnp.zeros((80 - chans, 128), F32)
    weight = jnp.concatenate(
        [
            jnp.concatenate([wide[half, pl.ds(odd, 40, stride=2), :] for half in range(2)], 1)
            for odd in range(2)
        ],
        0,
    ).astype(BF)
    first = lax.broadcasted_iota(jnp.int32, (40, 128), 1) < 64

    def encode(g, carry):
        begin = pl.multiple_of(g * group, 8)
        cols = []
        for k in range(4):
            one = flat[pl.ds(begin + 2 * k, 40, stride=8), :]
            two = flat[pl.ds(begin + 2 * k + 1, 40, stride=8), :]
            even = jnp.where(first, one, pltpu.roll(two, 64, 1))
            odd = jnp.where(first, pltpu.roll(one, 64, 1), two)
            cols.append(jnp.concatenate([even, odd], 0))
        x = jnp.concatenate(cols, 1).astype(BF)
        v = lax.dot_general(x, weight, TN, preferred_element_type=F32)
        v = silu_twice(v).astype(BF).astype(F32)
        enc_ref[pl.ds(g * 8, 8)] = v.reshape(8, cells, 256)
        return carry

    lax.fori_loop(0, count // 8, encode, 0, unroll=True)

    enc_ref[pl.ds(count, 8)] = enc_ref[pl.ds(0, 8)]

    def window(k, carry):
        nest = k // 2
        part = k % 2
        anchor = anchor_ref[nest, tile]
        begin = anchor + (band - anchor + 512) % 8 + part * 48
        row = (begin % 512) // 8
        total = enc_ref[row]
        for m in range(1, 6):
            total = total + enc_ref[row + m]
        out_ref[nest, pl.ds(pl.multiple_of(part * cells, cells), cells), :] = total.astype(BF)
        return carry

    lax.fori_loop(0, 16, window, 0, unroll=4)


def pair_weight(w, a):
    zero = jnp.zeros_like(w(a, 0))
    own = jnp.concatenate(
        [jnp.concatenate([w(a, 1), w(a, 2)], 1), jnp.concatenate([w(a, 0), w(a, 1)], 1)], 0
    )
    rim = jnp.concatenate(
        [jnp.concatenate([w(a, 0), zero], 1), jnp.concatenate([zero, w(a, 2)], 1)], 0
    )
    return own, rim


def tall(ref, a, b):
    if not 0 <= b <= 2:
        return jnp.zeros((8, 128), F32)
    return jnp.concatenate([ref[3 * a + b].astype(F32), jnp.zeros((4, 128), F32)], 0)


def form_in(w, out):
    taps = [jnp.concatenate([tall(w, a, q - p) for p in range(2)], 1) for a in range(3) for q in range(4)]
    out[...] = (0.5 * jnp.concatenate(taps, 0)).astype(BF)


def form_out(w, out):
    taps = [
        jnp.concatenate([tall(w, a, q - p) for q in (1, 2, 0, 3)], 1) for a in range(3) for p in range(2)
    ]
    out[...] = jnp.concatenate(taps, 0).astype(BF)


def form_pairs(w, chans, out):
    half = jnp.asarray(0.5, BF)
    for a in range(3):
        own, rim = pair_weight(lambda i, b: w[3 * i + b][:, 0:chans] * half, a)
        out[:, 512 * a : 512 * a + 256] = own
        out[:, 512 * a + 256 : 512 * a + 512] = rim


def form_down(w, out):
    half = jnp.asarray(0.5, BF)
    for a in range(3):
        out[:, 256 * a : 256 * a + 128] = w[3 * a + 1] * half
        out[:, 256 * a + 128 : 256 * a + 256] = w[3 * a + 2] * half
        out[:, 768 + 128 * a : 896 + 128 * a] = w[3 * a] * half


def form_mid(w, out):
    half = jnp.asarray(0.5, BF)
    for a in range(3):
        for b in range(3):
            out[:, 768 * a + 256 * b : 768 * a + 256 * b + 256] = w[3 * a + b] * half


def form_up(w, even, odd):
    def up(a, b):
        return 0.5 * w[3 * a + b][:, 128:384].astype(F32)

    for out, sets in ((even, ((0,), (1, 2))), (odd, ((0, 1), (2,)))):
        for k, taps in enumerate(sets):
            col = [sum(up(a, b) for a in taps) for b in range(3)]
            zero = jnp.zeros_like(col[0])
            out[:, 768 * k : 768 * k + 256] = jnp.concatenate([col[0], zero], 0).astype(BF)
            out[:, 768 * k + 256 : 768 * k + 512] = jnp.concatenate(
                [col[1] + col[2], col[0] + col[1]], 0
            ).astype(BF)
            out[:, 768 * k + 512 : 768 * k + 768] = jnp.concatenate([zero, col[2]], 0).astype(BF)


def parts(total, most):
    count = -(-total // most)
    cuts = [total * i // count for i in range(count + 1)]
    return [(a, b - a) for a, b in zip(cuts, cuts[1:])]


class Field:
    def __init__(self, width, masks):
        self.tile = lax.axis_index("tile")
        self.masks = masks
        lane = lax.broadcasted_iota(jnp.int32, (HALF, 256), 1)
        pair = lax.broadcasted_iota(jnp.int32, (HALF, 256), 0)
        masks[0] = jnp.zeros((HALF, 256), F32)
        masks[1] = (2 * pair + lane // 128 < width).astype(F32)
        masks[2] = (2 * pair < width).astype(F32)
        self.natural = (lax.broadcasted_iota(jnp.int32, (4, 256), 1) < width).astype(F32)

    def fine_ok(self, rho):
        row = self.tile * 4 + rho
        return jnp.logical_and(row >= 0, row < ROWS).astype(jnp.int32)

    def half_ok(self, h):
        row = self.tile * 2 + h
        return jnp.logical_and(row >= 0, row < ROWS // 2).astype(jnp.int32)

    def keep_pairs(self, y, center, rim, at, rho):
        y = y * self.masks[self.fine_ok(rho)]
        center[at] = y.astype(BF)
        rim[at] = jnp.concatenate([slide(y[:, 128:], 1), slide(y[:, :128], -1)], 1).astype(BF)

    def keep_half(self, y, center, left, right, at, h):
        y = y * self.masks[2 * self.half_ok(h)]
        center[at] = y.astype(BF)
        left[at] = slide(y, 1).astype(BF)
        right[at] = slide(y, -1).astype(BF)


def embedding(w_sigma, now):
    return jnp.concatenate([w_sigma[...], w_sigma[...]], 1) * jnp.log(now)


def slide(x, by):
    x = pltpu.roll(x, by % HALF, 0)
    where = lax.broadcasted_iota(jnp.int32, (8, x.shape[1]), 0)
    if by == 1:
        return jnp.concatenate([jnp.where(where == 0, 0.0, x[:8]), x[8:]], 0)
    return jnp.concatenate([x[: HALF - 8], jnp.where(where == 7, 0.0, x[HALF - 8 :])], 0)


def stacked(ref, at, n, step=1):
    return jnp.concatenate([ref[at + step * k] for k in range(n)], 0)


def encoder(field, rows, state, spread, scale, bias, f_in, f_enc, firstc, firste, secondc, seconde):
    n_state = rows["scaled"][1]
    first_lo, n_first = rows["first"]
    second_lo, n_second = rows["second"]
    col = lax.broadcasted_iota(jnp.int32, (256, 512), 0)
    place = lax.broadcasted_iota(jnp.int32, (256, 512), 1)
    pick = (col == 2 * (place % 128) + place // 128 - 1).astype(F32).astype(BF)
    scaled = (state[0 : 8 * n_state, :] * scale).astype(BF)
    spread[0 : 8 * n_state, :] = jnp.dot(scaled, pick, preferred_element_type=F32)
    for at, n in parts(n_first, BLOCKS[0]):
        cols = [
            jnp.concatenate(
                [
                    spread[8 * (k + a) : 8 * (k + a) + 8, 128 * q : 128 * q + 128]
                    for a in range(3)
                    for q in range(4)
                ],
                0,
            )
            for k in range(at, at + n)
        ]
        x = jnp.concatenate(cols, 1).astype(BF)
        y = lax.dot_general(x, f_in[...], TN, preferred_element_type=F32)
        for k in range(n):
            part = silu_twice(y[k * HALF : (k + 1) * HALF] + bias)
            field.keep_pairs(part, firstc, firste, at + k, first_lo + at + k)

    for at, n in parts(n_second, BLOCKS[1]):
        x = jnp.concatenate([stacked(ref, at + a, n) for a in range(3) for ref in (firstc, firste)], 1)
        y = dot_nt(x, f_enc[...])
        for k in range(n):
            part = silu_twice(y[k * HALF : (k + 1) * HALF])
            field.keep_pairs(part, secondc, seconde, at + k, second_lo + at + k)

def first_kernel(
    width_ref, sigma_ref, own, up3, down3, near_up, near_down, w_sigma, w_in, w_enc,
    state_ref, secondc, seconde,
    state, spread, firstc, firste, masks, f_in, f_enc,
):
    field = Field(width_ref[0], masks)
    form_in(w_in, f_in)
    form_pairs(w_enc, 128, f_enc)
    sigma, scale = levels(sigma_ref, 0)[:2]

    empty = jnp.zeros((4, 256), F32)
    held = {-3: (up3, 0), 3: (down3, 0)}
    for slot in range(3):
        held[3 * slot - 4] = (near_up, 128 + 32 * slot)
        held[3 * slot - 2] = (near_down, 128 + 32 * slot)
    state_lo = STEP_ROWS[0]["scaled"][0]
    for tile_off in range(-4, 4):
        if tile_off == 0:
            value = own[...]
        else:
            ref, begin = held[tile_off]
            value = ref[begin : begin + 16, :].astype(F32) + ref[begin + 16 : begin + 32, :].astype(F32)
        for r in range(4):
            rho = 4 * tile_off + r
            if rho >= state_lo:
                row = jnp.concatenate([value[4 * r : 4 * r + 4], empty], 0)
                at = 8 * (rho - state_lo)
                state[at : at + 8, :] = row * field.fine_ok(rho).astype(F32)

    rows = STEP_ROWS[0]
    out_lo, n_out = rows["out"]
    state_ref[...] = state[8 * (out_lo - state_lo) : 8 * (out_lo - state_lo + n_out), :]
    bias = 0.5 * embedding(w_sigma, sigma)
    encoder(field, rows, state, spread, scale, bias, f_in, f_enc, firstc, firste, secondc, seconde)


def second_kernel(
    width_ref, sigma_ref, state_in, secondc0, seconde0, near_up, near_down, cond_own, far_up, far_down,
    w_sigma, w_in, w_out, w_enc, w_down, w_mid, w_dec,
    out_ref,
    state, spread, firstc, firste, secondc1, seconde1, third, thirdl, thirdr, fourth, fourthl, fourthr,
    fifthc, fifthe, prod, picked, masks,
    f_in, f_out, f_enc, f_down, f_mid, f_dec, f_even, f_odd,
):
    field = Field(width_ref[0], masks)
    form_in(w_in, f_in)
    form_out(w_out, f_out)
    form_pairs(w_enc, 128, f_enc)
    form_down(w_down, f_down)
    form_mid(w_mid, f_mid)
    form_pairs(w_dec, 128, f_dec)
    form_up(w_dec, f_even, f_odd)

    empty = jnp.zeros((4, 256), F32)
    weave_j = lax.broadcasted_iota(jnp.int32, (256, 256), 0)
    weave_c = lax.broadcasted_iota(jnp.int32, (256, 256), 1)
    weave = (weave_c == 2 * (weave_j % HALF) + weave_j // HALF).astype(F32).astype(BF)
    repeat = (
        lax.broadcasted_iota(jnp.int32, (HALF, 64), 0) // 2 == lax.broadcasted_iota(jnp.int32, (HALF, 64), 1)
    ).astype(F32)
    repeat = (0.5 * repeat).astype(BF)
    conds = [
        (ref, r)
        for ref, n in ((far_up, 4), (near_up, 2), (cond_own, 2), (near_down, 2), (far_down, 4))
        for r in range(n)
    ]

    for step in range(2):
        rows = STEP_ROWS[step]
        sigma, scale, keep, mix, move = levels(sigma_ref, step)
        second_lo = rows["second"][0]
        third_lo, n_third = rows["third"]
        fourth_lo, n_fourth = rows["fourth"]
        fifth_lo, n_fifth = rows["fifth"]
        out_lo, n_out = rows["out"]

        secondc, seconde = (secondc0, seconde0) if step == 0 else (secondc1, seconde1)
        if step == 1:
            bias = 0.5 * embedding(w_sigma, sigma)
            encoder(field, rows, state, spread, scale, bias, f_in, f_enc, firstc, firste, secondc, seconde)

        for at, n in parts(n_third, BLOCKS[2]):
            begin = 2 * (third_lo + at) - 1 - second_lo
            x = jnp.concatenate(
                [stacked(secondc, begin + a, n, 2) for a in range(3)]
                + [
                    jnp.concatenate([seconde[begin + a + 2 * k][:, :128] for k in range(n)], 0)
                    for a in range(3)
                ],
                1,
            )
            y = dot_nt(x, f_down[...])
            for k in range(n):
                ref, r = conds[third_lo + at + k + 6]
                add = jnp.dot(repeat, ref[64 * r : 64 * r + 64, :], preferred_element_type=F32)
                part = silu_twice(y[k * HALF : (k + 1) * HALF] + add)
                field.keep_half(part, third, thirdl, thirdr, at + k, third_lo + at + k)

        for at, n in parts(n_fourth, BLOCKS[3]):
            x = jnp.concatenate(
                [stacked(ref, at + a, n) for a in range(3) for ref in (thirdl, third, thirdr)], 1
            )
            y = dot_nt(x, f_mid[...])
            for k in range(n):
                part = silu_twice(y[k * HALF : (k + 1) * HALF])
                field.keep_half(part, fourth, fourthl, fourthr, at + k, fourth_lo + at + k)

        for parity in range(2):
            for cut, n in parts((n_fifth - parity + 1) // 2, BLOCKS[4]):
                at = parity + 2 * cut
                rho = fifth_lo + at
                odd = rho % 2
                begin = rho - 1 - second_lo
                h = (rho - odd) // 2 - fourth_lo - (0 if odd else 1)
                x = jnp.concatenate(
                    [stacked(ref, begin + a, n, 2) for a in range(3) for ref in (secondc, seconde)], 1
                )
                z = jnp.concatenate(
                    [stacked(ref, h + a, n) for a in range(2) for ref in (fourthl, fourth, fourthr)], 1
                )
                y = dot_nt(x, f_dec[...]) + dot_nt(z, (f_odd if odd else f_even)[...])
                for k in range(n):
                    part = silu_twice(y[k * HALF : (k + 1) * HALF])
                    field.keep_pairs(part, fifthc, fifthe, at + 2 * k, fifth_lo + at + 2 * k)

        for at, n in parts(n_fifth, BLOCKS[5]):
            x = jnp.concatenate([stacked(fifthc, at, n), stacked(fifthe, at, n)], 1)
            prod[:, at * HALF : (at + n) * HALF] = dot_nt(f_out[...], x)
        for k in range(n_out):
            for p in range(2):
                picked[8 * k : 8 * k + 8, HALF * p : HALF * p + HALF] = sum(
                    prod[16 * a + 8 * p : 16 * a + 8 * p + 8, (k + a) * HALF : (k + a + 1) * HALF]
                    for a in range(3)
                )
        value = picked[0 : 8 * n_out, :]
        high = value.astype(BF)
        low = (value - high.astype(F32)).astype(BF)
        net = jnp.dot(high, weave, preferred_element_type=F32) + jnp.dot(low, weave, preferred_element_type=F32)
        if step == 0:
            now = state_in[...]
        else:
            skip = 8 * (out_lo - rows["scaled"][0])
            now = state[skip : skip + 8 * n_out, :]
        denoised = keep * now + mix * net
        now = now + move * (now - denoised)
        for k in range(n_out):
            if step == 0:
                mask = field.natural * field.fine_ok(out_lo + k).astype(F32)
                state[8 * k : 8 * k + 8, :] = jnp.concatenate([now[8 * k : 8 * k + 4] * mask, empty], 0)
            else:
                out_ref[:, k, :] = now[8 * k : 8 * k + 4] * field.natural


def turn(x, by):
    n = lax.axis_size("tile")
    return lax.ppermute(x, "tile", [(i, (i + by) % n) for i in range(n)])


VMEM = pl.BlockSpec(memory_space=pltpu.VMEM)
SMEM = pl.BlockSpec(memory_space=pltpu.SMEM)


LIMIT = 24


def limit(mib):
    return pltpu.CompilerParams(vmem_limit_bytes=mib << 20)


def rowbuf(n):
    return pltpu.VMEM((n, HALF, 256), BF)


def cost(passes):
    return pl.CostEstimate(flops=passes * 128 * 65536 * 2, bytes_accessed=1 << 20, transcendentals=0)


def first_call(*args):
    rows = STEP_ROWS[0]
    n = rows["scaled"][1]
    return pl.pallas_call(
        first_kernel,
        out_shape=[
            jax.ShapeDtypeStruct((rows["out"][1] * 8, 256), F32),
            *[jax.ShapeDtypeStruct((rows["second"][1], HALF, 256), BF)] * 2,
        ],
        in_specs=[SMEM, SMEM] + [VMEM] * 8,
        out_specs=[VMEM] * 3,
        scratch_shapes=[
            pltpu.VMEM((n * 8, 256), F32), pltpu.VMEM((n * 8, 512), F32),
            *[rowbuf(rows["first"][1])] * 2,
            pltpu.VMEM((3, HALF, 256), F32),
            pltpu.VMEM((96, 256), BF), pltpu.VMEM((256, 1536), BF),
        ],
        compiler_params=limit(16),
        cost_estimate=cost(200),
        name="first",
    )(*args)


def second_call(*args):
    rows, late = STEP_ROWS
    n = late["scaled"][1]
    return pl.pallas_call(
        second_kernel,
        out_shape=jax.ShapeDtypeStruct((4, 4, 256), F32),
        in_specs=[SMEM, SMEM] + [VMEM] * 15,
        out_specs=VMEM,
        scratch_shapes=[
            pltpu.VMEM((n * 8, 256), F32), pltpu.VMEM((n * 8, 512), F32),
            *[rowbuf(late["first"][1])] * 2, *[rowbuf(late["second"][1])] * 2,
            *[rowbuf(rows["third"][1])] * 3, *[rowbuf(rows["fourth"][1])] * 3, *[rowbuf(rows["fifth"][1])] * 2,
            pltpu.VMEM((48, rows["fifth"][1] * HALF), F32),
            pltpu.VMEM((rows["out"][1] * 8, 256), F32),
            pltpu.VMEM((3, HALF, 256), F32),
            *[
                pltpu.VMEM(shape, BF)
                for shape in (
                    (96, 256), (48, 512), (256, 1536), (256, 1152), (256, 2304),
                    (256, 1536), (256, 1536), (256, 1536),
                )
            ],
        ],
        compiler_params=limit(LIMIT),
        cost_estimate=cost(600),
        name="second",
    )(*args)


def encode_call(block_anchor, nest_width, sigmas, coarse_blocks, w_context, noise):
    chans = w_context.shape[1]
    cells = coarse_blocks.shape[1] // chans
    count = coarse_blocks.shape[0]
    tiles = coarse_blocks.shape[1] // 128
    return pl.pallas_call(
        encode_kernel,
        out_shape=[
            jax.ShapeDtypeStruct((8, 2 * cells, 256), BF),
            jax.ShapeDtypeStruct((16, 256), F32),
            jax.ShapeDtypeStruct((32, 256), BF),
        ],
        in_specs=[SMEM, SMEM, SMEM, VMEM, VMEM, VMEM],
        out_specs=[VMEM] * 3,
        scratch_shapes=[
            pltpu.VMEM((count + 8, cells, 256), F32),
            pltpu.VMEM((count * tiles + 64, 128), F32),
            pltpu.VMEM((2, 80, 128), F32),
        ],
        compiler_params=limit(56),
        cost_estimate=cost(100),
        name="encode",
    )(block_anchor, nest_width, sigmas, coarse_blocks, w_context.T, noise)


def per_device(
    coarse_blocks, block_anchor, nest_width, sigmas, noise,
    w_context, w_in, w_sigma, w_enc, w_down, w_mid, w_dec, w_out,
):
    partial, own, own_parts = encode_call(
        block_anchor, nest_width, sigmas, coarse_blocks, w_context, noise[0]
    )
    arrived = lax.all_to_all(partial, "band", 0, 0, tiled=True)

    up3 = turn(own_parts, 3)
    down3 = turn(own_parts, -3)
    arrived, up3, down3 = lax.optimization_barrier((arrived, up3, down3))

    cond = (jnp.sum(arrived.astype(F32), axis=0) * (1.0 / math.sqrt(K // 2))).astype(BF)
    parcel = jnp.concatenate([cond, up3, own_parts, down3], 0)
    near_up = turn(parcel, 1)
    near_down = turn(parcel, -1)
    far_up = turn(jnp.concatenate([near_up[:128], cond], 0), 2)
    far_down = turn(jnp.concatenate([cond, near_down[:128]], 0), -2)
    w_sigma = w_sigma.reshape(1, -1)
    w_in = w_in.transpose(0, 2, 1)
    fields = first_call(nest_width, sigmas, own, up3, down3, near_up, near_down, w_sigma, w_in, w_enc)
    out = second_call(
        nest_width, sigmas, *fields, near_up, near_down, cond, far_up, far_down,
        w_sigma, w_in, w_out, w_enc, w_down, w_mid, w_dec,
    )
    return out[None]


def solution(mesh):
    return jax.shard_map(
        per_device,
        mesh=mesh,
        in_specs=(
            P("band", None), P(), P("band"), P(), P("band", None, "tile", None),
            P(), P(), P(), P(), P(), P(), P(), P(),
        ),
        out_specs=P("band", None, "tile", None),
        check_vma=False,
    )
```

```python
import functools
import math

import jax
import jax.numpy as jnp
from jax import lax
from jax.experimental import pallas as pl
from jax.experimental.pallas import tpu as pltpu
from jax.sharding import PartitionSpec as P

K = 96
SIGMA_DATA = 0.5
BF = jnp.bfloat16
F32 = jnp.float32
HALF = 128
ROWS = 256
NT = (((1,), (1,)), ((), ()))
TN = (((0,), (0,)), ((), ()))

BLOCKS = (5, 5, 3, 2, 5, 6)
FIELDS = ("scaled", "first", "second", "third", "fourth", "fifth", "out")
STEP_ROWS = (
    dict(zip(FIELDS, ((-7, 21), (-6, 19), (-5, 17), (-2, 8), (-1, 6), (-1, 10), (0, 8)))),
    dict(zip(FIELDS, ((-7, 17), (-6, 15), (-5, 13), (-2, 6), (-1, 4), (-1, 6), (0, 4)))),
)


def silu_twice(h):
    return h + h * jnp.tanh(h)


def dot_nt(a, b):
    return lax.dot_general(a, b, NT, preferred_element_type=F32)


def levels(sigma_ref, step):
    now = jnp.full((1, 256), sigma_ref[step], F32)
    after = jnp.full((1, 256), sigma_ref[step + 1], F32)
    var = now * now + SIGMA_DATA * SIGMA_DATA
    root = jnp.sqrt(var)
    return now, 1.0 / root, SIGMA_DATA * SIGMA_DATA / var, now * SIGMA_DATA / root, (after - now) / now


def encode_kernel(
    anchor_ref, width_ref, sigma_ref, blocks_ref, w_ref, noise_ref, out_ref, state_ref, scaled_ref, parts_ref, enc_ref, flat, wide
):
    band = lax.axis_index("band")
    tile = lax.axis_index("tile")
    count = blocks_ref.shape[0]
    cells = enc_ref.shape[1]
    chans = w_ref.shape[0]
    tiles = blocks_ref.shape[1] // 128
    group = 8 * tiles

    flat[count * tiles :, :] = jnp.zeros((flat.shape[0] - count * tiles, 128), F32)
    for g in range(count // 16):
        for t in range(tiles):
            v = blocks_ref[16 * g : 16 * g + 16, 128 * t : 128 * t + 128].astype(F32)
            flat[2 * g * group + 8 * t : 2 * g * group + 8 * t + 8, :] = v[:8]
            flat[(2 * g + 1) * group + 8 * t : (2 * g + 1) * group + 8 * t + 8, :] = v[8:]

    sigma, scale = levels(sigma_ref, 0)[:2]
    natural = (lax.broadcasted_iota(jnp.int32, (4, 256), 1) < width_ref[0]).astype(F32)
    for r in range(4):
        row = sigma * noise_ref[:, r, :] * natural
        state_ref[4 * r : 4 * r + 4, :] = row
        scaled_ref[4 * r : 4 * r + 4, :] = (row * scale).astype(BF)
    state = state_ref[...]
    high = state.astype(BF)
    parts_ref[0:16, :] = high
    parts_ref[16:32, :] = (state - high.astype(F32)).astype(BF)

    w = 0.5 * w_ref[...].astype(F32)
    for half in range(2):
        wide[half, 0:chans, :] = w[:, 128 * half : 128 * half + 128]
        wide[half, chans:80, :] = jnp.zeros((80 - chans, 128), F32)
    weight = jnp.concatenate(
        [
            jnp.concatenate([wide[half, pl.ds(odd, 40, stride=2), :] for half in range(2)], 1)
            for odd in range(2)
        ],
        0,
    ).astype(BF)
    first = lax.broadcasted_iota(jnp.int32, (40, 128), 1) < 64

    def encode(g, carry):
        begin = pl.multiple_of(g * group, 8)
        cols = []
        for k in range(4):
            one = flat[pl.ds(begin + 2 * k, 40, stride=8), :]
            two = flat[pl.ds(begin + 2 * k + 1, 40, stride=8), :]
            even = jnp.where(first, one, pltpu.roll(two, 64, 1))
            odd = jnp.where(first, pltpu.roll(one, 64, 1), two)
            cols.append(jnp.concatenate([even, odd], 0))
        x = jnp.concatenate(cols, 1).astype(BF)
        v = lax.dot_general(x, weight, TN, preferred_element_type=F32)
        v = silu_twice(v).astype(BF).astype(F32)
        enc_ref[pl.ds(g * 8, 8)] = v.reshape(8, cells, 256)
        return carry

    lax.fori_loop(0, count // 8, encode, 0, unroll=True)

    enc_ref[pl.ds(count, 8)] = enc_ref[pl.ds(0, 8)]

    def window(k, carry):
        nest = k // 2
        part = k % 2
        anchor = anchor_ref[nest, tile]
        begin = anchor + (band - anchor + 512) % 8 + part * 48
        row = (begin % 512) // 8
        total = enc_ref[row]
        for m in range(1, 6):
            total = total + enc_ref[row + m]
        out_ref[nest, pl.ds(pl.multiple_of(part * cells, cells), cells), :] = total.astype(BF)
        return carry

    lax.fori_loop(0, 16, window, 0, unroll=4)


def pair_weight(w, a):
    zero = jnp.zeros_like(w(a, 0))
    own = jnp.concatenate(
        [jnp.concatenate([w(a, 1), w(a, 2)], 1), jnp.concatenate([w(a, 0), w(a, 1)], 1)], 0
    )
    rim = jnp.concatenate(
        [jnp.concatenate([w(a, 0), zero], 1), jnp.concatenate([zero, w(a, 2)], 1)], 0
    )
    return own, rim


def tall(ref, a, b):
    if not 0 <= b <= 2:
        return jnp.zeros((8, 128), F32)
    return jnp.concatenate([ref[3 * a + b].astype(F32), jnp.zeros((4, 128), F32)], 0)


def form_in(w, out):
    taps = [jnp.concatenate([tall(w, a, q - p) for p in range(2)], 1) for a in range(3) for q in range(4)]
    out[...] = (0.5 * jnp.concatenate(taps, 0)).astype(BF)


def form_out(w, out):
    taps = [
        jnp.concatenate([tall(w, a, q - p) for q in (1, 2, 0, 3)], 1) for a in range(3) for p in range(2)
    ]
    out[...] = jnp.concatenate(taps, 0).astype(BF)


def form_pairs(w, chans, out):
    half = jnp.asarray(0.5, BF)
    for a in range(3):
        own, rim = pair_weight(lambda i, b: w[3 * i + b][:, 0:chans] * half, a)
        out[:, 512 * a : 512 * a + 256] = own
        out[:, 512 * a + 256 : 512 * a + 512] = rim


def form_down(w, out):
    half = jnp.asarray(0.5, BF)
    for a in range(3):
        out[:, 256 * a : 256 * a + 128] = w[3 * a + 1] * half
        out[:, 256 * a + 128 : 256 * a + 256] = w[3 * a + 2] * half
        out[:, 768 + 128 * a : 896 + 128 * a] = w[3 * a] * half


def form_mid(w, out):
    half = jnp.asarray(0.5, BF)
    for a in range(3):
        for b in range(3):
            out[:, 768 * a + 256 * b : 768 * a + 256 * b + 256] = w[3 * a + b] * half


def form_up(w, even, odd):
    def up(a, b):
        return 0.5 * w[3 * a + b][:, 128:384].astype(F32)

    for out, sets in ((even, ((0,), (1, 2))), (odd, ((0, 1), (2,)))):
        for k, taps in enumerate(sets):
            col = [sum(up(a, b) for a in taps) for b in range(3)]
            zero = jnp.zeros_like(col[0])
            out[:, 768 * k : 768 * k + 256] = jnp.concatenate([col[0], zero], 0).astype(BF)
            out[:, 768 * k + 256 : 768 * k + 512] = jnp.concatenate(
                [col[1] + col[2], col[0] + col[1]], 0
            ).astype(BF)
            out[:, 768 * k + 512 : 768 * k + 768] = jnp.concatenate([zero, col[2]], 0).astype(BF)


def parts(total, most):
    count = -(-total // most)
    cuts = [total * i // count for i in range(count + 1)]
    return [(a, b - a) for a, b in zip(cuts, cuts[1:])]


class Field:
    def __init__(self, width, masks):
        self.tile = lax.axis_index("tile")
        self.masks = masks
        lane = lax.broadcasted_iota(jnp.int32, (HALF, 256), 1)
        pair = lax.broadcasted_iota(jnp.int32, (HALF, 256), 0)
        masks[0] = jnp.zeros((HALF, 256), F32)
        masks[1] = (2 * pair + lane // 128 < width).astype(F32)
        masks[2] = (2 * pair < width).astype(F32)
        self.natural = (lax.broadcasted_iota(jnp.int32, (4, 256), 1) < width).astype(F32)

    def fine_ok(self, rho):
        row = self.tile * 4 + rho
        return jnp.logical_and(row >= 0, row < ROWS).astype(jnp.int32)

    def half_ok(self, h):
        row = self.tile * 2 + h
        return jnp.logical_and(row >= 0, row < ROWS // 2).astype(jnp.int32)

    def keep_pairs(self, y, center, rim, at, rho):
        y = y * self.masks[self.fine_ok(rho)]
        center[at] = y.astype(BF)
        rim[at] = jnp.concatenate([slide(y[:, 128:], 1), slide(y[:, :128], -1)], 1).astype(BF)

    def keep_half(self, y, center, left, right, at, h):
        y = y * self.masks[2 * self.half_ok(h)]
        center[at] = y.astype(BF)
        left[at] = slide(y, 1).astype(BF)
        right[at] = slide(y, -1).astype(BF)


def embedding(w_sigma, now):
    return jnp.concatenate([w_sigma[...], w_sigma[...]], 1) * jnp.log(now)


def slide(x, by):
    x = pltpu.roll(x, by % HALF, 0)
    where = lax.broadcasted_iota(jnp.int32, (8, x.shape[1]), 0)
    if by == 1:
        return jnp.concatenate([jnp.where(where == 0, 0.0, x[:8]), x[8:]], 0)
    return jnp.concatenate([x[: HALF - 8], jnp.where(where == 7, 0.0, x[HALF - 8 :])], 0)


def stacked(ref, at, n, step=1):
    return jnp.concatenate([ref[at + step * k] for k in range(n)], 0)


def encoder(field, rows, scaled, spread, bias, f_in, f_enc, firstc, firste, secondc, seconde):
    n_state = rows["scaled"][1]
    first_lo, n_first = rows["first"]
    second_lo, n_second = rows["second"]
    col = lax.broadcasted_iota(jnp.int32, (256, 512), 0)
    place = lax.broadcasted_iota(jnp.int32, (256, 512), 1)
    pick = (col == 2 * (place % 128) + place // 128 - 1).astype(F32).astype(BF)
    spread[0 : 8 * n_state, :] = jnp.dot(scaled[...].astype(BF), pick, preferred_element_type=F32)
    for at, n in parts(n_first, BLOCKS[0]):
        cols = [
            jnp.concatenate(
                [
                    spread[8 * (k + a) : 8 * (k + a) + 8, 128 * q : 128 * q + 128]
                    for a in range(3)
                    for q in range(4)
                ],
                0,
            )
            for k in range(at, at + n)
        ]
        x = jnp.concatenate(cols, 1).astype(BF)
        y = lax.dot_general(x, f_in[...], TN, preferred_element_type=F32)
        for k in range(n):
            part = silu_twice(y[k * HALF : (k + 1) * HALF] + bias)
            field.keep_pairs(part, firstc, firste, at + k, first_lo + at + k)

    for at, n in parts(n_second, BLOCKS[1]):
        x = jnp.concatenate([stacked(ref, at + a, n) for a in range(3) for ref in (firstc, firste)], 1)
        y = dot_nt(x, f_enc[...])
        for k in range(n):
            part = silu_twice(y[k * HALF : (k + 1) * HALF])
            field.keep_pairs(part, secondc, seconde, at + k, second_lo + at + k)

def step_kernel(
    step, width_ref, sigma_ref, own, halo, conds, weights, state_ref, scaled_ref,
    state, spread, firstc, firste, secondc, seconde, third, thirdl, thirdr, fourth, fourthl, fourthr,
    fifthc, fifthe, prod, picked, masks,
    f_in, f_out, f_enc, f_down, f_mid, f_dec, f_even, f_odd,
):
    w_sigma, w_in, w_out, w_enc, w_down, w_mid, w_dec = weights
    field = Field(width_ref[0], masks)
    form_in(w_in, f_in)
    form_out(w_out, f_out)
    form_pairs(w_enc, 128, f_enc)
    form_down(w_down, f_down)
    form_mid(w_mid, f_mid)
    form_pairs(w_dec, 128, f_dec)
    form_up(w_dec, f_even, f_odd)
    rows = STEP_ROWS[step]
    sigma, scale, keep, mix, move = levels(sigma_ref, step)
    scaled_lo, n_scaled = rows["scaled"]
    second_lo = rows["second"][0]
    third_lo, n_third = rows["third"]
    fourth_lo, n_fourth = rows["fourth"]
    fifth_lo, n_fifth = rows["fifth"]
    n_out = rows["out"][1]

    empty = jnp.zeros((4, 256), F32)
    pieces = [(rho, ref[begin : begin + 4 * n, :].astype(F32), n) for rho, n, ref, begin in halo]
    pieces += [(rho, (value * scale).astype(BF).astype(F32), n) for rho, value, n in own]
    for lo, value, n in pieces:
        for r in range(n):
            rho = lo + r
            if scaled_lo <= rho < scaled_lo + n_scaled:
                row = jnp.concatenate([value[4 * r : 4 * r + 4], empty], 0)
                at = 8 * (rho - scaled_lo)
                state[at : at + 8, :] = row * field.fine_ok(rho).astype(F32)
    weave_j = lax.broadcasted_iota(jnp.int32, (256, 256), 0)
    weave_c = lax.broadcasted_iota(jnp.int32, (256, 256), 1)
    weave = (weave_c == 2 * (weave_j % HALF) + weave_j // HALF).astype(F32).astype(BF)
    repeat = (
        lax.broadcasted_iota(jnp.int32, (HALF, 64), 0) // 2 == lax.broadcasted_iota(jnp.int32, (HALF, 64), 1)
    ).astype(F32)
    repeat = (0.5 * repeat).astype(BF)
    bias = 0.5 * embedding(w_sigma, sigma)
    encoder(field, rows, state, spread, bias, f_in, f_enc, firstc, firste, secondc, seconde)

    for at, n in parts(n_third, BLOCKS[2]):
        begin = 2 * (third_lo + at) - 1 - second_lo
        x = jnp.concatenate(
            [stacked(secondc, begin + a, n, 2) for a in range(3)]
            + [
                jnp.concatenate([seconde[begin + a + 2 * k][:, :128] for k in range(n)], 0)
                for a in range(3)
            ],
            1,
        )
        y = dot_nt(x, f_down[...])
        for k in range(n):
            ref, r = conds[at + k]
            add = jnp.dot(repeat, ref[64 * r : 64 * r + 64, :], preferred_element_type=F32)
            part = silu_twice(y[k * HALF : (k + 1) * HALF] + add)
            field.keep_half(part, third, thirdl, thirdr, at + k, third_lo + at + k)

    for at, n in parts(n_fourth, BLOCKS[3]):
        x = jnp.concatenate(
            [stacked(ref, at + a, n) for a in range(3) for ref in (thirdl, third, thirdr)], 1
        )
        y = dot_nt(x, f_mid[...])
        for k in range(n):
            part = silu_twice(y[k * HALF : (k + 1) * HALF])
            field.keep_half(part, fourth, fourthl, fourthr, at + k, fourth_lo + at + k)

    for parity in range(2):
        for cut, n in parts((n_fifth - parity + 1) // 2, BLOCKS[4]):
            at = parity + 2 * cut
            rho = fifth_lo + at
            odd = rho % 2
            begin = rho - 1 - second_lo
            h = (rho - odd) // 2 - fourth_lo - (0 if odd else 1)
            x = jnp.concatenate(
                [stacked(ref, begin + a, n, 2) for a in range(3) for ref in (secondc, seconde)], 1
            )
            z = jnp.concatenate(
                [stacked(ref, h + a, n) for a in range(2) for ref in (fourthl, fourth, fourthr)], 1
            )
            y = dot_nt(x, f_dec[...]) + dot_nt(z, (f_odd if odd else f_even)[...])
            for k in range(n):
                part = silu_twice(y[k * HALF : (k + 1) * HALF])
                field.keep_pairs(part, fifthc, fifthe, at + 2 * k, fifth_lo + at + 2 * k)

    for at, n in parts(n_fifth, BLOCKS[5]):
        x = jnp.concatenate([stacked(fifthc, at, n), stacked(fifthe, at, n)], 1)
        prod[:, at * HALF : (at + n) * HALF] = dot_nt(f_out[...], x)
    for k in range(n_out):
        for p in range(2):
            picked[8 * k : 8 * k + 8, HALF * p : HALF * p + HALF] = sum(
                prod[16 * a + 8 * p : 16 * a + 8 * p + 8, (k + a) * HALF : (k + a + 1) * HALF]
                for a in range(3)
            )
    value = picked[0 : 8 * n_out, :]
    high = value.astype(BF)
    low = (value - high.astype(F32)).astype(BF)
    net = jnp.dot(high, weave, preferred_element_type=F32) + jnp.dot(low, weave, preferred_element_type=F32)
    states = jnp.concatenate([value for _, value, _ in own], 0)
    if step == 0:
        next_scale = levels(sigma_ref, 1)[1]
    for k in range(n_out):
        now = states[4 * k : 4 * k + 4]
        denoised = keep * now + mix * net[8 * k : 8 * k + 4]
        now = (now + move * (now - denoised)) * (field.natural * field.fine_ok(k).astype(F32))
        if step == 0:
            state_ref[4 * k : 4 * k + 4, :] = now
            scaled_ref[4 * k : 4 * k + 4, :] = (now * next_scale).astype(BF)
        else:
            state_ref[:, k, :] = now


def turn(x, by):
    n = lax.axis_size("tile")
    return lax.ppermute(x, "tile", [(i, (i + by) % n) for i in range(n)])


VMEM = pl.BlockSpec(memory_space=pltpu.VMEM)
SMEM = pl.BlockSpec(memory_space=pltpu.SMEM)


LIMIT = 20


def limit(mib):
    return pltpu.CompilerParams(vmem_limit_bytes=mib << 20)


def rowbuf(n):
    return pltpu.VMEM((n, HALF, 256), BF)


def cost(passes):
    return pl.CostEstimate(flops=passes * 128 * 65536 * 2, bytes_accessed=1 << 20, transcendentals=0)


def step_call(step, arrays, width, sigmas, weights):
    rows = STEP_ROWS[step]
    n_arrays, n_weights = len(arrays), len(weights)
    n_out = rows["out"][1]
    if step == 0:
        outs = [jax.ShapeDtypeStruct((4 * n_out, 256), F32), jax.ShapeDtypeStruct((4 * n_out, 256), BF)]
    else:
        outs = [jax.ShapeDtypeStruct((4, 4, 256), F32)]

    def kernel(width_ref, sigma_ref, *refs):
        held, refs = refs[:n_arrays], refs[n_arrays:]
        weight_refs, refs = refs[:n_weights], refs[n_weights:]
        out_refs, refs = list(refs[: len(outs)]), refs[len(outs) :]
        near_up, near_down, cond, cond_far = held[:4]
        conds = [(ref, r) for ref in (near_up, cond, near_down, cond_far) for r in range(2)]
        if step == 0:
            own_ref, two_down = held[4:]
            below = near_down[128:144, :].astype(F32) + near_down[144:160, :].astype(F32)
            own = [(0, own_ref[...], 4), (4, below, 4)]
            halo = [(-8, 8, near_up, 128), (8, 4, two_down, 0), (12, 4, near_down, 160)]
        else:
            own_ref, up, down, top = held[4:]
            own = [(0, own_ref[...], 8)]
            second = lax.axis_index("tile") == 1
            near = jnp.where(second, top[...].astype(F32), up[16:32, :].astype(F32))
            halo = [(-8, 4, up, 0), (-4, 4, near, 0), (8, 4, down, 0)]
        step_kernel(
            step, width_ref, sigma_ref, own, halo, conds, weight_refs, *(out_refs + [None])[:2], *refs
        )

    return pl.pallas_call(
        kernel,
        out_shape=outs,
        in_specs=[SMEM, SMEM] + [VMEM] * (n_arrays + n_weights),
        out_specs=[VMEM] * len(outs),
        scratch_shapes=[
            pltpu.VMEM((rows["scaled"][1] * 8, 256), F32), pltpu.VMEM((rows["scaled"][1] * 8, 512), F32),
            *[
                rowbuf(rows[name][1])
                for name, n in (("first", 2), ("second", 2), ("third", 3), ("fourth", 3), ("fifth", 2))
                for _ in range(n)
            ],
            pltpu.VMEM((48, rows["fifth"][1] * HALF), F32),
            pltpu.VMEM((8 * n_out, 256), F32),
            pltpu.VMEM((3, HALF, 256), F32),
            *[
                pltpu.VMEM(shape, BF)
                for shape in (
                    (96, 256), (48, 512), (256, 1536), (256, 1152), (256, 2304),
                    (256, 1536), (256, 1536), (256, 1536),
                )
            ],
        ],
        compiler_params=limit(LIMIT),
        cost_estimate=cost(300),
        name="step" + str(step),
    )(width, sigmas, *arrays, *weights)


def encode_call(block_anchor, nest_width, sigmas, coarse_blocks, w_context, noise):
    chans = w_context.shape[1]
    cells = coarse_blocks.shape[1] // chans
    count = coarse_blocks.shape[0]
    tiles = coarse_blocks.shape[1] // 128
    return pl.pallas_call(
        encode_kernel,
        out_shape=[
            jax.ShapeDtypeStruct((8, 2 * cells, 256), BF),
            jax.ShapeDtypeStruct((16, 256), F32),
            jax.ShapeDtypeStruct((16, 256), BF),
            jax.ShapeDtypeStruct((32, 256), BF),
        ],
        in_specs=[SMEM, SMEM, SMEM, VMEM, VMEM, VMEM],
        out_specs=[VMEM] * 4,
        scratch_shapes=[
            pltpu.VMEM((count + 8, cells, 256), F32),
            pltpu.VMEM((count * tiles + 64, 128), F32),
            pltpu.VMEM((2, 80, 128), F32),
        ],
        compiler_params=limit(56),
        cost_estimate=cost(100),
        name="encode",
    )(block_anchor, nest_width, sigmas, coarse_blocks, w_context.T, noise)


def per_device(
    coarse_blocks, block_anchor, nest_width, sigmas, noise,
    w_context, w_in, w_sigma, w_enc, w_down, w_mid, w_dec, w_out,
):
    partial, state, scaled, own_parts = encode_call(
        block_anchor, nest_width, sigmas, coarse_blocks, w_context, noise[0]
    )
    arrived = lax.all_to_all(partial, "band", 0, 0, tiled=True)

    one_up = turn(scaled, 1)
    two_down = turn(scaled, -2)
    arrived, one_up, two_down = lax.optimization_barrier((arrived, one_up, two_down))

    cond = (jnp.sum(arrived.astype(F32), axis=0) * (1.0 / math.sqrt(K // 2))).astype(BF)
    cond_far = turn(cond, -2)
    near_up = turn(jnp.concatenate([cond, one_up, scaled], 0), 1)
    near_down = turn(jnp.concatenate([cond, own_parts, two_down], 0), -1)
    weights = (w_sigma.reshape(1, -1), w_in.transpose(0, 2, 1), w_out, w_enc, w_down, w_mid, w_dec)
    conds = (near_up, near_down, cond, cond_far)
    state, scaled = step_call(0, (*conds, state, two_down), nest_width, sigmas, weights)
    up = turn(scaled, 2)
    down = turn(scaled[16:], -1)
    top = lax.ppermute(scaled[:16], "tile", [(0, 1)])
    (out,) = step_call(1, (*conds, state, up, down, top), nest_width, sigmas, weights)
    return out[None]


def solution(mesh):
    return jax.shard_map(
        per_device,
        mesh=mesh,
        in_specs=(
            P("band", None), P(), P("band"), P(), P("band", None, "tile", None),
            P(), P(), P(), P(), P(), P(), P(), P(),
        ),
        out_specs=P("band", None, "tile", None),
        check_vma=False,
    )
```

```python
import functools
import math

import jax
import jax.numpy as jnp
from jax import lax
from jax.experimental import pallas as pl
from jax.experimental.pallas import tpu as pltpu
from jax.sharding import PartitionSpec as P

K = 96
SIGMA_DATA = 0.5
BF = jnp.bfloat16
F32 = jnp.float32
HALF = 128
ROWS = 256
NT = (((1,), (1,)), ((), ()))
TN = (((0,), (0,)), ((), ()))

BLOCKS = ((5, 5, 3, 2, 5, 6), (4, 4, 4, 3, 3, 5))
FIELDS = ("scaled", "first", "second", "third", "fourth", "fifth", "out")
STEP_ROWS = (
    dict(zip(FIELDS, ((-7, 21), (-6, 19), (-5, 17), (-2, 8), (-1, 6), (-1, 10), (0, 8)))),
    dict(zip(FIELDS, ((-7, 17), (-6, 15), (-5, 13), (-2, 6), (-1, 4), (-1, 6), (0, 4)))),
)


def silu_twice(h):
    return h + h * jnp.tanh(h)


def dot_nt(a, b):
    return lax.dot_general(a, b, NT, preferred_element_type=F32)


def levels(sigma_ref, step):
    now = jnp.full((1, 256), sigma_ref[step], F32)
    after = jnp.full((1, 256), sigma_ref[step + 1], F32)
    var = now * now + SIGMA_DATA * SIGMA_DATA
    root = jnp.sqrt(var)
    return now, 1.0 / root, SIGMA_DATA * SIGMA_DATA / var, now * SIGMA_DATA / root, (after - now) / now


def encode_kernel(
    anchor_ref, width_ref, sigma_ref, blocks_ref, w_ref, noise_ref, out_ref, state_ref, scaled_ref, parts_ref, enc_ref, flat, wide
):
    band = lax.axis_index("band")
    tile = lax.axis_index("tile")
    count = blocks_ref.shape[0]
    cells = enc_ref.shape[1]
    chans = w_ref.shape[0]
    tiles = blocks_ref.shape[1] // 128
    group = 8 * tiles

    flat[count * tiles :, :] = jnp.zeros((flat.shape[0] - count * tiles, 128), F32)
    for g in range(count // 16):
        for t in range(tiles):
            v = blocks_ref[16 * g : 16 * g + 16, 128 * t : 128 * t + 128].astype(F32)
            flat[2 * g * group + 8 * t : 2 * g * group + 8 * t + 8, :] = v[:8]
            flat[(2 * g + 1) * group + 8 * t : (2 * g + 1) * group + 8 * t + 8, :] = v[8:]

    sigma, scale = levels(sigma_ref, 0)[:2]
    natural = (lax.broadcasted_iota(jnp.int32, (4, 256), 1) < width_ref[0]).astype(F32)
    for r in range(4):
        row = sigma * noise_ref[:, r, :] * natural
        state_ref[4 * r : 4 * r + 4, :] = row
        scaled_ref[4 * r : 4 * r + 4, :] = (row * scale).astype(BF)
    state = state_ref[...]
    high = state.astype(BF)
    parts_ref[0:16, :] = high
    parts_ref[16:32, :] = (state - high.astype(F32)).astype(BF)

    w = 0.5 * w_ref[...].astype(F32)
    for half in range(2):
        wide[half, 0:chans, :] = w[:, 128 * half : 128 * half + 128]
        wide[half, chans:80, :] = jnp.zeros((80 - chans, 128), F32)
    weight = jnp.concatenate(
        [
            jnp.concatenate([wide[half, pl.ds(odd, 40, stride=2), :] for half in range(2)], 1)
            for odd in range(2)
        ],
        0,
    ).astype(BF)
    first = lax.broadcasted_iota(jnp.int32, (40, 128), 1) < 64

    def encode(g, carry):
        begin = pl.multiple_of(g * group, 8)
        cols = []
        for k in range(4):
            one = flat[pl.ds(begin + 2 * k, 40, stride=8), :]
            two = flat[pl.ds(begin + 2 * k + 1, 40, stride=8), :]
            even = jnp.where(first, one, pltpu.roll(two, 64, 1))
            odd = jnp.where(first, pltpu.roll(one, 64, 1), two)
            cols.append(jnp.concatenate([even, odd], 0))
        x = jnp.concatenate(cols, 1).astype(BF)
        v = lax.dot_general(x, weight, TN, preferred_element_type=F32)
        v = silu_twice(v).astype(BF).astype(F32)
        enc_ref[pl.ds(g * 8, 8)] = v.reshape(8, cells, 256)
        return carry

    lax.fori_loop(0, count // 8, encode, 0, unroll=True)

    enc_ref[pl.ds(count, 8)] = enc_ref[pl.ds(0, 8)]

    def window(k, carry):
        nest = k // 2
        part = k % 2
        anchor = anchor_ref[nest, tile]
        begin = anchor + (band - anchor + 512) % 8 + part * 48
        row = (begin % 512) // 8
        total = enc_ref[row]
        for m in range(1, 6):
            total = total + enc_ref[row + m]
        out_ref[nest, pl.ds(pl.multiple_of(part * cells, cells), cells), :] = total.astype(BF)
        return carry

    lax.fori_loop(0, 16, window, 0, unroll=4)


def pair_weight(w, a):
    zero = jnp.zeros_like(w(a, 0))
    own = jnp.concatenate(
        [jnp.concatenate([w(a, 1), w(a, 2)], 1), jnp.concatenate([w(a, 0), w(a, 1)], 1)], 0
    )
    rim = jnp.concatenate(
        [jnp.concatenate([w(a, 0), zero], 1), jnp.concatenate([zero, w(a, 2)], 1)], 0
    )
    return own, rim


def tall(ref, a, b):
    if not 0 <= b <= 2:
        return jnp.zeros((8, 128), F32)
    return jnp.concatenate([ref[3 * a + b].astype(F32), jnp.zeros((4, 128), F32)], 0)


def form_in(w, out):
    taps = [jnp.concatenate([tall(w, a, q - p) for p in range(2)], 1) for a in range(3) for q in range(4)]
    out[...] = (0.5 * jnp.concatenate(taps, 0)).astype(BF)


def form_out(w, out):
    taps = [
        jnp.concatenate([tall(w, a, q - p) for q in (1, 2, 0, 3)], 1) for a in range(3) for p in range(2)
    ]
    out[...] = jnp.concatenate(taps, 0).astype(BF)


def form_pairs(w, chans, out):
    half = jnp.asarray(0.5, BF)
    for a in range(3):
        own, rim = pair_weight(lambda i, b: w[3 * i + b][:, 0:chans] * half, a)
        out[:, 512 * a : 512 * a + 256] = own
        out[:, 512 * a + 256 : 512 * a + 512] = rim


def form_down(w, out):
    half = jnp.asarray(0.5, BF)
    for a in range(3):
        out[:, 256 * a : 256 * a + 128] = w[3 * a + 1] * half
        out[:, 256 * a + 128 : 256 * a + 256] = w[3 * a + 2] * half
        out[:, 768 + 128 * a : 896 + 128 * a] = w[3 * a] * half


def form_mid(w, out):
    half = jnp.asarray(0.5, BF)
    for a in range(3):
        for b in range(3):
            out[:, 768 * a + 256 * b : 768 * a + 256 * b + 256] = w[3 * a + b] * half


def form_up(w, even, odd):
    def up(a, b):
        return 0.5 * w[3 * a + b][:, 128:384].astype(F32)

    for out, sets in ((even, ((0,), (1, 2))), (odd, ((0, 1), (2,)))):
        for k, taps in enumerate(sets):
            col = [sum(up(a, b) for a in taps) for b in range(3)]
            zero = jnp.zeros_like(col[0])
            out[:, 768 * k : 768 * k + 256] = jnp.concatenate([col[0], zero], 0).astype(BF)
            out[:, 768 * k + 256 : 768 * k + 512] = jnp.concatenate(
                [col[1] + col[2], col[0] + col[1]], 0
            ).astype(BF)
            out[:, 768 * k + 512 : 768 * k + 768] = jnp.concatenate([zero, col[2]], 0).astype(BF)


def parts(total, most):
    count = -(-total // most)
    cuts = [total * i // count for i in range(count + 1)]
    return [(a, b - a) for a, b in zip(cuts, cuts[1:])]


class Field:
    def __init__(self, width, masks):
        self.tile = lax.axis_index("tile")
        self.masks = masks
        lane = lax.broadcasted_iota(jnp.int32, (HALF, 256), 1)
        pair = lax.broadcasted_iota(jnp.int32, (HALF, 256), 0)
        masks[0] = jnp.zeros((HALF, 256), F32)
        masks[1] = (2 * pair + lane // 128 < width).astype(F32)
        masks[2] = (2 * pair < width).astype(F32)
        self.natural = (lax.broadcasted_iota(jnp.int32, (4, 256), 1) < width).astype(F32)

    def fine_ok(self, rho):
        row = self.tile * 4 + rho
        return jnp.logical_and(row >= 0, row < ROWS).astype(jnp.int32)

    def half_ok(self, h):
        row = self.tile * 2 + h
        return jnp.logical_and(row >= 0, row < ROWS // 2).astype(jnp.int32)

    def keep_pairs(self, y, center, rim, at, rho):
        y = y * self.masks[self.fine_ok(rho)]
        center[at] = y.astype(BF)
        rim[at] = jnp.concatenate([slide(y[:, 128:], 1), slide(y[:, :128], -1)], 1).astype(BF)

    def keep_half(self, y, center, left, right, at, h):
        y = y * self.masks[2 * self.half_ok(h)]
        center[at] = y.astype(BF)
        left[at] = slide(y, 1).astype(BF)
        right[at] = slide(y, -1).astype(BF)


def embedding(w_sigma, now):
    return jnp.concatenate([w_sigma[...], w_sigma[...]], 1) * jnp.log(now)


def slide(x, by):
    x = pltpu.roll(x, by % HALF, 0)
    where = lax.broadcasted_iota(jnp.int32, (8, x.shape[1]), 0)
    if by == 1:
        return jnp.concatenate([jnp.where(where == 0, 0.0, x[:8]), x[8:]], 0)
    return jnp.concatenate([x[: HALF - 8], jnp.where(where == 7, 0.0, x[HALF - 8 :])], 0)


def stacked(ref, at, n, step=1):
    return jnp.concatenate([ref[at + step * k] for k in range(n)], 0)


def encoder(field, rows, blocks, scaled, spread, bias, f_in, f_enc, firstc, firste, secondc, seconde):
    n_state = rows["scaled"][1]
    first_lo, n_first = rows["first"]
    second_lo, n_second = rows["second"]
    col = lax.broadcasted_iota(jnp.int32, (256, 512), 0)
    place = lax.broadcasted_iota(jnp.int32, (256, 512), 1)
    pick = (col == 2 * (place % 128) + place // 128 - 1).astype(F32).astype(BF)
    spread[0 : 8 * n_state, :] = jnp.dot(scaled[...].astype(BF), pick, preferred_element_type=F32)
    for at, n in parts(n_first, blocks[0]):
        cols = [
            jnp.concatenate(
                [
                    spread[8 * (k + a) : 8 * (k + a) + 8, 128 * q : 128 * q + 128]
                    for a in range(3)
                    for q in range(4)
                ],
                0,
            )
            for k in range(at, at + n)
        ]
        x = jnp.concatenate(cols, 1).astype(BF)
        y = lax.dot_general(x, f_in[...], TN, preferred_element_type=F32)
        for k in range(n):
            part = silu_twice(y[k * HALF : (k + 1) * HALF] + bias)
            field.keep_pairs(part, firstc, firste, at + k, first_lo + at + k)

    for at, n in parts(n_second, blocks[1]):
        x = jnp.concatenate([stacked(ref, at + a, n) for a in range(3) for ref in (firstc, firste)], 1)
        y = dot_nt(x, f_enc[...])
        for k in range(n):
            part = silu_twice(y[k * HALF : (k + 1) * HALF])
            field.keep_pairs(part, secondc, seconde, at + k, second_lo + at + k)

def step_kernel(
    step, width_ref, sigma_ref, own, halo, conds, weights, state_ref, scaled_ref,
    state, spread, firstc, firste, secondc, seconde, third, thirdl, thirdr, fourth, fourthl, fourthr,
    fifthc, fifthe, prod, picked, masks,
    f_in, f_out, f_enc, f_down, f_mid, f_dec, f_even, f_odd,
):
    w_sigma, w_in, w_out, w_enc, w_down, w_mid, w_dec = weights
    field = Field(width_ref[0], masks)
    form_in(w_in, f_in)
    form_out(w_out, f_out)
    form_pairs(w_enc, 128, f_enc)
    form_down(w_down, f_down)
    form_mid(w_mid, f_mid)
    form_pairs(w_dec, 128, f_dec)
    form_up(w_dec, f_even, f_odd)
    rows = STEP_ROWS[step]
    sigma, scale, keep, mix, move = levels(sigma_ref, step)
    scaled_lo, n_scaled = rows["scaled"]
    second_lo = rows["second"][0]
    third_lo, n_third = rows["third"]
    fourth_lo, n_fourth = rows["fourth"]
    fifth_lo, n_fifth = rows["fifth"]
    n_out = rows["out"][1]

    empty = jnp.zeros((4, 256), F32)
    pieces = [(rho, ref[begin : begin + 4 * n, :].astype(F32), n) for rho, n, ref, begin in halo]
    pieces += [(rho, (value * scale).astype(BF).astype(F32), n) for rho, value, n in own]
    for lo, value, n in pieces:
        for r in range(n):
            rho = lo + r
            if scaled_lo <= rho < scaled_lo + n_scaled:
                row = jnp.concatenate([value[4 * r : 4 * r + 4], empty], 0)
                at = 8 * (rho - scaled_lo)
                state[at : at + 8, :] = row * field.fine_ok(rho).astype(F32)
    weave_j = lax.broadcasted_iota(jnp.int32, (256, 256), 0)
    weave_c = lax.broadcasted_iota(jnp.int32, (256, 256), 1)
    weave = (weave_c == 2 * (weave_j % HALF) + weave_j // HALF).astype(F32).astype(BF)
    repeat = (
        lax.broadcasted_iota(jnp.int32, (HALF, 64), 0) // 2 == lax.broadcasted_iota(jnp.int32, (HALF, 64), 1)
    ).astype(F32)
    repeat = (0.5 * repeat).astype(BF)
    bias = 0.5 * embedding(w_sigma, sigma)
    encoder(field, rows, BLOCKS[step], state, spread, bias, f_in, f_enc, firstc, firste, secondc, seconde)

    for at, n in parts(n_third, BLOCKS[step][2]):
        begin = 2 * (third_lo + at) - 1 - second_lo
        x = jnp.concatenate(
            [stacked(secondc, begin + a, n, 2) for a in range(3)]
            + [
                jnp.concatenate([seconde[begin + a + 2 * k][:, :128] for k in range(n)], 0)
                for a in range(3)
            ],
            1,
        )
        y = dot_nt(x, f_down[...])
        for k in range(n):
            ref, r = conds[at + k]
            add = jnp.dot(repeat, ref[64 * r : 64 * r + 64, :], preferred_element_type=F32)
            part = silu_twice(y[k * HALF : (k + 1) * HALF] + add)
            field.keep_half(part, third, thirdl, thirdr, at + k, third_lo + at + k)

    for at, n in parts(n_fourth, BLOCKS[step][3]):
        x = jnp.concatenate(
            [stacked(ref, at + a, n) for a in range(3) for ref in (thirdl, third, thirdr)], 1
        )
        y = dot_nt(x, f_mid[...])
        for k in range(n):
            part = silu_twice(y[k * HALF : (k + 1) * HALF])
            field.keep_half(part, fourth, fourthl, fourthr, at + k, fourth_lo + at + k)

    for parity in range(2):
        for cut, n in parts((n_fifth - parity + 1) // 2, BLOCKS[step][4]):
            at = parity + 2 * cut
            rho = fifth_lo + at
            odd = rho % 2
            begin = rho - 1 - second_lo
            h = (rho - odd) // 2 - fourth_lo - (0 if odd else 1)
            x = jnp.concatenate(
                [stacked(ref, begin + a, n, 2) for a in range(3) for ref in (secondc, seconde)], 1
            )
            z = jnp.concatenate(
                [stacked(ref, h + a, n) for a in range(2) for ref in (fourthl, fourth, fourthr)], 1
            )
            y = dot_nt(x, f_dec[...]) + dot_nt(z, (f_odd if odd else f_even)[...])
            for k in range(n):
                part = silu_twice(y[k * HALF : (k + 1) * HALF])
                field.keep_pairs(part, fifthc, fifthe, at + 2 * k, fifth_lo + at + 2 * k)

    for at, n in parts(n_fifth, BLOCKS[step][5]):
        x = jnp.concatenate([stacked(fifthc, at, n), stacked(fifthe, at, n)], 1)
        prod[:, at * HALF : (at + n) * HALF] = dot_nt(f_out[...], x)
    for k in range(n_out):
        for p in range(2):
            picked[8 * k : 8 * k + 8, HALF * p : HALF * p + HALF] = sum(
                prod[16 * a + 8 * p : 16 * a + 8 * p + 8, (k + a) * HALF : (k + a + 1) * HALF]
                for a in range(3)
            )
    value = picked[0 : 8 * n_out, :]
    high = value.astype(BF)
    low = (value - high.astype(F32)).astype(BF)
    net = jnp.dot(high, weave, preferred_element_type=F32) + jnp.dot(low, weave, preferred_element_type=F32)
    states = jnp.concatenate([value for _, value, _ in own], 0)
    if step == 0:
        next_scale = levels(sigma_ref, 1)[1]
    for k in range(n_out):
        now = states[4 * k : 4 * k + 4]
        denoised = keep * now + mix * net[8 * k : 8 * k + 4]
        now = (now + move * (now - denoised)) * (field.natural * field.fine_ok(k).astype(F32))
        if step == 0:
            state_ref[4 * k : 4 * k + 4, :] = now
            scaled_ref[4 * k : 4 * k + 4, :] = (now * next_scale).astype(BF)
        else:
            state_ref[:, k, :] = now


def pack_kernel(arrived, above, scaled, own_parts, below, cond, to_below, to_above):
    for at in range(0, 128, 32):
        total = arrived[0, at : at + 32, :].astype(F32)
        for k in range(1, 8):
            total = total + arrived[k, at : at + 32, :].astype(F32)
        total = (total * (1.0 / math.sqrt(K // 2))).astype(BF)
        for ref in (cond, to_below, to_above):
            ref[at : at + 32, :] = total
    to_below[128:144, :] = above[...]
    to_below[144:160, :] = scaled[...]
    to_above[128:160, :] = own_parts[...]
    to_above[160:176, :] = below[...]


def pack_call(*args):
    return pl.pallas_call(
        pack_kernel,
        out_shape=[jax.ShapeDtypeStruct((n, 256), BF) for n in (128, 160, 176)],
        in_specs=[VMEM] * 5,
        out_specs=[VMEM] * 3,
        compiler_params=limit(4),
        cost_estimate=cost(4),
        name="pack",
    )(*args)


def turn(x, by):
    n = lax.axis_size("tile")
    return lax.ppermute(x, "tile", [(i, (i + by) % n) for i in range(n)])


VMEM = pl.BlockSpec(memory_space=pltpu.VMEM)
SMEM = pl.BlockSpec(memory_space=pltpu.SMEM)


LIMIT = 20


def limit(mib):
    return pltpu.CompilerParams(vmem_limit_bytes=mib << 20)


def rowbuf(n):
    return pltpu.VMEM((n, HALF, 256), BF)


def cost(passes):
    return pl.CostEstimate(flops=passes * 128 * 65536 * 2, bytes_accessed=1 << 20, transcendentals=0)


def step_call(step, arrays, width, sigmas, weights):
    rows = STEP_ROWS[step]
    n_arrays, n_weights = len(arrays), len(weights)
    n_out = rows["out"][1]
    if step == 0:
        outs = [jax.ShapeDtypeStruct((4 * n_out, 256), F32), jax.ShapeDtypeStruct((4 * n_out, 256), BF)]
    else:
        outs = [jax.ShapeDtypeStruct((4, 4, 256), F32)]

    def kernel(width_ref, sigma_ref, *refs):
        held, refs = refs[:n_arrays], refs[n_arrays:]
        weight_refs, refs = refs[:n_weights], refs[n_weights:]
        out_refs, refs = list(refs[: len(outs)]), refs[len(outs) :]
        near_up, near_down, cond, cond_far = held[:4]
        conds = [(ref, r) for ref in (near_up, cond, near_down, cond_far) for r in range(2)]
        if step == 0:
            own_ref, two_down = held[4:]
            below = near_down[128:144, :].astype(F32) + near_down[144:160, :].astype(F32)
            own = [(0, own_ref[...], 4), (4, below, 4)]
            halo = [(-8, 8, near_up, 128), (8, 4, two_down, 0), (12, 4, near_down, 160)]
        else:
            own_ref, up, down, top = held[4:]
            own = [(0, own_ref[...], 8)]
            second = lax.axis_index("tile") == 1
            near = jnp.where(second, top[...].astype(F32), up[16:32, :].astype(F32))
            halo = [(-8, 4, up, 0), (-4, 4, near, 0), (8, 4, down, 0)]
        step_kernel(
            step, width_ref, sigma_ref, own, halo, conds, weight_refs, *(out_refs + [None])[:2], *refs
        )

    return pl.pallas_call(
        kernel,
        out_shape=outs,
        in_specs=[SMEM, SMEM] + [VMEM] * (n_arrays + n_weights),
        out_specs=[VMEM] * len(outs),
        scratch_shapes=[
            pltpu.VMEM((rows["scaled"][1] * 8, 256), F32), pltpu.VMEM((rows["scaled"][1] * 8, 512), F32),
            *[
                rowbuf(rows[name][1])
                for name, n in (("first", 2), ("second", 2), ("third", 3), ("fourth", 3), ("fifth", 2))
                for _ in range(n)
            ],
            pltpu.VMEM((48, rows["fifth"][1] * HALF), F32),
            pltpu.VMEM((8 * n_out, 256), F32),
            pltpu.VMEM((3, HALF, 256), F32),
            *[
                pltpu.VMEM(shape, BF)
                for shape in (
                    (96, 256), (48, 512), (256, 1536), (256, 1152), (256, 2304),
                    (256, 1536), (256, 1536), (256, 1536),
                )
            ],
        ],
        compiler_params=limit(LIMIT),
        cost_estimate=cost(300),
        name="step" + str(step),
    )(width, sigmas, *arrays, *weights)


def encode_call(block_anchor, nest_width, sigmas, coarse_blocks, w_context, noise):
    chans = w_context.shape[1]
    cells = coarse_blocks.shape[1] // chans
    count = coarse_blocks.shape[0]
    tiles = coarse_blocks.shape[1] // 128
    return pl.pallas_call(
        encode_kernel,
        out_shape=[
            jax.ShapeDtypeStruct((8, 2 * cells, 256), BF),
            jax.ShapeDtypeStruct((16, 256), F32),
            jax.ShapeDtypeStruct((16, 256), BF),
            jax.ShapeDtypeStruct((32, 256), BF),
        ],
        in_specs=[SMEM, SMEM, SMEM, VMEM, VMEM, VMEM],
        out_specs=[VMEM] * 4,
        scratch_shapes=[
            pltpu.VMEM((count + 8, cells, 256), F32),
            pltpu.VMEM((count * tiles + 64, 128), F32),
            pltpu.VMEM((2, 80, 128), F32),
        ],
        compiler_params=limit(56),
        cost_estimate=cost(100),
        name="encode",
    )(block_anchor, nest_width, sigmas, coarse_blocks, w_context.T, noise)


def per_device(
    coarse_blocks, block_anchor, nest_width, sigmas, noise,
    w_context, w_in, w_sigma, w_enc, w_down, w_mid, w_dec, w_out,
):
    partial, state, scaled, own_parts = encode_call(
        block_anchor, nest_width, sigmas, coarse_blocks, w_context, noise[0]
    )
    arrived = lax.all_to_all(partial, "band", 0, 0, tiled=True)

    one_up = turn(scaled, 1)
    two_down = turn(scaled, -2)
    arrived, one_up, two_down = lax.optimization_barrier((arrived, one_up, two_down))

    cond, to_below, to_above = pack_call(arrived, one_up, scaled, own_parts, two_down)
    near_up = turn(to_below, 1)
    near_down = turn(to_above, -1)
    cond_far = turn(cond, -2)
    weights = (w_sigma.reshape(1, -1), w_in.transpose(0, 2, 1), w_out, w_enc, w_down, w_mid, w_dec)
    conds = (near_up, near_down, cond, cond_far)
    state, scaled = step_call(0, (*conds, state, two_down), nest_width, sigmas, weights)
    up = turn(scaled, 2)
    down = turn(scaled[16:], -1)
    top = lax.ppermute(scaled[:16], "tile", [(0, 1)])
    (out,) = step_call(1, (*conds, state, up, down, top), nest_width, sigmas, weights)
    return out[None]


def solution(mesh):
    return jax.shard_map(
        per_device,
        mesh=mesh,
        in_specs=(
            P("band", None), P(), P("band"), P(), P("band", None, "tile", None),
            P(), P(), P(), P(), P(), P(), P(), P(),
        ),
        out_specs=P("band", None, "tile", None),
        check_vma=False,
    )
```

```python
import functools
import math

import jax
import jax.numpy as jnp
from jax import lax
from jax.experimental import pallas as pl
from jax.experimental.pallas import tpu as pltpu
from jax.sharding import PartitionSpec as P

K = 96
SIGMA_DATA = 0.5
BF = jnp.bfloat16
F32 = jnp.float32
HALF = 128
ROWS = 256
NT = (((1,), (1,)), ((), ()))
TN = (((0,), (0,)), ((), ()))

BLOCKS = ((5, 5, 3, 2, 5, 6), (4, 4, 4, 3, 3, 5))
FIELDS = ("scaled", "first", "second", "third", "fourth", "fifth", "out")
STEP_ROWS = (
    dict(zip(FIELDS, ((-7, 21), (-6, 19), (-5, 17), (-2, 8), (-1, 6), (-1, 10), (0, 8)))),
    dict(zip(FIELDS, ((-7, 17), (-6, 15), (-5, 13), (-2, 6), (-1, 4), (-1, 6), (0, 4)))),
)


def silu_twice(h):
    return h + h * jnp.tanh(h)


def dot_nt(a, b):
    return lax.dot_general(a, b, NT, preferred_element_type=F32)


def levels(sigma_ref, step):
    now = jnp.full((1, 256), sigma_ref[step], F32)
    after = jnp.full((1, 256), sigma_ref[step + 1], F32)
    var = now * now + SIGMA_DATA * SIGMA_DATA
    root = jnp.sqrt(var)
    return now, 1.0 / root, SIGMA_DATA * SIGMA_DATA / var, now * SIGMA_DATA / root, (after - now) / now


def encode_kernel(
    anchor_ref, width_ref, sigma_ref, blocks_ref, w_ref, noise_ref, out_ref, state_ref, scaled_ref, parts_ref, enc_ref, flat, wide
):
    band = lax.axis_index("band")
    tile = lax.axis_index("tile")
    count = blocks_ref.shape[0]
    cells = enc_ref.shape[1]
    chans = w_ref.shape[0]
    tiles = blocks_ref.shape[1] // 128
    group = 8 * tiles

    flat[count * tiles :, :] = jnp.zeros((flat.shape[0] - count * tiles, 128), F32)
    for g in range(count // 16):
        for t in range(tiles):
            v = blocks_ref[16 * g : 16 * g + 16, 128 * t : 128 * t + 128].astype(F32)
            flat[2 * g * group + 8 * t : 2 * g * group + 8 * t + 8, :] = v[:8]
            flat[(2 * g + 1) * group + 8 * t : (2 * g + 1) * group + 8 * t + 8, :] = v[8:]

    sigma, scale = levels(sigma_ref, 0)[:2]
    natural = (lax.broadcasted_iota(jnp.int32, (4, 256), 1) < width_ref[0]).astype(F32)
    for r in range(4):
        row = sigma * noise_ref[:, r, :] * natural
        state_ref[4 * r : 4 * r + 4, :] = row
        scaled_ref[4 * r : 4 * r + 4, :] = (row * scale).astype(BF)
    state = state_ref[...]
    high = state.astype(BF)
    parts_ref[0:16, :] = high
    parts_ref[16:32, :] = (state - high.astype(F32)).astype(BF)

    w = 0.5 * w_ref[...].astype(F32)
    for half in range(2):
        wide[half, 0:chans, :] = w[:, 128 * half : 128 * half + 128]
        wide[half, chans:80, :] = jnp.zeros((80 - chans, 128), F32)
    weight = jnp.concatenate(
        [
            jnp.concatenate([wide[half, pl.ds(odd, 40, stride=2), :] for half in range(2)], 1)
            for odd in range(2)
        ],
        0,
    ).astype(BF)
    first = lax.broadcasted_iota(jnp.int32, (40, 128), 1) < 64

    def encode(g, carry):
        begin = pl.multiple_of(g * group, 8)
        cols = []
        for k in range(4):
            one = flat[pl.ds(begin + 2 * k, 40, stride=8), :]
            two = flat[pl.ds(begin + 2 * k + 1, 40, stride=8), :]
            even = jnp.where(first, one, pltpu.roll(two, 64, 1))
            odd = jnp.where(first, pltpu.roll(one, 64, 1), two)
            cols.append(jnp.concatenate([even, odd], 0))
        x = jnp.concatenate(cols, 1).astype(BF)
        v = lax.dot_general(x, weight, TN, preferred_element_type=F32)
        v = silu_twice(v).astype(BF).astype(F32)
        enc_ref[pl.ds(g * 8, 8)] = v.reshape(8, cells, 256)
        return carry

    lax.fori_loop(0, count // 8, encode, 0, unroll=True)

    enc_ref[pl.ds(count, 8)] = enc_ref[pl.ds(0, 8)]

    def window(k, carry):
        nest = k // 2
        part = k % 2
        anchor = anchor_ref[nest, tile]
        begin = anchor + (band - anchor + 512) % 8 + part * 48
        row = (begin % 512) // 8
        total = enc_ref[row]
        for m in range(1, 6):
            total = total + enc_ref[row + m]
        out_ref[nest, pl.ds(pl.multiple_of(part * cells, cells), cells), :] = total.astype(BF)
        return carry

    lax.fori_loop(0, 16, window, 0, unroll=4)


def pair_weight(w, a):
    zero = jnp.zeros_like(w(a, 0))
    own = jnp.concatenate(
        [jnp.concatenate([w(a, 1), w(a, 2)], 1), jnp.concatenate([w(a, 0), w(a, 1)], 1)], 0
    )
    rim = jnp.concatenate(
        [jnp.concatenate([w(a, 0), zero], 1), jnp.concatenate([zero, w(a, 2)], 1)], 0
    )
    return own, rim


def tall(ref, a, b):
    if not 0 <= b <= 2:
        return jnp.zeros((8, 128), F32)
    return jnp.concatenate([ref[3 * a + b].astype(F32), jnp.zeros((4, 128), F32)], 0)


def form_in(w, out):
    taps = [jnp.concatenate([tall(w, a, q - p) for p in range(2)], 1) for a in range(3) for q in range(4)]
    out[...] = (0.5 * jnp.concatenate(taps, 0)).astype(BF)


def form_out(w, out):
    taps = [
        jnp.concatenate([tall(w, a, q - p) for q in (1, 2, 0, 3)], 1) for a in range(3) for p in range(2)
    ]
    out[...] = jnp.concatenate(taps, 0).astype(BF)


def form_pairs(w, chans, out):
    half = jnp.asarray(0.5, BF)
    for a in range(3):
        own, rim = pair_weight(lambda i, b: w[3 * i + b][:, 0:chans] * half, a)
        out[:, 512 * a : 512 * a + 256] = own
        out[:, 512 * a + 256 : 512 * a + 512] = rim


def form_down(w, out):
    half = jnp.asarray(0.5, BF)
    for a in range(3):
        out[:, 256 * a : 256 * a + 128] = w[3 * a + 1] * half
        out[:, 256 * a + 128 : 256 * a + 256] = w[3 * a + 2] * half
        out[:, 768 + 128 * a : 896 + 128 * a] = w[3 * a] * half


def form_mid(w, out):
    half = jnp.asarray(0.5, BF)
    for a in range(3):
        for b in range(3):
            out[:, 768 * a + 256 * b : 768 * a + 256 * b + 256] = w[3 * a + b] * half


def form_up(w, even, odd):
    def up(a, b):
        return 0.5 * w[3 * a + b][:, 128:384].astype(F32)

    for out, sets in ((even, ((0,), (1, 2))), (odd, ((0, 1), (2,)))):
        for k, taps in enumerate(sets):
            col = [sum(up(a, b) for a in taps) for b in range(3)]
            zero = jnp.zeros_like(col[0])
            out[:, 768 * k : 768 * k + 256] = jnp.concatenate([col[0], zero], 0).astype(BF)
            out[:, 768 * k + 256 : 768 * k + 512] = jnp.concatenate(
                [col[1] + col[2], col[0] + col[1]], 0
            ).astype(BF)
            out[:, 768 * k + 512 : 768 * k + 768] = jnp.concatenate([zero, col[2]], 0).astype(BF)


def parts(total, most):
    count = -(-total // most)
    cuts = [total * i // count for i in range(count + 1)]
    return [(a, b - a) for a, b in zip(cuts, cuts[1:])]


class Field:
    def __init__(self, width, masks):
        self.tile = lax.axis_index("tile")
        self.masks = masks
        lane = lax.broadcasted_iota(jnp.int32, (HALF, 256), 1)
        pair = lax.broadcasted_iota(jnp.int32, (HALF, 256), 0)
        masks[0] = jnp.zeros((HALF, 256), F32)
        masks[1] = (2 * pair + lane // 128 < width).astype(F32)
        masks[2] = (2 * pair < width).astype(F32)
        self.natural = (lax.broadcasted_iota(jnp.int32, (4, 256), 1) < width).astype(F32)

    def fine_ok(self, rho):
        row = self.tile * 4 + rho
        return jnp.logical_and(row >= 0, row < ROWS).astype(jnp.int32)

    def half_ok(self, h):
        row = self.tile * 2 + h
        return jnp.logical_and(row >= 0, row < ROWS // 2).astype(jnp.int32)

    def keep_pairs(self, y, center, rim, at, rho):
        y = y * self.masks[self.fine_ok(rho)]
        center[at] = y.astype(BF)
        rim[at] = jnp.concatenate([slide(y[:, 128:], 1), slide(y[:, :128], -1)], 1).astype(BF)

    def keep_half(self, y, center, left, right, at, h):
        y = y * self.masks[2 * self.half_ok(h)]
        center[at] = y.astype(BF)
        left[at] = slide(y, 1).astype(BF)
        right[at] = slide(y, -1).astype(BF)


def embedding(w_sigma, now):
    return jnp.concatenate([w_sigma[...], w_sigma[...]], 1) * jnp.log(now)


def slide(x, by):
    x = pltpu.roll(x, by % HALF, 0)
    where = lax.broadcasted_iota(jnp.int32, (8, x.shape[1]), 0)
    if by == 1:
        return jnp.concatenate([jnp.where(where == 0, 0.0, x[:8]), x[8:]], 0)
    return jnp.concatenate([x[: HALF - 8], jnp.where(where == 7, 0.0, x[HALF - 8 :])], 0)


def stacked(ref, at, n, step=1):
    return jnp.concatenate([ref[at + step * k] for k in range(n)], 0)


def encoder(field, rows, blocks, scaled, spread, bias, f_in, f_enc, firstc, firste, secondc, seconde):
    n_state = rows["scaled"][1]
    first_lo, n_first = rows["first"]
    second_lo, n_second = rows["second"]
    col = lax.broadcasted_iota(jnp.int32, (256, 512), 0)
    place = lax.broadcasted_iota(jnp.int32, (256, 512), 1)
    pick = (col == 2 * (place % 128) + place // 128 - 1).astype(F32).astype(BF)
    spread[0 : 8 * n_state, :] = jnp.dot(scaled[...].astype(BF), pick, preferred_element_type=F32)
    for at, n in parts(n_first, blocks[0]):
        cols = [
            jnp.concatenate(
                [
                    spread[8 * (k + a) : 8 * (k + a) + 8, 128 * q : 128 * q + 128]
                    for a in range(3)
                    for q in range(4)
                ],
                0,
            )
            for k in range(at, at + n)
        ]
        x = jnp.concatenate(cols, 1).astype(BF)
        y = lax.dot_general(x, f_in[...], TN, preferred_element_type=F32)
        for k in range(n):
            part = silu_twice(y[k * HALF : (k + 1) * HALF] + bias)
            field.keep_pairs(part, firstc, firste, at + k, first_lo + at + k)

    for at, n in parts(n_second, blocks[1]):
        x = jnp.concatenate([stacked(ref, at + a, n) for a in range(3) for ref in (firstc, firste)], 1)
        y = dot_nt(x, f_enc[...])
        for k in range(n):
            part = silu_twice(y[k * HALF : (k + 1) * HALF])
            field.keep_pairs(part, secondc, seconde, at + k, second_lo + at + k)

def step_kernel(
    step, width_ref, sigma_ref, own, halo, conds, weights, state_ref, scaled_ref,
    state, spread, firstc, firste, secondc, seconde, third, thirdl, thirdr, fourth, fourthl, fourthr,
    fifthc, fifthe, prod, picked, masks,
    f_in, f_out, f_enc, f_down, f_mid, f_dec, f_even, f_odd,
):
    w_sigma, w_in, w_out, w_enc, w_down, w_mid, w_dec = weights
    field = Field(width_ref[0], masks)
    form_in(w_in, f_in)
    form_out(w_out, f_out)
    form_pairs(w_enc, 128, f_enc)
    form_down(w_down, f_down)
    form_mid(w_mid, f_mid)
    form_pairs(w_dec, 128, f_dec)
    form_up(w_dec, f_even, f_odd)
    rows = STEP_ROWS[step]
    sigma, scale, keep, mix, move = levels(sigma_ref, step)
    scaled_lo, n_scaled = rows["scaled"]
    second_lo = rows["second"][0]
    third_lo, n_third = rows["third"]
    fourth_lo, n_fourth = rows["fourth"]
    fifth_lo, n_fifth = rows["fifth"]
    n_out = rows["out"][1]

    empty = jnp.zeros((4, 256), F32)
    pieces = [(rho, ref[begin : begin + 4 * n, :].astype(F32), n) for rho, n, ref, begin in halo]
    pieces += [(rho, (value * scale).astype(BF).astype(F32), n) for rho, value, n in own]
    for lo, value, n in pieces:
        for r in range(n):
            rho = lo + r
            if scaled_lo <= rho < scaled_lo + n_scaled:
                row = jnp.concatenate([value[4 * r : 4 * r + 4], empty], 0)
                at = 8 * (rho - scaled_lo)
                state[at : at + 8, :] = row * field.fine_ok(rho).astype(F32)
    weave_j = lax.broadcasted_iota(jnp.int32, (256, 256), 0)
    weave_c = lax.broadcasted_iota(jnp.int32, (256, 256), 1)
    weave = (weave_c == 2 * (weave_j % HALF) + weave_j // HALF).astype(F32).astype(BF)
    repeat = (
        lax.broadcasted_iota(jnp.int32, (HALF, 64), 0) // 2 == lax.broadcasted_iota(jnp.int32, (HALF, 64), 1)
    ).astype(F32)
    repeat = (0.5 * repeat).astype(BF)
    bias = 0.5 * embedding(w_sigma, sigma)
    encoder(field, rows, BLOCKS[step], state, spread, bias, f_in, f_enc, firstc, firste, secondc, seconde)

    for at, n in parts(n_third, BLOCKS[step][2]):
        begin = 2 * (third_lo + at) - 1 - second_lo
        x = jnp.concatenate(
            [stacked(secondc, begin + a, n, 2) for a in range(3)]
            + [
                jnp.concatenate([seconde[begin + a + 2 * k][:, :128] for k in range(n)], 0)
                for a in range(3)
            ],
            1,
        )
        y = dot_nt(x, f_down[...])
        for k in range(n):
            ref, r = conds[at + k]
            add = jnp.dot(repeat, ref[64 * r : 64 * r + 64, :], preferred_element_type=F32)
            part = silu_twice(y[k * HALF : (k + 1) * HALF] + add)
            field.keep_half(part, third, thirdl, thirdr, at + k, third_lo + at + k)

    for at, n in parts(n_fourth, BLOCKS[step][3]):
        x = jnp.concatenate(
            [stacked(ref, at + a, n) for a in range(3) for ref in (thirdl, third, thirdr)], 1
        )
        y = dot_nt(x, f_mid[...])
        for k in range(n):
            part = silu_twice(y[k * HALF : (k + 1) * HALF])
            field.keep_half(part, fourth, fourthl, fourthr, at + k, fourth_lo + at + k)

    for parity in range(2):
        for cut, n in parts((n_fifth - parity + 1) // 2, BLOCKS[step][4]):
            at = parity + 2 * cut
            rho = fifth_lo + at
            odd = rho % 2
            begin = rho - 1 - second_lo
            h = (rho - odd) // 2 - fourth_lo - (0 if odd else 1)
            x = jnp.concatenate(
                [stacked(ref, begin + a, n, 2) for a in range(3) for ref in (secondc, seconde)], 1
            )
            z = jnp.concatenate(
                [stacked(ref, h + a, n) for a in range(2) for ref in (fourthl, fourth, fourthr)], 1
            )
            y = dot_nt(x, f_dec[...]) + dot_nt(z, (f_odd if odd else f_even)[...])
            for k in range(n):
                part = silu_twice(y[k * HALF : (k + 1) * HALF])
                field.keep_pairs(part, fifthc, fifthe, at + 2 * k, fifth_lo + at + 2 * k)

    for at, n in parts(n_fifth, BLOCKS[step][5]):
        x = jnp.concatenate([stacked(fifthc, at, n), stacked(fifthe, at, n)], 1)
        prod[:, at * HALF : (at + n) * HALF] = dot_nt(f_out[...], x)
    for k in range(n_out):
        for p in range(2):
            picked[8 * k : 8 * k + 8, HALF * p : HALF * p + HALF] = sum(
                prod[16 * a + 8 * p : 16 * a + 8 * p + 8, (k + a) * HALF : (k + a + 1) * HALF]
                for a in range(3)
            )
    value = picked[0 : 8 * n_out, :]
    high = value.astype(BF)
    low = (value - high.astype(F32)).astype(BF)
    net = jnp.dot(high, weave, preferred_element_type=F32) + jnp.dot(low, weave, preferred_element_type=F32)
    states = jnp.concatenate([value for _, value, _ in own], 0)
    if step == 0:
        next_scale = levels(sigma_ref, 1)[1]
    for k in range(n_out):
        now = states[4 * k : 4 * k + 4]
        denoised = keep * now + mix * net[8 * k : 8 * k + 4]
        now = (now + move * (now - denoised)) * (field.natural * field.fine_ok(k).astype(F32))
        if step == 0:
            state_ref[4 * k : 4 * k + 4, :] = now
            scaled_ref[4 * k : 4 * k + 4, :] = (now * next_scale).astype(BF)
        else:
            state_ref[:, k, :] = now


def hold_kernel(scaled, own_parts, scaled_out, parts_out):
    scaled_out[...] = scaled[...]
    parts_out[...] = own_parts[...]


def pack_kernel(arrived, above, scaled, own_parts, below, cond, to_below, to_above):
    for at in range(0, 128, 32):
        total = arrived[0, at : at + 32, :].astype(F32)
        for k in range(1, 8):
            total = total + arrived[k, at : at + 32, :].astype(F32)
        total = (total * (1.0 / math.sqrt(K // 2))).astype(BF)
        for ref in (cond, to_below, to_above):
            ref[at : at + 32, :] = total
    to_below[128:144, :] = above[...]
    to_below[144:160, :] = scaled[...]
    to_above[128:160, :] = own_parts[...]
    to_above[160:176, :] = below[...]


def small_call(kernel, name, sizes, *args):
    return pl.pallas_call(
        kernel,
        out_shape=[jax.ShapeDtypeStruct((n, 256), BF) for n in sizes],
        in_specs=[VMEM] * len(args),
        out_specs=[VMEM] * len(sizes),
        compiler_params=limit(4),
        cost_estimate=cost(4),
        name=name,
    )(*args)


def turn(x, by):
    n = lax.axis_size("tile")
    return lax.ppermute(x, "tile", [(i, (i + by) % n) for i in range(n)])


VMEM = pl.BlockSpec(memory_space=pltpu.VMEM)
SMEM = pl.BlockSpec(memory_space=pltpu.SMEM)


LIMIT = 20


def limit(mib):
    return pltpu.CompilerParams(vmem_limit_bytes=mib << 20)


def rowbuf(n):
    return pltpu.VMEM((n, HALF, 256), BF)


def cost(passes):
    return pl.CostEstimate(flops=passes * 128 * 65536 * 2, bytes_accessed=1 << 20, transcendentals=0)


def step_call(step, arrays, width, sigmas, weights):
    rows = STEP_ROWS[step]
    n_arrays, n_weights = len(arrays), len(weights)
    n_out = rows["out"][1]
    if step == 0:
        outs = [jax.ShapeDtypeStruct((4 * n_out, 256), F32), jax.ShapeDtypeStruct((4 * n_out, 256), BF)]
    else:
        outs = [jax.ShapeDtypeStruct((4, 4, 256), F32)]

    def kernel(width_ref, sigma_ref, *refs):
        held, refs = refs[:n_arrays], refs[n_arrays:]
        weight_refs, refs = refs[:n_weights], refs[n_weights:]
        out_refs, refs = list(refs[: len(outs)]), refs[len(outs) :]
        near_up, near_down, cond, cond_far = held[:4]
        conds = [(ref, r) for ref in (near_up, cond, near_down, cond_far) for r in range(2)]
        if step == 0:
            own_ref, two_down = held[4:]
            below = near_down[128:144, :].astype(F32) + near_down[144:160, :].astype(F32)
            own = [(0, own_ref[...], 4), (4, below, 4)]
            halo = [(-8, 8, near_up, 128), (8, 4, two_down, 0), (12, 4, near_down, 160)]
        else:
            own_ref, up, down, top = held[4:]
            own = [(0, own_ref[...], 8)]
            second = lax.axis_index("tile") == 1
            near = jnp.where(second, top[...].astype(F32), up[16:32, :].astype(F32))
            halo = [(-8, 4, up, 0), (-4, 4, near, 0), (8, 4, down, 0)]
        step_kernel(
            step, width_ref, sigma_ref, own, halo, conds, weight_refs, *(out_refs + [None])[:2], *refs
        )

    return pl.pallas_call(
        kernel,
        out_shape=outs,
        in_specs=[SMEM, SMEM] + [VMEM] * (n_arrays + n_weights),
        out_specs=[VMEM] * len(outs),
        scratch_shapes=[
            pltpu.VMEM((rows["scaled"][1] * 8, 256), F32), pltpu.VMEM((rows["scaled"][1] * 8, 512), F32),
            *[
                rowbuf(rows[name][1])
                for name, n in (("first", 2), ("second", 2), ("third", 3), ("fourth", 3), ("fifth", 2))
                for _ in range(n)
            ],
            pltpu.VMEM((48, rows["fifth"][1] * HALF), F32),
            pltpu.VMEM((8 * n_out, 256), F32),
            pltpu.VMEM((3, HALF, 256), F32),
            *[
                pltpu.VMEM(shape, BF)
                for shape in (
                    (96, 256), (48, 512), (256, 1536), (256, 1152), (256, 2304),
                    (256, 1536), (256, 1536), (256, 1536),
                )
            ],
        ],
        compiler_params=limit(LIMIT),
        cost_estimate=cost(300),
        name="step" + str(step),
    )(width, sigmas, *arrays, *weights)


def encode_call(block_anchor, nest_width, sigmas, coarse_blocks, w_context, noise):
    chans = w_context.shape[1]
    cells = coarse_blocks.shape[1] // chans
    count = coarse_blocks.shape[0]
    tiles = coarse_blocks.shape[1] // 128
    return pl.pallas_call(
        encode_kernel,
        out_shape=[
            jax.ShapeDtypeStruct((8, 2 * cells, 256), BF),
            jax.ShapeDtypeStruct((16, 256), F32),
            jax.ShapeDtypeStruct((16, 256), BF),
            jax.ShapeDtypeStruct((32, 256), BF),
        ],
        in_specs=[SMEM, SMEM, SMEM, VMEM, VMEM, VMEM],
        out_specs=[VMEM] * 4,
        scratch_shapes=[
            pltpu.VMEM((count + 8, cells, 256), F32),
            pltpu.VMEM((count * tiles + 64, 128), F32),
            pltpu.VMEM((2, 80, 128), F32),
        ],
        compiler_params=limit(56),
        cost_estimate=cost(100),
        name="encode",
    )(block_anchor, nest_width, sigmas, coarse_blocks, w_context.T, noise)


def per_device(
    coarse_blocks, block_anchor, nest_width, sigmas, noise,
    w_context, w_in, w_sigma, w_enc, w_down, w_mid, w_dec, w_out,
):
    partial, state, scaled, own_parts = encode_call(
        block_anchor, nest_width, sigmas, coarse_blocks, w_context, noise[0]
    )
    arrived = lax.all_to_all(partial, "band", 0, 0, tiled=True)

    one_up = turn(scaled, 1)
    two_down = turn(scaled, -2)
    scaled, own_parts = small_call(hold_kernel, "hold", (16, 32), scaled, own_parts)
    arrived, one_up, two_down, scaled, own_parts = lax.optimization_barrier(
        (arrived, one_up, two_down, scaled, own_parts)
    )

    cond, to_below, to_above = small_call(
        pack_kernel, "pack", (128, 160, 176), arrived, one_up, scaled, own_parts, two_down
    )
    near_up = turn(to_below, 1)
    near_down = turn(to_above, -1)
    cond_far = turn(cond, -2)
    weights = (w_sigma.reshape(1, -1), w_in.transpose(0, 2, 1), w_out, w_enc, w_down, w_mid, w_dec)
    conds = (near_up, near_down, cond, cond_far)
    state, scaled = step_call(0, (*conds, state, two_down), nest_width, sigmas, weights)
    up = turn(scaled, 2)
    down = turn(scaled[16:], -1)
    top = lax.ppermute(scaled[:16], "tile", [(0, 1)])
    (out,) = step_call(1, (*conds, state, up, down, top), nest_width, sigmas, weights)
    return out[None]


def solution(mesh):
    return jax.shard_map(
        per_device,
        mesh=mesh,
        in_specs=(
            P("band", None), P(), P("band"), P(), P("band", None, "tile", None),
            P(), P(), P(), P(), P(), P(), P(), P(),
        ),
        out_specs=P("band", None, "tile", None),
        check_vma=False,
    )
```
